32 devices in a mesh: seq: 4 (over z), chan: 8 (over y, x, core).
Axes of the slice: x: 2, y: 2, z: 4, core: 2. Of those that a mesh axis runs over, the one named last changes fastest.
Arguments:
- tokens: bfloat16 [8192, 768], P(('seq', 'chan')), may hold values from -6 to 6
- resets: int32 [8192], P('seq'), may hold values 0 or 1
- cotangent: bfloat16 [8192, 768], P(('seq', 'chan')), may hold values from -6 to 6
- norm_gain: float32 [768], replicated, may hold values from 0.5 to 1.5
- in_weight: float32 [2, 768, 1536], P(None, None, 'chan'), may hold values from -0.21875 to 0.21875
- x_weight: float32 [1536, 80], P('chan'), may hold values from -0.15625 to 0.15625
- dt_weight: float32 [48, 1536], P(None, 'chan'), may hold values from -1.5 to 1.5
- out_weight: float32 [1536, 768], P('chan'), may hold values from -0.375 to 0.375
- chan_params: float32 [23, 1536], P(None, 'chan'), may hold values from -7 to 3, as said below
- gain_first: float32 [768], replicated, may hold values from -56 to 56
- gain_second: float32 [768], replicated, may hold values from 3.2768 to 52.4288
- in_first: float32 [2, 768, 1536], P(None, None, 'chan'), may hold values from -28 to 28
- in_second: float32 [2, 768, 1536], P(None, None, 'chan'), may hold values from 0.8192 to 13.1072
- x_first: float32 [1536, 80], P('chan'), may hold values from -320 to 320
- x_second: float32 [1536, 80], P('chan'), may hold values from 102.4 to 1638.4
- dt_first: float32 [48, 1536], P(None, 'chan'), may hold values from -32 to 32
- dt_second: float32 [48, 1536], P(None, 'chan'), may hold values from 1.024 to 16.384
- out_first: float32 [1536, 768], P('chan'), may hold values from -24 to 24
- out_second: float32 [1536, 768], P('chan'), may hold values from 0.65536 to 10.6496
- chan_first: float32 [23, 1536], P(None, 'chan'), may hold values from -32 to 32
- chan_second: float32 [23, 1536], P(None, 'chan'), may hold values from 1.024 to 16.384
Outputs:
- mixed: bfloat16 [8192, 768], P(('seq', 'chan'))
- tokens_grad: float32 [8192, 768], P(('seq', 'chan'))
- gain_master: float32 [768], replicated
- gain_first_out: float32 [768], replicated
- gain_second_out: float32 [768], replicated
- gain_copy: bfloat16 [768], replicated
- in_master: float32 [2, 768, 1536], P(None, None, 'chan')
- in_first_out: float32 [2, 768, 1536], P(None, None, 'chan')
- in_second_out: float32 [2, 768, 1536], P(None, None, 'chan')
- in_copy: bfloat16 [2, 768, 1536], P(None, None, 'chan')
- x_master: float32 [1536, 80], P('chan')
- x_first_out: float32 [1536, 80], P('chan')
- x_second_out: float32 [1536, 80], P('chan')
- x_copy: bfloat16 [1536, 80], P('chan')
- dt_master: float32 [48, 1536], P(None, 'chan')
- dt_first_out: float32 [48, 1536], P(None, 'chan')
- dt_second_out: float32 [48, 1536], P(None, 'chan')
- dt_copy: bfloat16 [48, 1536], P(None, 'chan')
- out_master: float32 [1536, 768], P('chan')
- out_first_out: float32 [1536, 768], P('chan')
- out_second_out: float32 [1536, 768], P('chan')
- out_copy: bfloat16 [1536, 768], P('chan')
- chan_master: float32 [23, 1536], P(None, 'chan')
- chan_first_out: float32 [23, 1536], P(None, 'chan')
- chan_second_out: float32 [23, 1536], P(None, 'chan')
- chan_copy: bfloat16 [23, 1536], P(None, 'chan')
The draws below stay inside these ranges and needn't reach their ends.
Inputs may be any that keep to these rules, and one draw needn't show every extreme that they name: `resets`: 1 marks the first token of a document; every packed row of 2048 tokens starts one as well. `chan_params`: the step bias row holds softplus inverses of steps between 0.001 and 0.1.
All inputs are finite; a program needn't handle non-finite values. No bound on the sum of `resets` on one device may be relied on, other than what follows from the above.
Results may differ from the reference program's by a relative error of at most 0.018.
Values may be sent and summed in bfloat16 or wider, within the bound.
A program may use at most 448 MiB of HBM per device.

```python
import math
import jax
import jax.numpy as jnp
from jax import lax

D = 768
DI = 1536
DS = 16
DR = 48
KC = 4
XP = 80
SEQ_LEN = 2048
BLOCK = 8
STEP = 10
TOKENS = 8192


def draw_chan_params(key, part):
    key = jax.random.fold_in(key, 11)
    key_list = jax.random.split(key, 5)
    tap_bound = 0.5
    step_low = 0.001
    skip_top = 1.5
    rate_low = 0.01
    rate_high = 16.0
    tap_rows = jax.random.uniform(key_list[0], (KC, DI), jnp.float32, -tap_bound, tap_bound)
    conv_bias = jax.random.uniform(key_list[1], (1, DI), jnp.float32, -tap_bound, tap_bound)
    step_init = jnp.exp(jax.random.uniform(key_list[2], (1, DI), jnp.float32, math.log(step_low), math.log(0.1)))
    skip_gain = jax.random.uniform(key_list[3], (1, DI), jnp.float32, 0.5, skip_top)
    log_rates = jax.random.uniform(key_list[4], (DS, DI), jnp.float32, math.log(rate_low), math.log(rate_high))
    step_bias = jnp.log(jnp.expm1(step_init))
    return jnp.concatenate([tap_rows, conv_bias, step_bias, skip_gain, log_rates], axis=0)


def with_ends(array, stream_key, smallest, largest):
    spot = [jax.random.randint(jax.random.fold_in(stream_key, axis), (), 0, length) for axis, length in enumerate(array.shape)]
    widest = array.shape.index(max(array.shape))
    next_to = spot[:widest] + [(spot[widest] + 1) % array.shape[widest]] + spot[widest + 1:]
    return array.at[tuple(spot)].set(smallest).at[tuple(next_to)].set(largest)


def block_levels(key, dims, pieces, low, high):
    loudness, own = 1.0, jax.random.fold_in(key, 6)
    for dim, blocks in pieces:
        draws = jnp.exp(jax.random.uniform(jax.random.fold_in(own, dim), (blocks,), jnp.float32, low / len(pieces), high / len(pieces)))
        loudness = loudness * jnp.repeat(draws, dims[dim] // blocks).reshape([-1 if axis == dim else 1 for axis in range(len(dims))])
    return loudness


def noise(rng, shape, scale, limit, cuts=(), kind=jnp.bfloat16):
    factor_of = block_levels(rng, shape, cuts, -0.22, 0.18) if cuts else 1.0
    entries = jax.random.normal(rng, shape, jnp.float32) * scale * factor_of
    return jnp.minimum(jnp.maximum(entries, -limit), limit).astype(kind)


def setup_inputs(seed: int = 0) -> dict:
    keys = jax.random.split(jax.random.key(seed), 22)
    return {
        "tokens": noise(keys[0], (TOKENS, D), 1.0, 6.0, ((0, 32),)),
        "resets": with_ends((jax.random.randint(keys[1], (TOKENS,), 0, SEQ_LEN // 2) < 1).astype(jnp.int32), jax.random.fold_in(keys[1], 1), 0, 1),
        "cotangent": noise(keys[2], (TOKENS, D), 1.0, 6.0, ((0, 32),)),
        "norm_gain": jnp.clip(1.0 + 0.1 * jax.random.normal(keys[3], (D,), jnp.float32), 0.5, 1.5),
        "in_weight": noise(keys[4], (2, D, DI), D ** -0.5, 0.21875, ((2, 8),), jnp.float32),
        "x_weight": noise(keys[5], (DI, XP), DI ** -0.5, 0.15625, ((0, 8),), jnp.float32),
        "dt_weight": noise(keys[6], (DR, DI), (DR // 3) ** -0.5, 1.5, ((1, 8),), jnp.float32),
        "out_weight": noise(keys[7], (DI, D), (DI // 6) ** -0.5, 0.375, ((0, 8),), jnp.float32),
        "chan_params": draw_chan_params(jax.random.fold_in(keys[21], 71), 0),
        "gain_first": noise(keys[9], (D,), (0.1 * TOKENS ** 0.5), 56.0, (), jnp.float32),
        "gain_second": jnp.clip(jnp.exp(jax.random.uniform(keys[10], (D,), jnp.float32, math.log(3.2768), math.log(52.4288))), 3.2768, 52.4288),
        "in_first": noise(keys[11], (2, D, DI), (0.05 * TOKENS ** 0.5), 28.0, ((2, 8),), jnp.float32),
        "in_second": jnp.clip(jnp.exp(math.log(13.1072) - 2.7725887 * jax.random.uniform(keys[12], (2, D, DI), jnp.float32) ** block_levels(keys[12], (2, D, DI), ((2, 8),), -0.2, 0.2)), 0.8192, 13.1072),
        "x_first": noise(keys[13], (DI, XP), (0.55 * TOKENS ** 0.5), 320.0, ((0, 8),), jnp.float32),
        "x_second": jnp.clip(jnp.exp(math.log(1638.4) - 2.7725887 * jax.random.uniform(keys[14], (DI, XP), jnp.float32) ** block_levels(keys[14], (DI, XP), ((0, 8),), -0.2, 0.2)), 102.4, 1638.4),
        "dt_first": noise(keys[15], (DR, DI), (0.055 * TOKENS ** 0.5), 32.0, ((1, 8),), jnp.float32),
        "dt_second": jnp.clip(jnp.exp(math.log(16.384) - 2.7725887 * jax.random.uniform(keys[16], (DR, DI), jnp.float32) ** block_levels(keys[16], (DR, DI), ((1, 8),), -0.2, 0.2)), 1.024, 16.384),
        "out_first": noise(keys[17], (DI, D), (0.045 * TOKENS ** 0.5), 24.0, ((0, 8),), jnp.float32),
        "out_second": jnp.clip(jnp.exp(math.log(10.6496) - 2.7880929 * jax.random.uniform(keys[18], (DI, D), jnp.float32) ** block_levels(keys[18], (DI, D), ((0, 8),), -0.2, 0.2)), 0.65536, 10.6496),
        "chan_first": noise(keys[19], (KC + 3 + DS, DI), (0.055 * TOKENS ** 0.5), 32.0, ((1, 8),), jnp.float32),
        "chan_second": jnp.clip(jnp.exp(math.log(16.384) - 2.7725887 * jax.random.uniform(keys[20], (KC + 3 + DS, DI), jnp.float32) ** block_levels(keys[20], (KC + 3 + DS, DI), ((1, 8),), -0.2, 0.2)), 1.024, 16.384),
    }


@jax.custom_vjp
def low(v):
    return lax.optimization_barrier(v.astype(jnp.bfloat16)).astype(jnp.float32)

@jax.custom_vjp
def low_back(v):
    return v

def low_keep(v):
    return (low(v), None)

def low_pass(kept, grad):
    return (grad,)

def back_keep(v):
    return (v, None)

def back_low(kept, grad):
    return (low(grad),)
low.defvjp(low_keep, low_pass)
low_back.defvjp(back_keep, back_low)
highest = lax.Precision.HIGHEST
norm_epsilon = 1e-05
beta_first = 0.9
beta_second = 0.999
adam_epsilon = 1e-08
weight_decay = 0.1
rate_gain = 0.4
rate_inner = 0.05
rate_project = 0.04
rate_step = 0.1
rate_output = 0.08
rate_channel = 0.5

def rms_scale(values, gain_values):
    return values * lax.rsqrt(lax.optimization_barrier(jnp.mean(values * values, axis=-1, keepdims=True)) + norm_epsilon) * gain_values

def segment_numbers(resets):
    places = jnp.arange(resets.shape[0], dtype=jnp.int32)
    starts = jnp.maximum(resets, (places % SEQ_LEN == 0).astype(jnp.int32))
    return (starts, jnp.cumsum(starts).astype(jnp.int32))

def causal_conv(values, tap_rows, conv_bias, segments):
    result = conv_bias + tap_rows[KC - 1] * values
    for offset in range(1, KC):
        shifted = jnp.pad(values, ((offset, 0), (0, 0)))[:-offset]
        earlier = jnp.pad(segments, (offset, 0), constant_values=-1)[:-offset]
        same_doc = (earlier == segments).astype(values.dtype)
        result = result + tap_rows[KC - 1 - offset] * shifted * same_doc[:, None]
    return result

def adamw_core(master, moment_one, moment_two, gradient, rate_value):
    first_new = beta_first * moment_one + (1.0 - beta_first) * gradient
    second_new = beta_second * moment_two + (1.0 - beta_second) * gradient * gradient
    corrected = first_new / (1.0 - beta_first ** STEP) / (jnp.sqrt(second_new / (1.0 - beta_second ** STEP)) + adam_epsilon)
    master_new = master - rate_value * (corrected + weight_decay * master)
    return (master_new, first_new, second_new)

def sequential_scan(step_dt, decay_rate, b_input, c_input, activated, keeps):
    seq_count = step_dt.shape[0] // SEQ_LEN
    blocks = SEQ_LEN // BLOCK

    def arrange(values):
        shaped = values.reshape((seq_count, blocks, BLOCK) + values.shape[1:])
        return jnp.moveaxis(shaped, 0, 2)

    def one_step(carry_state, step_items):
        dt_now, u_now, b_now, c_now, keep_now = step_items
        carry_state = carry_state * jnp.exp(dt_now[:, None, :] * decay_rate[None]) * keep_now[:, None, None] + b_now[:, :, None] * (dt_now * u_now)[:, None, :]
        return (carry_state, lax.optimization_barrier(jnp.sum(c_now[:, :, None] * carry_state, axis=1)))

    @jax.checkpoint
    def one_block(carry_state, block_items):
        return lax.scan(one_step, carry_state, block_items)
    zero_state = jnp.zeros((seq_count, decay_rate.shape[0], decay_rate.shape[1]), step_dt.dtype)
    final_state, outputs = lax.scan(one_block, zero_state, (arrange(step_dt), arrange(activated), arrange(b_input), arrange(c_input), arrange(keeps)))
    return jnp.moveaxis(outputs, 2, 0).reshape(step_dt.shape)

def forward(token_rows, gain_values, inner_values, project_values, step_values, output_values, channel_values, segments, keeps):
    normed = low(rms_scale(token_rows, gain_values))
    inner_both = low_back(jnp.einsum('td,kdc->ktc', normed, low(inner_values), precision=highest))
    x_inner = inner_both[0]
    gate_inner = inner_both[1]
    activated = low(jax.nn.silu(causal_conv(x_inner, channel_values[:KC], channel_values[KC], segments)))
    projected = low_back(jnp.dot(activated, low(project_values), precision=highest))
    delta_low = low(projected[:, :DR])
    b_input = projected[:, DR:DR + DS]
    c_input = projected[:, DR + DS:]
    dt_raw = low_back(jnp.dot(delta_low, low(step_values), precision=highest) + channel_values[KC + 1])
    step_dt = jax.nn.softplus(dt_raw)
    decay_rate = -jnp.exp(channel_values[KC + 3:])
    scanned = sequential_scan(step_dt, decay_rate, b_input, c_input, activated, keeps)
    gated = low((scanned + channel_values[KC + 2] * activated) * jax.nn.silu(gate_inner))
    return token_rows + jnp.dot(gated, low(output_values), precision=highest)

def reference(tokens, resets, cotangent, norm_gain, in_weight, x_weight, dt_weight, out_weight, chan_params, gain_first, gain_second, in_first, in_second, x_first, x_second, dt_first, dt_second, out_first, out_second, chan_first, chan_second):
    starts, segments = segment_numbers(resets)
    keeps = 1.0 - starts.astype(jnp.float32)

    def layer(token_rows, gain_values, inner_values, project_values, step_values, output_values, channel_values):
        return forward(token_rows, gain_values, inner_values, project_values, step_values, output_values, channel_values, segments, keeps)
    result, pullback = jax.vjp(layer, tokens.astype(jnp.float32), norm_gain, in_weight, x_weight, dt_weight, out_weight, chan_params)
    grads_all = pullback(cotangent.astype(jnp.float32))
    gain_master, gain_first_out, gain_second_out = adamw_core(norm_gain, gain_first, gain_second, grads_all[1], rate_gain)
    in_master, in_first_out, in_second_out = adamw_core(in_weight, in_first, in_second, grads_all[2], rate_inner)
    x_master, x_first_out, x_second_out = adamw_core(x_weight, x_first, x_second, grads_all[3], rate_project)
    dt_master, dt_first_out, dt_second_out = adamw_core(dt_weight, dt_first, dt_second, grads_all[4], rate_step)
    out_master, out_first_out, out_second_out = adamw_core(out_weight, out_first, out_second, grads_all[5], rate_output)
    chan_master, chan_first_out, chan_second_out = adamw_core(chan_params, chan_first, chan_second, grads_all[6], rate_channel)
    return (result.astype(jnp.bfloat16), grads_all[0], gain_master, gain_first_out, gain_second_out, gain_master.astype(jnp.bfloat16), in_master, in_first_out, in_second_out, in_master.astype(jnp.bfloat16), x_master, x_first_out, x_second_out, x_master.astype(jnp.bfloat16), dt_master, dt_first_out, dt_second_out, dt_master.astype(jnp.bfloat16), out_master, out_first_out, out_second_out, out_master.astype(jnp.bfloat16), chan_master, chan_first_out, chan_second_out, chan_master.astype(jnp.bfloat16))
```

```python
import functools

import jax
import jax.numpy as jnp
from jax import lax
from jax.experimental import pallas as pl
from jax.experimental.pallas import tpu as pltpu
from jax.sharding import PartitionSpec as P

DS = 16
DR = 48
KC = 4
SEQ_LEN = 2048
STEP = 10
SLABS = 16
LANES = 128
NG = 4
CT = 2

highest = lax.Precision.HIGHEST
norm_epsilon = 1e-05
beta_first = 0.9
beta_second = 0.999
adam_epsilon = 1e-08
weight_decay = 0.1
rate_gain = 0.4
rate_inner = 0.05
rate_project = 0.04
rate_step = 0.1
rate_output = 0.08
rate_channel = 0.5
LOG2E = 1.4426950408889634
LN2 = 0.6931471805599453
HUGE = 1e30
f32 = jnp.float32
bf16 = jnp.bfloat16


def adamw_core(master, moment_one, moment_two, gradient, rate_value):
    first_new = beta_first * moment_one + (1.0 - beta_first) * gradient
    second_new = beta_second * moment_two + (1.0 - beta_second) * gradient * gradient
    corrected = (
        first_new
        / (1.0 - beta_first**STEP)
        / (jnp.sqrt(second_new / (1.0 - beta_second**STEP)) + adam_epsilon)
    )
    master_new = master - rate_value * (corrected + weight_decay * master)
    return (master_new, first_new, second_new)


def dot_nn(a, b, precision=None):
    return lax.dot_general(a, b, (((1,), (0,)), ((), ())), precision=precision, preferred_element_type=f32)


def dot_nt(a, b, precision=None):
    return lax.dot_general(a, b, (((1,), (1,)), ((), ())), precision=precision, preferred_element_type=f32)


def dot_tn(a, b, precision=None):
    return lax.dot_general(a, b, (((0,), (0,)), ((), ())), precision=precision, preferred_element_type=f32)


def slab(s):
    return slice(s * LANES, (s + 1) * LANES)


def scan_kernel(
    act_ref, gate_ref, dgated_ref, proj_ref, start_ref, dtw_ref, decay_ref, chan_ref,
    gated_ref, dgate_ref, dact_ref, pback_ref, cg_ref,
    b8, c8, db8, dc8, decb, raw_ref, step_ref, stepk_ref, du_ref, dy_ref,
    y_ref, s1_ref, ds2_ref, ssum_ref, red_ref, rb_ref, pb_acc, a_scr, ah_scr,
):
    r = pl.program_id(0)
    ci = pl.program_id(1)
    nc = pl.num_programs(1)
    cb = act_ref.shape[0]
    span = CT * 8
    tiles = cb // span

    row_i = lax.broadcasted_iota(jnp.int32, (DS * 8, DS), 0)
    col_i = lax.broadcasted_iota(jnp.int32, (DS * 8, DS), 1)
    expand = jnp.where(row_i // 8 == col_i, 1.0, 0.0).astype(f32)

    @pl.when(ci == 0)
    def _():
        b8[...] = dot_nn(expand, proj_ref[DR : DR + DS, :].astype(f32), highest)
        c8[...] = dot_nn(expand, proj_ref[DR + DS :, :].astype(f32), highest)
        db8[...] = jnp.zeros_like(db8)
        dc8[...] = jnp.zeros_like(dc8)

    @pl.when((ci == 0) & (r == 0))
    def _():
        cg_ref[...] = jnp.zeros_like(cg_ref)

    for n in range(DS):
        decb[n] = jnp.broadcast_to(decay_ref[:, n : n + 1], (cb, LANES))
    delta = proj_ref[0:DR, :]
    raw_ref[...] = dot_nn(dtw_ref[...], delta)

    def prelude(i, carry):
        rows = pl.ds(pl.multiple_of(i * span, span), span)
        bias = jnp.broadcast_to(chan_ref[rows, KC + 1 : KC + 2], (span, LANES))
        total = jnp.zeros((span, LANES), f32)
        for s in range(SLABS):
            raw = raw_ref[rows, slab(s)] + bias
            raw_ref[rows, slab(s)] = raw
            step = jnp.maximum(raw, 0.0) + jnp.log1p(jnp.exp(-jnp.abs(raw)))
            gate = gate_ref[rows, slab(s)]
            silu = gate / (1.0 + jnp.exp(-gate))
            start = jnp.broadcast_to(start_ref[0:1, slab(s)], (span, LANES))
            stepk = jnp.where(start > 0.0, HUGE, step)
            step_ref[rows, slab(s)] = step
            stepk_ref[rows, slab(s)] = stepk
            du_ref[rows, slab(s)] = step * act_ref[rows, slab(s)].astype(f32)
            dy_ref[rows, slab(s)] = dgated_ref[rows, slab(s)] * silu
            total = total + stepk
        ssum_ref[rows, :] = total
        y_ref[rows, :] = jnp.zeros((span, SEQ_LEN), f32)
        s1_ref[rows, :] = jnp.zeros((span, SEQ_LEN), f32)
        ds2_ref[rows, :] = jnp.zeros((span, SEQ_LEN), f32)
        return carry

    lax.fori_loop(0, tiles, prelude, 0)

    def tile4(ref, rows, s):
        return ref[rows, slab(s)].reshape(1, CT, 8, LANES)

    def group(index, carry):
        i = index // (DS // NG)
        g = index % (DS // NG)
        rows = pl.ds(pl.multiple_of(i * span, span), span)
        nrows = pl.ds(pl.multiple_of(g * (NG * 8), NG * 8), NG * 8)

        def lane4(ref, s):
            return ref[nrows, slab(s)].reshape(NG, 1, 8, LANES)

        dec = decb[pl.ds(g * NG, NG), rows, :].reshape(NG, CT, 8, LANES)
        gain = jnp.exp2(dec * ssum_ref[rows, :].reshape(1, CT, 8, LANES))
        h = jnp.zeros((NG, CT, 8, LANES), f32)
        for s in range(SLABS):
            a = jnp.exp2(dec * tile4(stepk_ref, rows, s))
            a_scr[s] = a
            h = a * h + lane4(b8, s) * tile4(du_ref, rows, s)
        p = jnp.zeros((NG, CT, 8, LANES), f32)
        for s in reversed(range(SLABS)):
            p = a_scr[s] * (tile4(dy_ref, rows, s) * lane4(c8, s) + p)
        gain_f = gain
        gain_b = gain
        shift = 1
        while shift < LANES:
            h = h + gain_f * pltpu.roll(h, shift, 3)
            p = p + gain_b * pltpu.roll(p, LANES - shift, 3)
            if shift * 2 < LANES:
                gain_f = gain_f * pltpu.roll(gain_f, shift, 3)
                gain_b = gain_b * pltpu.roll(gain_b, LANES - shift, 3)
            shift *= 2
        h = pltpu.roll(h, 1, 3)
        p = pltpu.roll(p, LANES - 1, 3)
        for s in range(SLABS):
            ah = a_scr[s] * h
            ah_scr[s] = ah
            h = ah + lane4(b8, s) * tile4(du_ref, rows, s)
            y_ref[rows, slab(s)] += jnp.sum(lane4(c8, s) * h, axis=0).reshape(span, LANES)
            dc8[nrows, slab(s)] += jnp.sum(tile4(dy_ref, rows, s) * h, axis=1).reshape(NG * 8, LANES)
        rate = jnp.zeros((NG, CT, 8, LANES), f32)
        for s in reversed(range(SLABS)):
            lam = tile4(dy_ref, rows, s) * lane4(c8, s) + p
            p = a_scr[s] * lam
            s1_ref[rows, slab(s)] += jnp.sum(lam * lane4(b8, s), axis=0).reshape(span, LANES)
            db8[nrows, slab(s)] += jnp.sum(lam * tile4(du_ref, rows, s), axis=1).reshape(NG * 8, LANES)
            q = lam * ah_scr[s]
            ds2_ref[rows, slab(s)] += jnp.sum(dec * q, axis=0).reshape(span, LANES)
            rate = rate + q * tile4(step_ref, rows, s)
        for n in range(NG):
            cols = pl.ds(pl.multiple_of((g * NG + n) * LANES, LANES), LANES)
            red_ref[rows, cols] = rate[n].reshape(span, LANES)
        return carry

    lax.fori_loop(0, tiles * (DS // NG), group, 0)

    def finish(i, carry):
        rows = pl.ds(pl.multiple_of(i * span, span), span)
        skip = jnp.broadcast_to(chan_ref[rows, KC + 2 : KC + 3], (span, LANES))
        skip_sum = jnp.zeros((span, LANES), f32)
        bias_sum = jnp.zeros((span, LANES), f32)
        for s in range(SLABS):
            act = act_ref[rows, slab(s)].astype(f32)
            gate = gate_ref[rows, slab(s)]
            sig = 1.0 / (1.0 + jnp.exp(-gate))
            silu = gate * sig
            y = y_ref[rows, slab(s)] + skip * act
            gated_ref[rows, slab(s)] = (y * silu).astype(bf16)
            dgate_ref[rows, slab(s)] = (
                dgated_ref[rows, slab(s)] * y * (sig * (1.0 + gate * (1.0 - sig)))
            ).astype(bf16)
            dy = dy_ref[rows, slab(s)]
            s1 = s1_ref[rows, slab(s)]
            step = step_ref[rows, slab(s)]
            dact_ref[rows, slab(s)] = dy * skip + s1 * step
            raw = raw_ref[rows, slab(s)]
            d_step = s1 * act + LN2 * ds2_ref[rows, slab(s)]
            back = (d_step / (1.0 + jnp.exp(-raw))).astype(bf16)
            rb_ref[rows, slab(s)] = back
            skip_sum = skip_sum + dy * act
            bias_sum = bias_sum + back.astype(f32)
        red_ref[rows, DS * LANES : (DS + 1) * LANES] = skip_sum
        red_ref[rows, (DS + 1) * LANES :] = bias_sum
        return carry

    lax.fori_loop(0, tiles, finish, 0)

    back_all = rb_ref[...]
    crow = pl.ds(pl.multiple_of(ci * cb, cb), cb)
    k_i = lax.broadcasted_iota(jnp.int32, ((DS + 2) * LANES, LANES), 0)
    n_i = lax.broadcasted_iota(jnp.int32, ((DS + 2) * LANES, LANES), 1)
    pick = jnp.where(k_i // LANES == n_i, 1.0, 0.0).astype(f32)
    padded = jnp.concatenate([jnp.zeros((64, SEQ_LEN), bf16), delta, jnp.zeros((64 - DR, SEQ_LEN), bf16)])
    cg_ref[crow, :] += dot_nn(red_ref[...], pick, highest) + dot_nt(back_all, padded)
    part = dot_tn(dtw_ref[...], back_all)

    @pl.when(ci == 0)
    def _():
        pb_acc[...] = part

    @pl.when(ci > 0)
    def _():
        pb_acc[...] += part

    @pl.when(ci == nc - 1)
    def _():
        pback_ref[0:DR, :] = pb_acc[...].astype(bf16)
        pback_ref[DR : DR + DS, :] = dot_tn(expand, db8[...], highest).astype(bf16)
        pback_ref[DR + DS :, :] = dot_tn(expand, dc8[...], highest).astype(bf16)


def scan_call(act, gate, dgated, proj, start, dtw_t, decay_t, chan_t):
    channels, tokens = act.shape
    rows = tokens // SEQ_LEN
    cb = 48 if channels % 48 == 0 else channels
    wide = pl.BlockSpec((cb, SEQ_LEN), lambda r, c: (c, r))
    big = (cb, SEQ_LEN)
    return pl.pallas_call(
        scan_kernel,
        grid=(rows, channels // cb),
        in_specs=[
            wide,
            wide,
            wide,
            pl.BlockSpec((DR + 2 * DS, SEQ_LEN), lambda r, c: (0, r)),
            pl.BlockSpec((1, SEQ_LEN), lambda r, c: (0, r)),
            pl.BlockSpec((cb, DR), lambda r, c: (c, 0)),
            pl.BlockSpec((cb, DS), lambda r, c: (c, 0)),
            pl.BlockSpec((cb, KC + 3), lambda r, c: (c, 0)),
        ],
        out_specs=[
            wide,
            wide,
            wide,
            pl.BlockSpec((DR + 2 * DS, SEQ_LEN), lambda r, c: (0, r)),
            pl.BlockSpec((channels, LANES), lambda r, c: (0, 0)),
        ],
        out_shape=[
            jax.ShapeDtypeStruct((channels, tokens), bf16),
            jax.ShapeDtypeStruct((channels, tokens), bf16),
            jax.ShapeDtypeStruct((channels, tokens), f32),
            jax.ShapeDtypeStruct((DR + 2 * DS, tokens), bf16),
            jax.ShapeDtypeStruct((channels, LANES), f32),
        ],
        scratch_shapes=[
            pltpu.VMEM((DS * 8, SEQ_LEN), f32),
            pltpu.VMEM((DS * 8, SEQ_LEN), f32),
            pltpu.VMEM((DS * 8, SEQ_LEN), f32),
            pltpu.VMEM((DS * 8, SEQ_LEN), f32),
            pltpu.VMEM((DS, cb, LANES), f32),
            pltpu.VMEM(big, f32),
            pltpu.VMEM(big, f32),
            pltpu.VMEM(big, f32),
            pltpu.VMEM(big, f32),
            pltpu.VMEM(big, f32),
            pltpu.VMEM(big, f32),
            pltpu.VMEM(big, f32),
            pltpu.VMEM(big, f32),
            pltpu.VMEM((cb, LANES), f32),
            pltpu.VMEM((cb, (DS + 2) * LANES), f32),
            pltpu.VMEM(big, bf16),
            pltpu.VMEM((DR, SEQ_LEN), f32),
            pltpu.VMEM((SLABS, NG, CT, 8, LANES), f32),
            pltpu.VMEM((SLABS, NG, CT, 8, LANES), f32),
        ],
        compiler_params=pltpu.CompilerParams(
            dimension_semantics=("arbitrary", "arbitrary"), vmem_limit_bytes=48 * 1024 * 1024
        ),
        name="scan",
    )(act, gate, dgated, proj, start, dtw_t, decay_t, chan_t)


MESH = pl.DeviceIdType.MESH
PIECES = 4


def flip(index, bits):
    result = index
    place = 1
    while place <= bits:
        if bits & place:
            result = result + place * (1 - 2 * ((index // place) % 2))
        place *= 2
    return result


class Here:
    def __init__(self, chan_size):
        self.seq = lax.axis_index("seq")
        self.chan = lax.axis_index("chan")
        self.chips = chan_size // 2
        self.core = self.chan % 2
        self.chip = self.chan // 2
        self.partner = self.chan + 1 - 2 * self.core

    def same_core(self, k):
        return flip(self.chip, k) * 2 + self.core

    def other_core(self, k):
        return flip(self.chip, k) * 2 + 1 - self.core

    def copy(self, src, dst, send, recv, chan):
        return pltpu.make_async_remote_copy(
            src_ref=src, dst_ref=dst, send_sem=send, recv_sem=recv,
            device_id=(self.seq, chan), device_id_type=MESH,
        )


class Gather:
    def __init__(self, here, buf, send, recv, rsend, rrecv):
        self.here, self.buf = here, buf
        self.send, self.recv, self.rsend, self.rrecv = send, recv, rsend, rrecv

    def place(self, j, q):
        per_row = self.buf.shape[2]
        step = SLABS // PIECES
        return self.buf.at[j // per_row, pl.ds(q * step, step), j % per_row]

    def direct(self, k, q, shard):
        h = self.here
        to = h.partner if k == 0 else h.same_core(k)
        return h.copy(self.place(shard, q), self.place(shard, q), self.send.at[k, q], self.recv.at[k, q], to)

    def relay(self, k, q, shard):
        return self.here.copy(
            self.place(shard, q), self.place(shard, q), self.rsend.at[k, q], self.rrecv.at[k, q], self.here.partner
        )

    def start(self):
        for q in range(PIECES):
            for k in range(1, self.here.chips):
                self.direct(k, q, self.here.chan).start()
            self.direct(0, q, self.here.chan).start()

    def pass_on(self, q):
        for k in range(1, self.here.chips):
            shard = self.here.same_core(k)
            self.direct(k, q, shard).wait_recv()
            self.relay(k, q, shard).start()

    def arrive(self, q):
        self.direct(0, q, self.here.partner).wait_recv()
        for k in range(1, self.here.chips):
            self.relay(k, q, self.here.other_core(k)).wait_recv()

    def close(self):
        for q in range(PIECES):
            for k in range(self.here.chips):
                self.direct(k, q, self.here.chan).wait_send()
            for k in range(1, self.here.chips):
                self.relay(k, q, self.here.same_core(k)).wait_send()


class Reduce:
    def __init__(self, here, part, from_pair, pair, from_chips, total, send, recv):
        self.here, self.part, self.from_pair, self.pair = here, part, from_pair, pair
        self.from_chips, self.total, self.send, self.recv = from_chips, total, send, recv
        self.half = part.shape[1] // 2
        self.own = self.half // here.chips

    def half_cols(self, core):
        return pl.ds(pl.multiple_of(core * self.half, LANES), self.half)

    def own_cols(self, chip):
        return pl.ds(pl.multiple_of(chip * self.own, LANES), self.own)

    def own_total(self, chip):
        start = pl.multiple_of(self.here.core * self.half + chip * self.own, LANES)
        return self.total.at[:, pl.ds(start, self.own)]

    def swap(self):
        h = self.here
        return h.copy(
            self.part.at[:, self.half_cols(1 - h.core)], self.from_pair, self.send.at[0], self.recv.at[0], h.partner
        )

    def scatter(self, k):
        h = self.here
        return h.copy(
            self.pair.at[:, self.own_cols(flip(h.chip, k))], self.from_chips.at[k - 1],
            self.send.at[k], self.recv.at[k], h.same_core(k),
        )

    def spread(self, k, chip):
        h = self.here
        index = h.chips + k
        return h.copy(
            self.own_total(chip), self.own_total(chip), self.send.at[index], self.recv.at[index], h.same_core(k)
        )

    def share(self, core):
        h = self.here
        cols = self.total.at[:, self.half_cols(core)]
        return h.copy(cols, cols, self.send.at[h.chips], self.recv.at[h.chips], h.partner)

    def step1(self):
        self.swap().start()

    def step2(self):
        self.swap().wait()
        pair = self.part[:, self.half_cols(self.here.core)].astype(f32) + self.from_pair[...].astype(f32)
        self.from_pair[...] = pair.astype(self.from_pair.dtype)
        self.pair[...] = pair.astype(bf16)
        for k in range(1, self.here.chips):
            self.scatter(k).start()

    def step3(self):
        total = self.from_pair[:, self.own_cols(self.here.chip)].astype(f32)
        for k in range(1, self.here.chips):
            self.scatter(k).wait_recv()
            total = total + self.from_chips[k - 1].astype(f32)
        start = pl.multiple_of(self.here.core * self.half + self.here.chip * self.own, LANES)
        self.total[:, pl.ds(start, self.own)] = total.astype(bf16)
        for k in range(1, self.here.chips):
            self.spread(k, self.here.chip).start()

    def step4(self):
        for k in range(1, self.here.chips):
            self.spread(k, flip(self.here.chip, k)).wait_recv()
        self.share(self.here.core).start()

    def step5(self):
        self.share(1 - self.here.core).wait_recv()

    def close(self):
        for k in range(1, self.here.chips):
            self.scatter(k).wait_send()
            self.spread(k, self.here.chip).wait_send()
        self.share(self.here.core).wait_send()


def reorder(own_rows):
    lanes = own_rows // SLABS
    r = lax.broadcasted_iota(jnp.int32, (own_rows, own_rows), 0)
    q = lax.broadcasted_iota(jnp.int32, (own_rows, own_rows), 1)
    return jnp.where(q == (r % lanes) * SLABS + r // lanes, 1.0, 0.0)


def front_kernel(
    chan_size,
    tok_ref, cot_ref, gain_ref, inw_ref, xw_ref, outw_ref, chan_ref, mask_ref,
    x_out, gate_out, act_out, dg_out, pj_out, ng_out, cg_out,
    ng, cg, xs, gs, acts, dgs, wx, wg, part, from_pair, pair, from_chips, pj,
    ag_send, ag_recv, ag_rsend, ag_rrecv, rd_send, rd_recv, out_sem,
):
    here = Here(chan_size)
    chips = here.chips
    own_rows, width = tok_ref.shape
    lanes = own_rows // SLABS
    rows_n, _, per_row = ng.shape[:3]
    channels, tokens = xs.shape

    barrier = pltpu.get_barrier_semaphore()
    for k in range(1, chips):
        pl.semaphore_signal(barrier, inc=1, device_id=(here.seq, here.same_core(k)), device_id_type=MESH)
    pl.semaphore_signal(barrier, inc=1, device_id=(here.seq, here.partner), device_id_type=MESH)

    order = reorder(own_rows).astype(bf16)
    values = tok_ref[...].astype(f32)
    normed = values * lax.rsqrt(jnp.mean(values * values, axis=-1, keepdims=True) + norm_epsilon) * gain_ref[...]
    shape = (SLABS, lanes, width)
    ng[here.chan // per_row, :, here.chan % per_row] = (
        dot_nn(order, normed.astype(bf16)).astype(bf16).reshape(shape)
    )
    cg[here.chan // per_row, :, here.chan % per_row] = dot_nn(order, cot_ref[...]).astype(bf16).reshape(shape)

    pl.semaphore_wait(barrier, chips)
    first = Gather(here, ng, ag_send.at[0], ag_recv.at[0], ag_rsend.at[0], ag_rrecv.at[0])
    second = Gather(here, cg, ag_send.at[1], ag_recv.at[1], ag_rsend.at[1], ag_rrecv.at[1])
    first.start()
    wx[...] = inw_ref[0].astype(bf16)
    wg[...] = inw_ref[1].astype(bf16)

    step = SLABS // PIECES
    span = step * per_row * lanes
    first.pass_on(0)
    for q in range(PIECES):
        first.arrive(q)
        if q + 1 < PIECES:
            first.pass_on(q + 1)
        else:
            second.start()
        for r in range(rows_n):
            block = ng[r, q * step : (q + 1) * step].reshape(span, width)
            cols = slice((r * PIECES + q) * span, (r * PIECES + q + 1) * span)
            xs[:, cols] = dot_nt(wx[...], block)
            gs[:, cols] = dot_nt(wg[...], block)
    x_copy = pltpu.make_async_copy(xs, x_out, out_sem.at[0])
    gate_copy = pltpu.make_async_copy(gs, gate_out, out_sem.at[1])
    ng_copy = pltpu.make_async_copy(ng, ng_out, out_sem.at[2])
    for c in (x_copy, gate_copy, ng_copy):
        c.start()

    def conv_tile(index, carry):
        i = index // rows_n
        r = index % rows_n
        rows = pl.ds(pl.multiple_of(i * 16, 16), 16)

        def cols(s):
            return pl.ds(pl.multiple_of(r * SEQ_LEN + s * LANES, LANES), LANES)

        taps = [jnp.broadcast_to(chan_ref[rows, k : k + 1], (16, LANES)) for k in range(KC + 1)]
        earlier = {s: pltpu.roll(xs[rows, cols(s)], 1, 1) for s in range(SLABS - KC + 1, SLABS)}
        for s in range(SLABS):
            conv = taps[KC]
            for j in range(KC):
                value = xs[rows, cols(s - j)] if s >= j else earlier[SLABS + s - j]
                if j > 0:
                    value = value * mask_ref[j : j + 1, cols(s)]
                conv = conv + taps[KC - 1 - j] * value
            acts[rows, cols(s)] = (conv / (1.0 + jnp.exp(-conv))).astype(bf16)
        return carry

    lax.fori_loop(0, channels // 16 * rows_n, conv_tile, 0)
    act_copy = pltpu.make_async_copy(acts, act_out, out_sem.at[3])
    act_copy.start()
    part[...] = dot_nn(xw_ref[...].astype(bf16), acts[...])
    reduce = Reduce(here, part, from_pair, pair, from_chips, pj, rd_send, rd_recv)
    reduce.step1()
    reduce.step2()
    reduce.step3()
    reduce.step4()
    second.pass_on(0)
    reduce.step5()
    pj_copy = pltpu.make_async_copy(pj, pj_out, out_sem.at[4])
    pj_copy.start()
    low = outw_ref[...].astype(bf16)
    for q in range(PIECES):
        second.arrive(q)
        if q + 1 < PIECES:
            second.pass_on(q + 1)
        for r in range(rows_n):
            block = cg[r, q * step : (q + 1) * step].reshape(span, width)
            cols = slice((r * PIECES + q) * span, (r * PIECES + q + 1) * span)
            dgs[:, cols] = dot_nt(low, block)
    dg_copy = pltpu.make_async_copy(dgs, dg_out, out_sem.at[5])
    cg_copy = pltpu.make_async_copy(cg, cg_out, out_sem.at[6])
    dg_copy.start()
    cg_copy.start()
    first.close()
    second.close()
    reduce.close()
    for c in (x_copy, gate_copy, ng_copy, act_copy, pj_copy, dg_copy, cg_copy):
        c.wait()


def front_call(chan_size, tokens, cotangent, gain, in_weight, x_weight, out_weight, chan_t, masks):
    own_rows, width = tokens.shape
    count = masks.shape[1]
    channels = out_weight.shape[0]
    chips = chan_size // 2
    rows = count // SEQ_LEN
    per_row = SEQ_LEN // own_rows
    wide = (channels, count)
    whole = (rows, SLABS, per_row, own_rows // SLABS, width)
    project = DR + 2 * DS
    any_spec = pl.BlockSpec(memory_space=pl.ANY)
    vmem = pl.BlockSpec(memory_space=pltpu.VMEM)
    gather_sems = (2, chips, PIECES)
    return pl.pallas_call(
        functools.partial(front_kernel, chan_size),
        in_specs=[vmem] * 8,
        out_specs=[any_spec] * 7,
        out_shape=[
            jax.ShapeDtypeStruct(wide, f32),
            jax.ShapeDtypeStruct(wide, f32),
            jax.ShapeDtypeStruct(wide, bf16),
            jax.ShapeDtypeStruct(wide, f32),
            jax.ShapeDtypeStruct((project, count), bf16),
            jax.ShapeDtypeStruct(whole, bf16),
            jax.ShapeDtypeStruct(whole, bf16),
        ],
        scratch_shapes=[
            pltpu.VMEM(whole, bf16),
            pltpu.VMEM(whole, bf16),
            pltpu.VMEM(wide, f32),
            pltpu.VMEM(wide, f32),
            pltpu.VMEM(wide, bf16),
            pltpu.VMEM(wide, f32),
            pltpu.VMEM((channels, width), bf16),
            pltpu.VMEM((channels, width), bf16),
            pltpu.VMEM((project, count), f32),
            pltpu.VMEM((project, count // 2), f32),
            pltpu.VMEM((project, count // 2), bf16),
            pltpu.VMEM((chips - 1, project, count // 2 // chips), bf16),
            pltpu.VMEM((project, count), bf16),
            pltpu.SemaphoreType.DMA(gather_sems),
            pltpu.SemaphoreType.DMA(gather_sems),
            pltpu.SemaphoreType.DMA(gather_sems),
            pltpu.SemaphoreType.DMA(gather_sems),
            pltpu.SemaphoreType.DMA((2 * chips,)),
            pltpu.SemaphoreType.DMA((2 * chips,)),
            pltpu.SemaphoreType.DMA((7,)),
        ],
        compiler_params=pltpu.CompilerParams(
            collective_id=0, has_side_effects=True, vmem_limit_bytes=56 * 1024 * 1024
        ),
        name="front",
    )(tokens, cotangent, gain, in_weight, x_weight, out_weight, chan_t, masks)


class Scatter:
    def __init__(self, here, part, pair, landed, send1, recv1, send2, recv2):
        self.here, self.part, self.pair, self.landed = here, part, pair, landed
        self.send1, self.recv1, self.send2, self.recv2 = send1, recv1, send2, recv2
        self.rows, self.per_row = part.shape[0], part.shape[2]

    def slabs(self, q):
        step = SLABS // PIECES
        return pl.ds(q * step, step)

    def swap(self, r, q):
        h = self.here
        index = r * PIECES + q
        return h.copy(
            self.part.at[r, self.slabs(q), :, 1 - h.core], self.pair.at[r, self.slabs(q)],
            self.send1.at[index], self.recv1.at[index], h.partner,
        )

    def out(self, k, q):
        h = self.here
        chip = flip(h.chip, k)
        index = (k - 1) * PIECES + q
        return h.copy(
            self.pair.at[chip // self.per_row, self.slabs(q), chip % self.per_row],
            self.landed.at[k - 1, self.slabs(q)],
            self.send2.at[index], self.recv2.at[index], h.same_core(k),
        )

    def step1(self, q):
        for r in range(self.rows):
            self.swap(r, q).start()

    def step2(self, q):
        step = SLABS // PIECES
        for r in range(self.rows):
            self.swap(r, q).wait()
            for s in range(q * step, (q + 1) * step):
                mine = self.part[r, s, :, self.here.core].astype(f32)
                self.pair[r, s] = (self.pair[r, s].astype(f32) + mine).astype(bf16)
        for k in range(1, self.here.chips):
            self.out(k, q).start()

    def finish(self, result):
        h = self.here
        lanes = self.part.shape[4]
        for q in range(PIECES):
            for k in range(1, h.chips):
                self.out(k, q).wait()
        for s in range(SLABS):
            total = self.pair[h.chip // self.per_row, s, h.chip % self.per_row].astype(f32)
            for k in range(1, h.chips):
                total = total + self.landed[k - 1, s].astype(f32)
            result[s * lanes : (s + 1) * lanes, :] = total


class SeqSum:
    def __init__(self, here, seq_size, buf, half_in, send, recv):
        self.here, self.size, self.buf, self.half_in = here, seq_size, buf, half_in
        self.send, self.recv = send, recv
        self.half = buf.shape[0] // 2
        self.levels = seq_size.bit_length() - 1

    def rows(self, side):
        return pl.ds(pl.multiple_of(side * self.half, 16), self.half)

    def copy(self, index, src, dst, bit):
        h = self.here
        return pltpu.make_async_remote_copy(
            src_ref=src, dst_ref=dst, send_sem=self.send.at[index], recv_sem=self.recv.at[index],
            device_id=(flip(h.seq, bit), h.chan), device_id_type=MESH,
        )

    def level(self, i):
        side = self.here.seq % 2
        rows = self.rows(1 - side) if i == 0 else self.rows(side)
        return self.copy(i, self.buf.at[rows], self.half_in.at[i], 1 << i)

    def back(self):
        return self.copy(self.levels, self.buf.at[self.rows(self.here.seq % 2)], self.half_in.at[self.levels], 1)

    def start(self):
        self.level(0).start()

    def step(self, i):
        side = self.here.seq % 2
        self.level(i).wait()
        rows = self.rows(side)
        total = self.buf[rows, :].astype(f32) + self.half_in[i].astype(f32)
        self.buf[rows, :] = total.astype(bf16)
        if i + 1 < self.levels:
            self.level(i + 1).start()
        else:
            self.back().start()

    def finish(self, out, sems):
        side = self.here.seq % 2
        self.back().wait()
        copies = [
            pltpu.make_async_copy(self.buf.at[self.rows(side)], out.at[self.rows(side)], sems.at[0]),
            pltpu.make_async_copy(self.half_in.at[self.levels], out.at[self.rows(1 - side)], sems.at[1]),
        ]
        for c in copies:
            c.start()
        return copies


def back_kernel(
    chan_size, seq_size,
    chan_ref, mask_ref, cgp_ref, xw_ref,
    pback_in, gated_in, outw_in, cot_in, dgate_in, normed_in, act_in, x_in, dact_in, inw_in,
    msum_ref, dsum_ref, za_out, zb_out, zc_out, gsum_ref,
    pback, gated, outw, dgate, act, x_buf, dact, inw, rows_buf, low, dx, dc, red, gin1,
    part, pair_m, pair_d, land_m, land_d, from_pair, pair, from_chips, pj,
    za, zb, zc, zha, zhb, zhc, gp, gz, gc,
    in_sem, out_sem, m_s1, m_r1, m_s2, m_r2, d_s1, d_r1, d_s2, d_r2,
    rd_send, rd_recv, z_send, z_recv, gz_send, gz_recv, gc_send, gc_recv,
):
    here = Here(chan_size)
    chips = here.chips
    channels, tokens = gated.shape
    rows_n, _, per_row, _, lanes, width = part.shape
    step = SLABS // PIECES

    loads = {}
    for index, (name, src, dst) in enumerate(
        (
            ("pback", pback_in, pback), ("gated", gated_in, gated), ("outw", outw_in, outw),
            ("cot", cot_in.at[0], rows_buf.at[0]), ("dgate", dgate_in, dgate),
            ("normed", normed_in.at[0], rows_buf.at[1]), ("x", x_in, x_buf), ("act", act_in, act),
            ("dact", dact_in, dact), ("inw", inw_in, inw),
        )
    ):
        loads[name] = pltpu.make_async_copy(src, dst, in_sem.at[index])
        loads[name].start()

    barrier = pltpu.get_barrier_semaphore()
    for k in range(1, chan_size):
        pl.semaphore_signal(barrier, inc=1, device_id=(here.seq, flip(here.chan, k)), device_id_type=MESH)
    for k in range(1, seq_size):
        pl.semaphore_signal(barrier, inc=1, device_id=(flip(here.seq, k), here.chan), device_id_type=MESH)

    reduce = Reduce(here, pback, from_pair, pair, from_chips, pj, rd_send, rd_recv)
    mixed = Scatter(here, part, pair_m, land_m, m_s1, m_r1, m_s2, m_r2)
    normed_grad = Scatter(here, part, pair_d, land_d, d_s1, d_r1, d_s2, d_r2)
    sum_a = SeqSum(here, seq_size, za, zha, z_send.at[0], z_recv.at[0])
    sum_b = SeqSum(here, seq_size, zb, zhb, z_send.at[1], z_recv.at[1])
    sum_c = SeqSum(here, seq_size, zc, zhc, z_send.at[2], z_recv.at[2])
    if za.shape[0] > channels:
        for buf in (za, zb, zc):
            buf[channels:, :] = jnp.zeros((buf.shape[0] - channels, buf.shape[1]), bf16)

    loads["pback"].wait()
    pl.semaphore_wait(barrier, chan_size - 1 + seq_size - 1)
    reduce.step1()

    loads["gated"].wait()
    loads["outw"].wait()
    low[0] = outw[...].astype(bf16)
    shape = (per_row, 2, lanes, width)

    def cols_of(r, s):
        return slice((r * SLABS + s) * LANES, (r * SLABS + s + 1) * LANES)

    for q in range(PIECES):
        for r in range(rows_n):
            for s in range(q * step, (q + 1) * step):
                part[r, s] = dot_tn(gated[:, cols_of(r, s)], low[0]).astype(bf16).reshape(shape)
        mixed.step1(q)
        if q == 0:
            reduce.step2()
    for q in range(PIECES // 2):
        mixed.step2(q)
    reduce.step3()
    for q in range(PIECES // 2, PIECES):
        mixed.step2(q)

    def row_block(slot):
        return rows_buf[slot].reshape(SEQ_LEN, width)

    def row_cols(r):
        return slice(r * SEQ_LEN, (r + 1) * SEQ_LEN)

    def fetch(src, r, slot, index):
        c = pltpu.make_async_copy(src.at[r], rows_buf.at[slot], in_sem.at[index])
        c.start()
        return c

    loads["cot"].wait()
    out_grad = dot_nn(gated[:, row_cols(0)], row_block(0))
    for r in range(1, rows_n):
        fetch(cot_in, r, 0, 3).wait()
        out_grad = out_grad + dot_nn(gated[:, row_cols(r)], row_block(0))
    za[0:channels, :] = out_grad.astype(bf16)
    sum_a.start()
    loads["dgate"].wait()
    loads["normed"].wait()
    in_grad = dot_nn(dgate[:, row_cols(0)], row_block(1))
    for r in range(1, rows_n):
        fetch(normed_in, r, 1, 5).wait()
        in_grad = in_grad + dot_nn(dgate[:, row_cols(r)], row_block(1))
    gin1[...] = in_grad
    zb[0:channels, 0:width] = in_grad.astype(bf16)
    zb[0:channels, width:] = cgp_ref[...].astype(bf16)
    sum_b.start()
    loads["inw"].wait()
    low[0] = inw[0].astype(bf16)
    low[1] = inw[1].astype(bf16)

    reduce.step4()
    sum_a.step(0)
    for name in ("x", "act", "dact"):
        loads[name].wait()
    reduce.step5()
    project = pj.shape[0]
    x_low = xw_ref[...].astype(bf16)
    for r in range(rows_n):
        dact[:, row_cols(r)] += dot_tn(x_low, pj[:, row_cols(r)])
    x_grad = dot_nt(act[...], pj[...])
    x_grad = jnp.concatenate([x_grad, jnp.zeros((channels, LANES - project), f32)], axis=1)

    def conv_tile(index, carry):
        i = index // rows_n
        r = index % rows_n
        rows = pl.ds(pl.multiple_of(i * 16, 16), 16)

        def cols(s):
            return pl.ds(pl.multiple_of(r * SEQ_LEN + s * LANES, LANES), LANES)

        taps = [jnp.broadcast_to(chan_ref[rows, k : k + 1], (16, LANES)) for k in range(KC + 1)]
        earlier = {s: pltpu.roll(x_buf[rows, cols(s)], 1, 1) for s in range(SLABS - KC + 1, SLABS)}
        sums = [jnp.zeros((16, LANES), f32) for _ in range(KC + 1)]
        for s in range(SLABS):
            inputs = []
            conv = taps[KC]
            for j in range(KC):
                value = x_buf[rows, cols(s - j)] if s >= j else earlier[SLABS + s - j]
                if j > 0:
                    value = value * mask_ref[j : j + 1, cols(s)]
                inputs.append(value)
                conv = conv + taps[KC - 1 - j] * value
            sig = 1.0 / (1.0 + jnp.exp(-conv))
            d_conv = dact[rows, cols(s)] * (sig * (1.0 + conv * (1.0 - sig)))
            dc[:, slab(s)] = d_conv
            for j in range(KC):
                sums[KC - 1 - j] = sums[KC - 1 - j] + d_conv * inputs[j]
            sums[KC] = sums[KC] + d_conv
        wrapped = {}
        for s in range(KC - 1):
            for j in range(s + 1, KC):
                wrapped[s, j] = pltpu.roll(dc[:, slab(s)] * mask_ref[j : j + 1, cols(s)], LANES - 1, 1)
        for s in range(SLABS):
            d_x = taps[KC - 1] * dc[:, slab(s)]
            for j in range(1, KC):
                if s + j < SLABS:
                    value = dc[:, slab(s + j)] * mask_ref[j : j + 1, cols(s + j)]
                else:
                    value = wrapped[s + j - SLABS, j]
                d_x = d_x + taps[KC - 1 - j] * value
            dx[rows, cols(s)] = d_x.astype(bf16)
        for k in range(KC + 1):
            @pl.when(r == 0)
            def _():
                red[rows, slab(k)] = sums[k]

            @pl.when(r > 0)
            def _():
                red[rows, slab(k)] += sums[k]
        return carry

    lax.fori_loop(0, channels // 16 * rows_n, conv_tile, 0)
    sum_b.step(0)

    for q in range(PIECES):
        for r in range(rows_n):
            for s in range(q * step, (q + 1) * step):
                cols = cols_of(r, s)
                part[r, s] = (dot_tn(dx[:, cols], low[0]) + dot_tn(dgate[:, cols], low[1])).astype(bf16).reshape(shape)
        normed_grad.step1(q)
    for q in range(PIECES):
        normed_grad.step2(q)

    if rows_n > 1:
        fetch(normed_in, 0, 1, 5).wait()
    in_grad = dot_nn(dx[:, row_cols(0)], row_block(1))
    for r in range(1, rows_n):
        fetch(normed_in, r, 1, 5).wait()
        in_grad = in_grad + dot_nn(dx[:, row_cols(r)], row_block(1))
    zc[0:channels, 0:width] = in_grad.astype(bf16)
    k_i = lax.broadcasted_iota(jnp.int32, ((KC + 1) * LANES, LANES), 0)
    n_i = lax.broadcasted_iota(jnp.int32, ((KC + 1) * LANES, LANES), 1)
    pick = jnp.where(k_i // LANES + project == n_i, 1.0, 0.0)
    zc[0:channels, width:] = (x_grad + dot_nn(red[...], pick, highest)).astype(bf16)
    sum_c.start()

    both = low[0].astype(f32) * in_grad + low[1].astype(f32) * gin1[...]
    gp[...] = jnp.sum(both.reshape(channels // 8, 8, width), axis=0)

    def gain_seq(k):
        return pltpu.make_async_remote_copy(
            src_ref=gp, dst_ref=gz.at[k - 1], send_sem=gz_send.at[k - 1], recv_sem=gz_recv.at[k - 1],
            device_id=(flip(here.seq, k), here.chan), device_id_type=MESH,
        )

    def gain_chan(k):
        return here.copy(gz.at[seq_size - 1], gc.at[k - 1], gc_send.at[k - 1], gc_recv.at[k - 1], flip(here.chan, k))

    for k in range(1, seq_size):
        gain_seq(k).start()

    levels = seq_size.bit_length() - 1
    for i in range(1, levels):
        sum_a.step(i)
    for k in range(1, seq_size):
        gain_seq(k).wait()
    total = gp[...]
    for k in range(1, seq_size):
        total = total + gz[k - 1]
    gz[seq_size - 1] = total
    for k in range(1, chan_size):
        gain_chan(k).start()
    mixed.finish(msum_ref)
    saves = sum_a.finish(za_out, out_sem.at[0])
    sum_c.step(0)
    for i in range(1, levels):
        sum_b.step(i)
    for k in range(1, chan_size):
        gain_chan(k).wait()
        total = total + gc[k - 1]
    gsum_ref[...] = total
    saves += sum_b.finish(zb_out, out_sem.at[1])
    for i in range(1, levels):
        sum_c.step(i)
    normed_grad.finish(dsum_ref)
    saves += sum_c.finish(zc_out, out_sem.at[2])
    reduce.close()
    for c in saves:
        c.wait()


def back_call(
    chan_size, seq_size, own_rows, chan_t, masks, cgp, x_weight, pback, gated, out_weight, cot_all, dgate, normed_all, act, x_cols,
    dact, in_weight,
):
    channels, width = out_weight.shape
    count = masks.shape[1]
    chips = chan_size // 2
    rows = count // SEQ_LEN
    per_row = SEQ_LEN // own_rows // 2
    lanes = own_rows // SLABS
    project = DR + 2 * DS
    wide = (channels, count)
    padded = (channels + 31) // 32 * 32
    levels = seq_size.bit_length() - 1
    any_spec = pl.BlockSpec(memory_space=pl.ANY)
    vmem = pl.BlockSpec(memory_space=pltpu.VMEM)
    dma = pltpu.SemaphoreType.DMA
    sums = ((padded, width), (padded, width + LANES), (padded, width + LANES))
    return pl.pallas_call(
        functools.partial(back_kernel, chan_size, seq_size),
        in_specs=[vmem] * 4 + [any_spec] * 10,
        out_specs=[vmem, vmem, any_spec, any_spec, any_spec, vmem],
        out_shape=[
            jax.ShapeDtypeStruct((own_rows, width), f32),
            jax.ShapeDtypeStruct((own_rows, width), f32),
            jax.ShapeDtypeStruct(sums[0], bf16),
            jax.ShapeDtypeStruct(sums[1], bf16),
            jax.ShapeDtypeStruct(sums[2], bf16),
            jax.ShapeDtypeStruct((8, width), f32),
        ],
        scratch_shapes=[
            pltpu.VMEM((project, count), bf16),
            pltpu.VMEM(wide, bf16),
            pltpu.VMEM((channels, width), f32),
            pltpu.VMEM(wide, bf16),
            pltpu.VMEM(wide, bf16),
            pltpu.VMEM(wide, f32),
            pltpu.VMEM(wide, f32),
            pltpu.VMEM((2, channels, width), f32),
            pltpu.VMEM((2, SLABS, 2 * per_row, lanes, width), bf16),
            pltpu.VMEM((2, channels, width), bf16),
            pltpu.VMEM(wide, bf16),
            pltpu.VMEM((16, SEQ_LEN), f32),
            pltpu.VMEM((channels, (KC + 1) * LANES), f32),
            pltpu.VMEM((channels, width), f32),
            pltpu.VMEM((rows, SLABS, per_row, 2, lanes, width), bf16),
            pltpu.VMEM((rows, SLABS, per_row, lanes, width), bf16),
            pltpu.VMEM((rows, SLABS, per_row, lanes, width), bf16),
            pltpu.VMEM((chips - 1, SLABS, lanes, width), bf16),
            pltpu.VMEM((chips - 1, SLABS, lanes, width), bf16),
            pltpu.VMEM((project, count // 2), bf16),
            pltpu.VMEM((project, count // 2), bf16),
            pltpu.VMEM((chips - 1, project, count // 2 // chips), bf16),
            pltpu.VMEM((project, count), bf16),
            pltpu.VMEM(sums[0], bf16),
            pltpu.VMEM(sums[1], bf16),
            pltpu.VMEM(sums[2], bf16),
            pltpu.VMEM((levels + 1, padded // 2, width), bf16),
            pltpu.VMEM((levels + 1, padded // 2, width + LANES), bf16),
            pltpu.VMEM((levels + 1, padded // 2, width + LANES), bf16),
            pltpu.VMEM((8, width), f32),
            pltpu.VMEM((seq_size, 8, width), f32),
            pltpu.VMEM((chan_size - 1, 8, width), f32),
            dma((10,)),
            dma((3, 2)),
            dma((rows * PIECES,)),
            dma((rows * PIECES,)),
            dma((chips * PIECES,)),
            dma((chips * PIECES,)),
            dma((rows * PIECES,)),
            dma((rows * PIECES,)),
            dma((chips * PIECES,)),
            dma((chips * PIECES,)),
            dma((2 * chips,)),
            dma((2 * chips,)),
            dma((3, levels + 1)),
            dma((3, levels + 1)),
            dma((seq_size,)),
            dma((seq_size,)),
            dma((chan_size,)),
            dma((chan_size,)),
        ],
        compiler_params=pltpu.CompilerParams(
            collective_id=1, has_side_effects=True, vmem_limit_bytes=60 * 1024 * 1024
        ),
        name="back",
    )(chan_t, masks, cgp, x_weight, pback, gated, out_weight, cot_all, dgate, normed_all, act, x_cols, dact, in_weight)


def update(grad, master, first, second, rate, outs):
    new = adamw_core(master, first, second, grad, rate)
    for ref, value in zip(outs, new):
        ref[...] = value
    outs[3][...] = new[0].astype(bf16)


def finish_kernel(
    tok_ref, cot_ref, msum_ref, dsum_ref, za_ref, zb_ref, zc_ref, zb_all, zc_all, gsum_ref,
    gain_m, gain_f, gain_s, in_m, in_f, in_s, x_m, x_f, x_s, dt_m, dt_f, dt_s, out_m, out_f, out_s, ch_m, ch_f, ch_s,
    mixed_ref, tgrad_ref, *rest,
):
    gain_o, in_o, x_o, dt_o, out_o, ch_o = (rest[i * 4 : i * 4 + 4] for i in range(6))
    ch_grad = rest[24]
    i = pl.program_id(0)
    width = tok_ref.shape[1]
    own_rows = msum_ref.shape[0]
    block = tok_ref.shape[0]
    lanes = own_rows // SLABS
    channels = x_m.shape[1]

    r = lax.broadcasted_iota(jnp.int32, (block, own_rows), 0) + i * block
    q = lax.broadcasted_iota(jnp.int32, (block, own_rows), 1)
    order = jnp.where(r == (q % lanes) * SLABS + q // lanes, 1.0, 0.0).astype(bf16)

    def in_order(ref):
        values = ref[...]
        high = values.astype(bf16)
        return dot_nn(order, high) + dot_nn(order, (values - high.astype(f32)).astype(bf16))

    values = tok_ref[...].astype(f32)
    mixed_ref[...] = (values + in_order(msum_ref)).astype(bf16)
    d_normed = in_order(dsum_ref)
    rstd = lax.rsqrt(jnp.mean(values * values, axis=-1, keepdims=True) + norm_epsilon)
    scaled = gain_m[...] * d_normed
    mean = jnp.mean(scaled * values, axis=-1, keepdims=True)
    tgrad_ref[...] = cot_ref[...].astype(f32) + rstd * scaled - values * (rstd * rstd * rstd * mean)

    out_grad = za_ref[...].astype(f32)
    update(out_grad, out_m[...], out_f[...], out_s[...], rate_output, out_o)
    for k, ref in ((0, zc_ref), (1, zb_ref)):
        grad = ref[:, 0:width].astype(f32)
        new = adamw_core(in_m[k], in_f[k], in_s[k], grad, rate_inner)
        for o, value in zip(in_o, new):
            o[k] = value
        in_o[3][k] = new[0].astype(bf16)

    @pl.when(i == 0)
    def _():
        grad_b = zb_all[...].astype(f32).T
        grad_c = zc_all[...].astype(f32).T
        update(grad_b[64 : 64 + DR, 0:channels], dt_m[...], dt_f[...], dt_s[...], rate_step, dt_o)
        project = x_m.shape[0]
        update(grad_c[0:project, 0:channels], x_m[...], x_f[...], x_s[...], rate_project, x_o)
        ch_grad[0 : KC + 1, :] = grad_c[project : project + KC + 1, 0:channels]
        ch_grad[KC + 1 : KC + 2, :] = grad_b[DS + 1 : DS + 2, 0:channels]
        ch_grad[KC + 2 : KC + 3, :] = grad_b[DS : DS + 1, 0:channels]
        ch_grad[KC + 3 :, :] = grad_b[0:DS, 0:channels] * -jnp.exp(ch_m[KC + 3 :, :])
        update(ch_grad[...], ch_m[...], ch_f[...], ch_s[...], rate_channel, ch_o)
        gain_grad = jnp.sum(gsum_ref[...], axis=0, keepdims=True) / gain_m[...]
        update(gain_grad, gain_m[...], gain_f[...], gain_s[...], rate_gain, gain_o)


def finish_call(tokens, cotangent, msum, dsum, za, zb, zc, gsum, gains, inners, projects, steps, outputs, chans):
    own_rows, width = tokens.shape
    channels = outputs[0].shape[0]
    cb = 48 if channels % 48 == 0 else channels
    grid = channels // cb
    block = own_rows // grid
    row = pl.BlockSpec((block, width), lambda i: (i, 0))

    def full(shape):
        return pl.BlockSpec(shape, lambda i: (0,) * len(shape))

    inner = pl.BlockSpec((2, cb, width), lambda i: (0, i, 0))
    outer = pl.BlockSpec((cb, width), lambda i: (i, 0))
    tail = pl.BlockSpec((zb.shape[0], LANES), lambda i: (0, width // LANES))
    zed = pl.BlockSpec((cb, width), lambda i: (i, 0))
    groups = (gains, inners, projects, steps, outputs, chans)
    specs = (full(gains[0].shape), inner, full(projects[0].shape), full(steps[0].shape), outer, full(chans[0].shape))
    in_specs = [row, row, full(msum.shape), full(dsum.shape), zed, zed, zed, tail, tail, full(gsum.shape)]
    out_specs = [row, row]
    out_shape = [jax.ShapeDtypeStruct(tokens.shape, bf16), jax.ShapeDtypeStruct(tokens.shape, f32)]
    args = [tokens, cotangent, msum, dsum, za, zb, zc, zb, zc, gsum]
    for arrays, spec in zip(groups, specs):
        in_specs += [spec] * 3
        out_specs += [spec] * 4
        out_shape += [jax.ShapeDtypeStruct(arrays[0].shape, f32)] * 3 + [jax.ShapeDtypeStruct(arrays[0].shape, bf16)]
        args += list(arrays)
    return pl.pallas_call(
        finish_kernel,
        grid=(grid,),
        in_specs=in_specs,
        out_specs=out_specs,
        out_shape=out_shape,
        scratch_shapes=[pltpu.VMEM(chans[0].shape, f32)],
        compiler_params=pltpu.CompilerParams(dimension_semantics=("arbitrary",), vmem_limit_bytes=48 * 1024 * 1024),
        name="finish",
    )(*args)


def shift_later(values, j):
    c = values.shape[0]
    v = values.reshape(c, -1, SLABS, LANES)
    return jnp.concatenate([jnp.roll(v[:, :, SLABS - j :], 1, axis=3), v[:, :, : SLABS - j]], axis=2).reshape(values.shape)


def per_device(
    tokens,
    resets,
    cotangent,
    norm_gain,
    in_weight,
    x_weight,
    dt_weight,
    out_weight,
    chan_params,
    gain_first,
    gain_second,
    in_first,
    in_second,
    x_first,
    x_second,
    dt_first,
    dt_second,
    out_first,
    out_second,
    chan_first,
    chan_second,
):
    count = resets.shape[0]
    own_count = tokens.shape[0]
    places = jnp.arange(count, dtype=jnp.int32)
    starts = jnp.maximum(resets, (places % SEQ_LEN == 0).astype(jnp.int32))
    start_row = jnp.swapaxes(starts.reshape(count // SEQ_LEN, LANES, SLABS), 1, 2).reshape(1, count)
    start_row = start_row.astype(f32)
    keep1 = 1.0 - start_row
    keep2 = keep1 * shift_later(keep1, 1)
    keep3 = keep2 * shift_later(keep1, 2)
    chan_size = lax.axis_size("chan")
    seq_size = lax.axis_size("seq")
    chan_t = chan_params[: KC + 3].T
    decay_t = -jnp.exp(chan_params[KC + 3 :].T)
    masks = jnp.concatenate([start_row, keep1, keep2, keep3])
    inners = [jnp.swapaxes(a, 1, 2) for a in (in_weight, in_first, in_second)]
    projects = [a.T for a in (x_weight, x_first, x_second)]
    x_cols, gate_cols, act, dgated, projected, normed_all, cot_all = front_call(
        chan_size, tokens, cotangent, norm_gain[None], inners[0], projects[0], out_weight, chan_t, masks
    )
    gated, d_gate, dact_tail, pback, cgp = scan_call(
        act, gate_cols, dgated, projected, start_row, dt_weight.T.astype(bf16), decay_t * LOG2E, chan_t
    )
    msum, dsum, za, zb, zc, gsum = back_call(
        chan_size, seq_size, own_count, chan_t, masks, cgp, projects[0], pback, gated, out_weight, cot_all, d_gate, normed_all,
        act, x_cols, dact_tail, inners[0],
    )
    result = finish_call(
        tokens, cotangent, msum, dsum, za, zb, zc, gsum,
        [a[None] for a in (norm_gain, gain_first, gain_second)],
        inners,
        projects,
        (dt_weight, dt_first, dt_second),
        (out_weight, out_first, out_second),
        (chan_params, chan_first, chan_second),
    )
    result = list(result)
    result[2:6] = [a[0] for a in result[2:6]]
    result[6:10] = [jnp.swapaxes(a, 1, 2) for a in result[6:10]]
    result[10:14] = [a.T for a in result[10:14]]
    return tuple(result)


def solution(mesh):
    rows = P(("seq", "chan"), None)
    inner = P(None, None, "chan")
    by_row = P("chan", None)
    by_col = P(None, "chan")
    placed = (rows, P("seq"), rows, P(), inner, by_row, by_col, by_row, by_col, P(), P())
    placed += (inner, inner, by_row, by_row, by_col, by_col, by_row, by_row, by_col, by_col)
    return jax.shard_map(
        per_device,
        mesh=mesh,
        in_specs=placed,
        out_specs=(rows, rows)
        + (P(),) * 4
        + (inner,) * 4
        + (by_row,) * 4
        + (by_col,) * 4
        + (by_row,) * 4
        + (by_col,) * 4,
        check_vma=False,
    )
```

```python
import functools

import jax
import jax.numpy as jnp
from jax import lax
from jax.experimental import pallas as pl
from jax.experimental.pallas import tpu as pltpu
from jax.sharding import PartitionSpec as P

DS = 16
DR = 48
KC = 4
SEQ_LEN = 2048
STEP = 10
SLABS = 16
LANES = 128
NG = 8
CT = 2
SEGMENTS = 4
PIECES = 4
MIB = 1024 * 1024
MESH = pl.DeviceIdType.MESH

highest = lax.Precision.HIGHEST
norm_epsilon = 1e-05
beta_first = 0.9
beta_second = 0.999
adam_epsilon = 1e-08
weight_decay = 0.1
rate_gain = 0.4
rate_inner = 0.05
rate_project = 0.04
rate_step = 0.1
rate_output = 0.08
rate_channel = 0.5
LOG2E = 1.4426950408889634
LN2 = 0.6931471805599453
HUGE = 1e30
f32 = jnp.float32
bf16 = jnp.bfloat16


def adamw_core(master, moment_one, moment_two, gradient, rate_value):
    first_new = beta_first * moment_one + (1.0 - beta_first) * gradient
    second_new = beta_second * moment_two + (1.0 - beta_second) * gradient * gradient
    corrected = (
        first_new
        / (1.0 - beta_first**STEP)
        / (jnp.sqrt(second_new / (1.0 - beta_second**STEP)) + adam_epsilon)
    )
    master_new = master - rate_value * (corrected + weight_decay * master)
    return (master_new, first_new, second_new)


def dot_nn(a, b, precision=None):
    return lax.dot_general(a, b, (((1,), (0,)), ((), ())), precision=precision, preferred_element_type=f32)


def dot_nt(a, b, precision=None):
    return lax.dot_general(a, b, (((1,), (1,)), ((), ())), precision=precision, preferred_element_type=f32)


def dot_tn(a, b, precision=None):
    return lax.dot_general(a, b, (((0,), (0,)), ((), ())), precision=precision, preferred_element_type=f32)


def slab(s):
    return slice(s * LANES, (s + 1) * LANES)


def flip(index, bits):
    result = index
    place = 1
    while place <= bits:
        if bits & place:
            result = result + place * (1 - 2 * ((index // place) % 2))
        place *= 2
    return result


class Here:
    def __init__(self, chan_size):
        self.seq = lax.axis_index("seq")
        self.chan = lax.axis_index("chan")
        self.chips = chan_size // 2
        self.core = self.chan % 2
        self.chip = self.chan // 2
        self.partner = self.chan + 1 - 2 * self.core

    def same_core(self, k):
        return flip(self.chip, k) * 2 + self.core

    def other_core(self, k):
        return flip(self.chip, k) * 2 + 1 - self.core

    def copy(self, src, dst, send, recv, chan):
        return pltpu.make_async_remote_copy(
            src_ref=src, dst_ref=dst, send_sem=send, recv_sem=recv,
            device_id=(self.seq, chan), device_id_type=MESH,
        )


class Gather:
    def __init__(self, here, buf, hop, send, recv, rsend, rrecv, fsend, frecv):
        self.here, self.buf, self.hop = here, buf, hop
        self.send, self.recv, self.rsend, self.rrecv = send, recv, rsend, rrecv
        self.fsend, self.frecv = fsend, frecv
        self.half = PIECES // 2

    def place(self, j, q):
        per_row = self.buf.shape[2]
        step = SLABS // PIECES
        return self.buf.at[j // per_row, pl.ds(q * step, step), j % per_row]

    def direct(self, k, q, shard):
        h = self.here
        to = h.partner if k == 0 else h.same_core(k)
        return h.copy(self.place(shard, q), self.place(shard, q), self.send.at[k, q], self.recv.at[k, q], to)

    def relay(self, k, q, shard):
        return self.here.copy(
            self.place(shard, q), self.place(shard, q), self.rsend.at[k, q], self.rrecv.at[k, q], self.here.partner
        )

    def onward(self, q, shard, k):
        return self.here.copy(
            self.place(shard, q), self.place(shard, q), self.fsend.at[q], self.frecv.at[q], self.here.same_core(k)
        )

    def pieces(self, k):
        every = list(range(PIECES))
        return every[self.half :] + every[: self.half] if k == 1 else every

    def start(self):
        h = self.here
        for i in range(PIECES):
            for k in range(1, 3 if self.hop else h.chips):
                self.direct(k, self.pieces(k)[i] if self.hop else i, h.chan).start()
        for q in range(PIECES):
            self.direct(0, q, h.chan).start()

    def take(self, k, q):
        shard = self.here.same_core(k)
        self.direct(k, q, shard).wait_recv()
        if self.hop and (q >= self.half) == (k == 1):
            self.onward(q, shard, 3 - k).start()
        self.relay(k, q, shard).start()

    def take_across(self, q):
        shard = self.here.same_core(3)
        self.onward(q, shard, 1).wait_recv()
        self.relay(3, q, shard).start()

    def pass_on(self, i):
        if not self.hop:
            if i < PIECES:
                for k in range(1, self.here.chips):
                    self.take(k, i)
        elif i < PIECES:
            self.take(1, self.pieces(1)[i])
            self.take(2, self.pieces(2)[i])
        else:
            for q in range(self.half):
                self.take_across(q)
                self.take_across(self.half + q)

    def arrive(self, q):
        self.direct(0, q, self.here.partner).wait_recv()
        for k in range(1, self.here.chips):
            self.relay(k, q, self.here.other_core(k)).wait_recv()

    def close(self):
        for q in range(PIECES):
            for k in range(3 if self.hop else self.here.chips):
                self.direct(k, q, self.here.chan).wait_send()
            if self.hop:
                k = 1 if q >= self.half else 2
                self.onward(q, self.here.same_core(k), 3 - k).wait_send()
            for k in range(1, self.here.chips):
                self.relay(k, q, self.here.same_core(k)).wait_send()


class Reduce:
    def __init__(self, here, part, from_pair, pair, from_chips, total, send, recv):
        self.here, self.part, self.from_pair, self.pair = here, part, from_pair, pair
        self.from_chips, self.total, self.send, self.recv = from_chips, total, send, recv
        self.half = part.shape[1] // 2
        self.own = self.half // here.chips

    def half_cols(self, core):
        return pl.ds(pl.multiple_of(core * self.half, LANES), self.half)

    def own_cols(self, chip):
        return pl.ds(pl.multiple_of(chip * self.own, LANES), self.own)

    def own_total(self, chip):
        start = pl.multiple_of(self.here.core * self.half + chip * self.own, LANES)
        return self.total.at[:, pl.ds(start, self.own)]

    def swap(self):
        h = self.here
        return h.copy(
            self.part.at[:, self.half_cols(1 - h.core)], self.from_pair, self.send.at[0], self.recv.at[0], h.partner
        )

    def scatter(self, k):
        h = self.here
        return h.copy(
            self.pair.at[:, self.own_cols(flip(h.chip, k))], self.from_chips.at[k - 1],
            self.send.at[k], self.recv.at[k], h.same_core(k),
        )

    def spread(self, k, chip):
        h = self.here
        index = h.chips + k
        return h.copy(
            self.own_total(chip), self.own_total(chip), self.send.at[index], self.recv.at[index], h.same_core(k)
        )

    def share(self, core):
        h = self.here
        cols = self.total.at[:, self.half_cols(core)]
        return h.copy(cols, cols, self.send.at[h.chips], self.recv.at[h.chips], h.partner)

    def step1(self):
        self.swap().start()

    def step2(self):
        self.swap().wait()
        pair = self.part[:, self.half_cols(self.here.core)].astype(f32) + self.from_pair[...].astype(f32)
        self.from_pair[...] = pair.astype(self.from_pair.dtype)
        self.pair[...] = pair.astype(bf16)
        for k in range(1, self.here.chips):
            self.scatter(k).start()

    def step3(self):
        total = self.from_pair[:, self.own_cols(self.here.chip)].astype(f32)
        for k in range(1, self.here.chips):
            self.scatter(k).wait_recv()
            total = total + self.from_chips[k - 1].astype(f32)
        start = pl.multiple_of(self.here.core * self.half + self.here.chip * self.own, LANES)
        self.total[:, pl.ds(start, self.own)] = total.astype(bf16)
        for k in range(1, self.here.chips):
            self.spread(k, self.here.chip).start()

    def step4(self):
        for k in range(1, self.here.chips):
            self.spread(k, flip(self.here.chip, k)).wait_recv()
        self.share(self.here.core).start()

    def step5(self):
        self.share(1 - self.here.core).wait_recv()

    def close(self):
        for k in range(1, self.here.chips):
            self.scatter(k).wait_send()
            self.spread(k, self.here.chip).wait_send()
        self.share(self.here.core).wait_send()


def reorder(own_rows):
    lanes = own_rows // SLABS
    r = lax.broadcasted_iota(jnp.int32, (own_rows, own_rows), 0)
    q = lax.broadcasted_iota(jnp.int32, (own_rows, own_rows), 1)
    return jnp.where(q == (r % lanes) * SLABS + r // lanes, 1.0, 0.0)


class Scatter:
    def __init__(self, here, part, pair, landed, send1, recv1, send2, recv2):
        self.here, self.part, self.pair, self.landed = here, part, pair, landed
        self.send1, self.recv1, self.send2, self.recv2 = send1, recv1, send2, recv2
        self.slots, self.rows, self.per_row = part.shape[0], pair.shape[0], pair.shape[2]

    def slabs(self, q):
        step = SLABS // PIECES
        return pl.ds(q * step, step)

    def swap(self, r, q):
        h = self.here
        index = r * PIECES + q
        return h.copy(
            self.part.at[r % self.slots, self.slabs(q), :, 1 - h.core], self.pair.at[r, self.slabs(q)],
            self.send1.at[index], self.recv1.at[index], h.partner,
        )

    def out(self, k, q):
        h = self.here
        chip = flip(h.chip, k)
        index = (k - 1) * PIECES + q
        return h.copy(
            self.pair.at[chip // self.per_row, self.slabs(q), chip % self.per_row],
            self.landed.at[k - 1, self.slabs(q)],
            self.send2.at[index], self.recv2.at[index], h.same_core(k),
        )

    def add(self, r, q):
        step = SLABS // PIECES
        self.swap(r, q).wait()
        for s in range(q * step, (q + 1) * step):
            mine = self.part[r % self.slots, s, :, self.here.core].astype(f32)
            self.pair[r, s] = (self.pair[r, s].astype(f32) + mine).astype(bf16)

    def produce(self, partial):
        step = SLABS // PIECES
        _, _, per_row, _, lanes, width = self.part.shape
        for r in range(self.rows):
            for q in range(PIECES):
                for s in range(q * step, (q + 1) * step):
                    self.part[r % self.slots, s] = partial(r, s).astype(bf16).reshape(per_row, 2, lanes, width)
                self.swap(r, q).start()
            if r + 1 < self.rows:
                for q in range(PIECES):
                    self.add(r, q)

    def send(self):
        for q in range(PIECES):
            self.add(self.rows - 1, q)
            for k in range(1, self.here.chips):
                self.out(k, q).start()

    def finish(self, result):
        h = self.here
        lanes = self.part.shape[4]
        for q in range(PIECES):
            for k in range(1, h.chips):
                self.out(k, q).wait()
        for s in range(SLABS):
            total = self.pair[h.chip // self.per_row, s, h.chip % self.per_row].astype(f32)
            for k in range(1, h.chips):
                total = total + self.landed[k - 1, s].astype(f32)
            result[s * lanes : (s + 1) * lanes, :] = total


class SeqSum:
    def __init__(self, here, seq_size, buf, half_in, send, recv):
        self.here, self.size, self.buf, self.half_in = here, seq_size, buf, half_in
        self.send, self.recv = send, recv
        self.half = buf.shape[0] // 2
        self.levels = seq_size.bit_length() - 1

    def rows(self, side):
        return pl.ds(pl.multiple_of(side * self.half, 16), self.half)

    def copy(self, index, src, dst, bit):
        h = self.here
        return pltpu.make_async_remote_copy(
            src_ref=src, dst_ref=dst, send_sem=self.send.at[index], recv_sem=self.recv.at[index],
            device_id=(flip(h.seq, bit), h.chan), device_id_type=MESH,
        )

    def level(self, i):
        side = self.here.seq % 2
        rows = self.rows(1 - side) if i == 0 else self.rows(side)
        return self.copy(i, self.buf.at[rows], self.half_in.at[i], 1 << i)

    def back(self):
        return self.copy(self.levels, self.buf.at[self.rows(self.here.seq % 2)], self.half_in.at[self.levels], 1)

    def start(self):
        self.level(0).start()

    def step(self, i):
        side = self.here.seq % 2
        self.level(i).wait()
        rows = self.rows(side)
        total = self.buf[rows, :].astype(f32) + self.half_in[i].astype(f32)
        self.buf[rows, :] = total.astype(bf16)
        if i + 1 < self.levels:
            self.level(i + 1).start()
        else:
            self.back().start()

    def finish(self, out, sems):
        side = self.here.seq % 2
        self.back().wait()
        copies = [
            pltpu.make_async_copy(self.buf.at[self.rows(side)], out.at[self.rows(side)], sems.at[0]),
            pltpu.make_async_copy(self.half_in.at[self.levels], out.at[self.rows(1 - side)], sems.at[1]),
        ]
        for c in copies:
            c.start()
        return copies


def iota(shape, dim):
    return lax.broadcasted_iota(jnp.int32, shape, dim)


def row_masks(resets_ref, mask_ref):
    per_row = SEQ_LEN // LANES
    chunk, place = iota((SLABS, LANES), 1), iota((SLABS, LANES), 0)
    group = LANES // SLABS
    pick_row = jnp.where(iota((LANES, per_row), 0) // group == iota((LANES, per_row), 1), 1.0, 0.0).astype(bf16)
    pick_place = jnp.where(iota((SLABS, LANES), 1) % SLABS == iota((SLABS, LANES), 0), 1.0, 0.0).astype(bf16)
    own_chunk = iota((LANES, LANES), 1) // SLABS == iota((LANES, LANES), 0) % group

    def before(values):
        moved = pltpu.roll(values, 1, 0)
        return jnp.where(place == 0, pltpu.roll(moved, 1, 1), moved)

    for r in range(mask_ref.shape[1] // SEQ_LEN):
        block = resets_ref[r * per_row : (r + 1) * per_row, :].astype(f32).astype(bf16)
        spread = jnp.where(own_chunk, dot_nn(pick_row, block), 0.0).astype(bf16)
        start = dot_nt(pick_place, spread)
        start = jnp.where((place == 0) & (chunk == 0), 1.0, start)
        keep1 = 1.0 - start
        keep2 = keep1 * before(keep1)
        keep3 = keep2 * before(before(keep1))
        for s in range(SLABS):
            cols = slice(r * SEQ_LEN + s * LANES, r * SEQ_LEN + (s + 1) * LANES)
            for j, values in enumerate((start, keep1, keep2, keep3)):
                mask_ref[j : j + 1, cols] = values[s : s + 1, :]


DECAY_COL = 8
DT_COL = 64


def softplus(values):
    return jnp.maximum(values, 0.0) + jnp.log1p(jnp.exp(-jnp.abs(values)))


def expand_matrix():
    return jnp.where(iota((DS * 8, DS), 0) // 8 == iota((DS * 8, DS), 1), 1.0, 0.0)


class Tiles:
    def __init__(self, channels, rows_n):
        self.rows_n, self.span = rows_n, CT * 8
        self.tiles, self.groups = channels // self.span, DS // NG
        self.per_row = self.tiles * self.groups
        self.count = rows_n * self.per_row

    def split(self, index):
        r, j = (0, index) if self.rows_n == 1 else (index // self.per_row, index % self.per_row)
        return r, j, j // self.groups, j % self.groups

    def rows(self, i):
        return pl.ds(pl.multiple_of(i * self.span, self.span), self.span)

    def cols(self, r, s):
        if self.rows_n == 1:
            return slab(s)
        return pl.ds(pl.multiple_of(r * SEQ_LEN + s * LANES, LANES), LANES)

    def loop(self, segment, body):
        lo, hi = (self.count * k // SEGMENTS for k in (segment, segment + 1))
        lax.fori_loop(lo, hi, body, 0)


def front_kernel(
    chan_size,
    tok_ref, cot_ref, gain_ref, inw_ref, xw_ref, outw_ref, ch_ref, dtw_ref, resets_ref,
    x_out, act_out, step_out, dy_out, gated_out, dgate_out, pj_out, ng_out, cg_out, h0_out, dec_out, mask_out, ct_out,
    ng, cg, xs, gs, slope, acts, dgs, wx, wg, part, from_pair, pair, from_chips, pj,
    mask, table, rowf, padded, step_ref, du_ref, y_ref, wf, b8, c8, decb, h0, a_scr, gated, dgate,
    ag_send, ag_recv, ag_rsend, ag_rrecv, ag_fsend, ag_frecv, rd_send, rd_recv, out_sem,
):
    here = Here(chan_size)
    chips = here.chips
    own_rows, width = tok_ref.shape
    lanes = own_rows // SLABS
    rows_n, _, per_row = ng.shape[:3]
    channels, tokens = xs.shape
    t = Tiles(channels, rows_n)
    copies = []

    def save(src, dst):
        c = pltpu.make_async_copy(src, dst, out_sem.at[len(copies)])
        c.start()
        copies.append(c)

    barrier = pltpu.get_barrier_semaphore()
    for k in range(1, chips):
        pl.semaphore_signal(barrier, inc=1, device_id=(here.seq, here.same_core(k)), device_id_type=MESH)
    pl.semaphore_signal(barrier, inc=1, device_id=(here.seq, here.partner), device_id_type=MESH)

    order = reorder(own_rows).astype(bf16)
    values = tok_ref[...].astype(f32)
    normed = values * lax.rsqrt(jnp.mean(values * values, axis=-1, keepdims=True) + norm_epsilon) * gain_ref[...]
    shape = (SLABS, lanes, width)
    ng[here.chan // per_row, :, here.chan % per_row] = (
        dot_nn(order, normed.astype(bf16)).astype(bf16).reshape(shape)
    )
    pl.semaphore_wait(barrier, chips)
    first = Gather(
        here, ng, chips == 4, ag_send.at[0], ag_recv.at[0], ag_rsend.at[0], ag_rrecv.at[0], ag_fsend, ag_frecv
    )
    second = Gather(here, cg, False, ag_send.at[1], ag_recv.at[1], ag_rsend.at[1], ag_rrecv.at[1], None, None)
    first.start()

    cg[here.chan // per_row, :, here.chan % per_row] = dot_nn(order, cot_ref[...]).astype(bf16).reshape(shape)
    wx[...] = inw_ref[0].astype(bf16)
    wg[...] = inw_ref[1].astype(bf16)
    row_masks(resets_ref, mask)
    rowf[...] = jnp.zeros_like(rowf)
    rowf[0 : KC + 3, :] = ch_ref[0 : KC + 3, :]
    rowf[DECAY_COL : DECAY_COL + DS, :] = -jnp.exp(ch_ref[KC + 3 :, :]) * LOG2E
    rowf[DT_COL : DT_COL + DR, :] = dtw_ref[...]
    table[...] = rowf[...].T
    for n in range(DS):
        decb[n] = jnp.broadcast_to(table[:, DECAY_COL + n : DECAY_COL + n + 1], (channels, LANES))
    padded[...] = jnp.zeros_like(padded)
    save(mask, mask_out)
    save(table, ct_out)
    save(decb, dec_out)

    step = SLABS // PIECES
    span = step * per_row * lanes

    def project(q):
        first.arrive(q)
        for r in range(rows_n):
            block = ng[r, q * step : (q + 1) * step].reshape(span, width)
            cols = slice((r * PIECES + q) * span, (r * PIECES + q + 1) * span)
            xs[:, cols] = dot_nt(wx[...], block)
            gs[:, cols] = dot_nt(wg[...], block)

    if first.hop:
        for i in range(PIECES + 1):
            first.pass_on(i)
        for q in range(PIECES):
            project(q)
    else:
        first.pass_on(0)
        for q in range(PIECES):
            if q + 1 < PIECES:
                first.pass_on(q + 1)
            project(q)
    save(xs, x_out)
    save(ng, ng_out)

    def conv_tile(index, carry):
        i = index // rows_n
        r = index % rows_n
        rows = pl.ds(pl.multiple_of(i * 16, 16), 16)
        taps = [jnp.broadcast_to(table[rows, k : k + 1], (16, LANES)) for k in range(KC + 1)]
        earlier = {s: pltpu.roll(xs[rows, t.cols(r, s)], 1, 1) for s in range(SLABS - KC + 1, SLABS)}
        for s in range(SLABS):
            conv = taps[KC]
            for j in range(KC):
                value = xs[rows, t.cols(r, s - j)] if s >= j else earlier[SLABS + s - j]
                if j > 0:
                    value = value * mask[j : j + 1, t.cols(r, s)]
                conv = conv + taps[KC - 1 - j] * value
            acts[rows, t.cols(r, s)] = (conv * jax.nn.sigmoid(conv)).astype(bf16)
        return carry

    lax.fori_loop(0, channels // 16 * rows_n, conv_tile, 0)
    part[...] = dot_nn(xw_ref[...].astype(bf16), acts[...])
    reduce = Reduce(here, part, from_pair, pair, from_chips, pj, rd_send, rd_recv)
    reduce.step1()
    save(acts, act_out)
    reduce.step2()

    def gate_tile(index, carry):
        i = index // rows_n
        r = index % rows_n
        rows = pl.ds(pl.multiple_of(i * 16, 16), 16)
        for s in range(SLABS):
            gate = gs[rows, t.cols(r, s)]
            sig = jax.nn.sigmoid(gate)
            gs[rows, t.cols(r, s)] = gate * sig
            slope[rows, t.cols(r, s)] = sig * (1.0 + gate * (1.0 - sig))
        return carry

    lax.fori_loop(0, channels // 16 * rows_n, gate_tile, 0)
    reduce.step3()
    reduce.step4()
    reduce.step5()
    second.start()
    save(pj, pj_out)

    padded[DT_COL : DT_COL + DR, :] = pj[0:DR, :]
    step_ref[...] = dot_nn(table[...].astype(bf16), padded[...])

    def prelude(index, carry):
        i = index // rows_n
        r = index % rows_n
        rows = pl.ds(pl.multiple_of(i * 16, 16), 16)
        bias = jnp.broadcast_to(table[rows, KC + 1 : KC + 2], (16, LANES))
        total = jnp.zeros((16, LANES), f32)
        for s in range(SLABS):
            cols = t.cols(r, s)
            value = softplus(step_ref[rows, cols] + bias)
            step_ref[rows, cols] = value
            du_ref[rows, cols] = value * acts[rows, cols].astype(f32)
            y_ref[rows, cols] = jnp.zeros((16, LANES), f32)
            total = total + jnp.where(mask[0:1, cols] > 0.0, HUGE, value)
        at = pl.ds(pl.multiple_of(r * channels + i * 16, 16), 16)
        for k in range(7):
            wf[k, at, :] = total
            total = total + pltpu.roll(total, 1 << k, 1)
        return carry

    lax.fori_loop(0, channels // 16 * rows_n, prelude, 0)
    save(step_ref, step_out)
    expand = expand_matrix()

    def group(index, carry):
        r, j, i, g = t.split(index)
        rows = t.rows(i)
        nrows = pl.ds(pl.multiple_of(g * (NG * 8), NG * 8), NG * 8)

        @pl.when(j == 0)
        def _():
            if rows_n == 1:
                block = pj[DR:, :]
            else:
                block = pj[DR:, pl.ds(pl.multiple_of(r * SEQ_LEN, SEQ_LEN), SEQ_LEN)]
            b8[...] = dot_nn(expand, block[0:DS].astype(f32), highest)
            c8[...] = dot_nn(expand, block[DS:].astype(f32), highest)

        def tile(ref, s):
            return ref[rows, t.cols(r, s)].reshape(1, CT, 8, LANES)

        def state(ref, s):
            return ref[nrows, slab(s)].reshape(NG, 1, 8, LANES)

        dec = decb[pl.ds(g * NG, NG), rows, :].reshape(NG, CT, 8, LANES)
        h = jnp.zeros((NG, CT, 8, LANES), f32)
        for s in range(SLABS):
            stepk = jnp.where(mask[0:1, t.cols(r, s)] > 0.0, HUGE, step_ref[rows, t.cols(r, s)])
            a = jnp.exp2(dec * stepk.reshape(1, CT, 8, LANES))
            a_scr[s] = a
            h = a * h + state(b8, s) * tile(du_ref, s)
        at = pl.ds(pl.multiple_of(r * channels + i * t.span, t.span), t.span)
        for k in range(7):
            gain = jnp.exp2(dec * wf[k, at, :].reshape(1, CT, 8, LANES))
            h = h + gain * pltpu.roll(h, 1 << k, 3)
        h = pltpu.roll(h, 1, 3)
        h0[pl.ds(r * DS + g * NG, NG), rows, :] = h.reshape(NG, t.span, LANES)
        for s in range(SLABS):
            h = a_scr[s] * h + state(b8, s) * tile(du_ref, s)
            y_ref[rows, t.cols(r, s)] += jnp.sum(state(c8, s) * h, axis=0).reshape(t.span, LANES)
        return carry

    for segment in range(SEGMENTS):
        t.loop(segment, group)
        if segment + 2 >= SEGMENTS:
            for q in range(PIECES // 2):
                second.pass_on(q + (segment + 2 - SEGMENTS) * PIECES // 2)
    save(h0, h0_out)

    def skip_tile(index, carry):
        i = index // rows_n
        r = index % rows_n
        rows = pl.ds(pl.multiple_of(i * 16, 16), 16)
        skip = jnp.broadcast_to(table[rows, KC + 2 : KC + 3], (16, LANES))
        for s in range(SLABS):
            cols = t.cols(r, s)
            y = y_ref[rows, cols] + skip * acts[rows, cols].astype(f32)
            gated[rows, cols] = (y * gs[rows, cols]).astype(bf16)
            y_ref[rows, cols] = y * slope[rows, cols]
        return carry

    lax.fori_loop(0, channels // 16 * rows_n, skip_tile, 0)
    save(gated, gated_out)
    low = outw_ref[...].astype(bf16)
    for q in range(PIECES):
        second.arrive(q)
        for r in range(rows_n):
            block = cg[r, q * step : (q + 1) * step].reshape(span, width)
            cols = slice((r * PIECES + q) * span, (r * PIECES + q + 1) * span)
            dgs[:, cols] = dot_nt(low, block)
    save(cg, cg_out)

    def grad_tile(index, carry):
        i = index // rows_n
        r = index % rows_n
        rows = pl.ds(pl.multiple_of(i * 16, 16), 16)
        for s in range(SLABS):
            cols = t.cols(r, s)
            dg = dgs[rows, cols]
            dgate[rows, cols] = (dg * y_ref[rows, cols]).astype(bf16)
            dgs[rows, cols] = dg * gs[rows, cols]
        return carry

    lax.fori_loop(0, channels // 16 * rows_n, grad_tile, 0)
    save(dgs, dy_out)
    save(dgate, dgate_out)
    first.close()
    second.close()
    reduce.close()
    for c in copies:
        c.wait()


def front_call(chan_size, tokens, cotangent, gain, in_weight, x_weight, out_weight, chan_params, dt_weight, resets):
    own_rows, width = tokens.shape
    count = resets.shape[0] * LANES
    channels = out_weight.shape[0]
    chips = chan_size // 2
    rows = count // SEQ_LEN
    wide = (channels, count)
    whole = (rows, SLABS, SEQ_LEN // own_rows, own_rows // SLABS, width)
    project = DR + 2 * DS
    any_spec = pl.BlockSpec(memory_space=pl.ANY)
    vmem = pl.BlockSpec(memory_space=pltpu.VMEM)
    dma = pltpu.SemaphoreType.DMA
    gather_sems = (2, chips, PIECES)
    states = (rows * DS, channels, LANES)
    decays = (DS, channels, LANES)
    outs = [
        (wide, f32), (wide, bf16), (wide, f32), (wide, f32), (wide, bf16), (wide, bf16), ((project, count), bf16),
        (whole, bf16), (whole, bf16), (states, f32), (decays, f32), ((4, count), f32), ((channels, LANES), f32),
    ]
    scratch = [
        (whole, bf16), (whole, bf16), (wide, f32), (wide, f32), (wide, f32), (wide, bf16), (wide, f32),
        ((channels, width), bf16), ((channels, width), bf16),
        ((project, count), f32), ((project, count // 2), f32), ((project, count // 2), bf16),
        ((chips - 1, project, count // 2 // chips), bf16), ((project, count), bf16),
        ((4, count), f32), ((channels, LANES), f32), ((LANES, channels), f32), ((LANES, count), bf16),
        (wide, f32), (wide, f32), (wide, f32), ((7, rows * channels, LANES), f32),
        ((DS * 8, SEQ_LEN), f32), ((DS * 8, SEQ_LEN), f32), (decays, f32), (states, f32),
        ((SLABS, NG, CT, 8, LANES), f32), (wide, bf16), (wide, bf16),
    ]
    return pl.pallas_call(
        functools.partial(front_kernel, chan_size),
        in_specs=[vmem] * 9,
        out_specs=[any_spec] * len(outs),
        out_shape=[jax.ShapeDtypeStruct(*o) for o in outs],
        scratch_shapes=[pltpu.VMEM(*s) for s in scratch]
        + [dma(gather_sems)] * 4
        + [dma((PIECES,))] * 2
        + [dma((2 * chips,))] * 2
        + [dma((len(outs),))],
        compiler_params=pltpu.CompilerParams(collective_id=0, has_side_effects=True, vmem_limit_bytes=60 * MIB),
        name="front",
    )(tokens, cotangent, gain, in_weight, x_weight, out_weight, chan_params, dt_weight, resets)


def back_kernel(
    chan_size, seq_size,
    table, mask, xw_ref,
    gated_in, outw_in, cot_in, step_in, act_in, pj_in, dec_in, dy_in, h0_in, dgate_in, normed_in, inw_in, x_in,
    msum_ref, dsum_ref, za_out, zb_out, zc_out, gsum_ref,
    gated, outw, step_ref, act, pjf, decb, dy, h0, dgate, inw, rows_buf, low, dx, dc, taps_red, gin1,
    du, s1, ds2, wb, b8, c8, db8, dc8, red, a_scr, ah_scr, padded, pback,
    part, pair_buf, land, from_pair, pair, from_chips, pj,
    za, zb, zc, zha, zhb, zhc, gp, gz, gc,
    in_sem, out_sem, m_s1, m_r1, m_s2, m_r2, d_s1, d_r1, d_s2, d_r2,
    rd_send, rd_recv, z_send, z_recv, gz_send, gz_recv, gc_send, gc_recv,
):
    here = Here(chan_size)
    channels, tokens = gated.shape
    rows_n = pair_buf.shape[0]
    width = outw.shape[1]
    project = pj.shape[0]
    t = Tiles(channels, rows_n)
    tile_count = channels // 16 * rows_n

    loads = {}
    for index, (name, src, dst) in enumerate(
        (
            ("gated", gated_in, gated), ("outw", outw_in, outw), ("cot", cot_in.at[0], rows_buf.at[0]),
            ("step", step_in, step_ref), ("act", act_in, act), ("pj", pj_in, pjf), ("dec", dec_in, decb),
            ("dy", dy_in, dy), ("h0", h0_in, h0), ("dgate", dgate_in, dgate),
            ("normed", normed_in.at[0], rows_buf.at[1]), ("inw", inw_in, inw), ("x", x_in, du),
        )
    ):
        loads[name] = pltpu.make_async_copy(src, dst, in_sem.at[index])
        if name != "x":
            loads[name].start()

    barrier = pltpu.get_barrier_semaphore()
    for k in range(1, chan_size):
        pl.semaphore_signal(barrier, inc=1, device_id=(here.seq, flip(here.chan, k)), device_id_type=MESH)
    for k in range(1, seq_size):
        pl.semaphore_signal(barrier, inc=1, device_id=(flip(here.seq, k), here.chan), device_id_type=MESH)

    reduce = Reduce(here, pback, from_pair, pair, from_chips, pj, rd_send, rd_recv)
    mixed = Scatter(here, part, pair_buf, land, m_s1, m_r1, m_s2, m_r2)
    normed_grad = Scatter(here, part, pair_buf, land, d_s1, d_r1, d_s2, d_r2)
    sum_a = SeqSum(here, seq_size, za, zha, z_send.at[0], z_recv.at[0])
    sum_b = SeqSum(here, seq_size, zb, zhb, z_send.at[1], z_recv.at[1])
    sum_c = SeqSum(here, seq_size, zc, zhc, z_send.at[2], z_recv.at[2])
    if za.shape[0] > channels:
        for buf in (za, zb, zc):
            buf[channels:, :] = jnp.zeros((buf.shape[0] - channels, buf.shape[1]), bf16)

    def cols_of(r, s):
        return slice((r * SLABS + s) * LANES, (r * SLABS + s + 1) * LANES)

    def row_block(slot):
        return rows_buf[slot].reshape(SEQ_LEN, width)

    def row_cols(r):
        return slice(r * SEQ_LEN, (r + 1) * SEQ_LEN)

    def fetch(src, r, slot, name):
        index = list(loads).index(name)
        c = pltpu.make_async_copy(src.at[r], rows_buf.at[slot], in_sem.at[index])
        c.start()
        return c

    loads["gated"].wait()
    loads["outw"].wait()
    low[0] = outw[...].astype(bf16)
    pl.semaphore_wait(barrier, chan_size - 1 + seq_size - 1)
    mixed.produce(lambda r, s: dot_tn(gated[:, cols_of(r, s)], low[0]))
    loads["cot"].wait()
    out_grad = dot_nn(gated[:, row_cols(0)], row_block(0))
    for r in range(1, rows_n):
        fetch(cot_in, r, 0, "cot").wait()
        out_grad = out_grad + dot_nn(gated[:, row_cols(r)], row_block(0))
    za[0:channels, :] = out_grad.astype(bf16)
    sum_a.start()
    mixed.send()
    loads["dgate"].wait()
    loads["normed"].wait()
    in_grad = dot_nn(dgate[:, row_cols(0)], row_block(1))
    for r in range(1, rows_n):
        fetch(normed_in, r, 1, "normed").wait()
        in_grad = in_grad + dot_nn(dgate[:, row_cols(r)], row_block(1))
    gin1[...] = in_grad
    zb[0:channels, :] = in_grad.astype(bf16)
    sum_b.start()
    loads["inw"].wait()
    low[0] = inw[0].astype(bf16)
    low[1] = inw[1].astype(bf16)

    for name in ("step", "act", "pj", "dec", "dy", "h0"):
        loads[name].wait()
    padded[...] = jnp.zeros_like(padded)
    padded[DT_COL : DT_COL + DR, :] = pjf[0:DR, :]
    red[...] = jnp.zeros_like(red)

    def prelude(index, carry):
        i = index // rows_n
        r = index % rows_n
        rows = pl.ds(pl.multiple_of(i * 16, 16), 16)
        total = jnp.zeros((16, LANES), f32)
        for s in range(SLABS):
            cols = t.cols(r, s)
            value = step_ref[rows, cols]
            du[rows, cols] = value * act[rows, cols].astype(f32)
            s1[rows, cols] = jnp.zeros((16, LANES), f32)
            ds2[rows, cols] = jnp.zeros((16, LANES), f32)
            total = total + jnp.where(mask[0:1, cols] > 0.0, HUGE, value)
        at = pl.ds(pl.multiple_of(r * channels + i * 16, 16), 16)
        for k in range(7):
            wb[k, at, :] = total
            total = total + pltpu.roll(total, LANES - (1 << k), 1)
        return carry

    lax.fori_loop(0, tile_count, prelude, 0)
    expand = expand_matrix()

    def group(index, carry):
        r, j, i, g = t.split(index)
        rows = t.rows(i)
        nrows = pl.ds(pl.multiple_of(g * (NG * 8), NG * 8), NG * 8)
        whole_row = slice(0, SEQ_LEN) if rows_n == 1 else pl.ds(pl.multiple_of(r * SEQ_LEN, SEQ_LEN), SEQ_LEN)

        @pl.when(j == 0)
        def _():
            block = pjf[DR:, whole_row]
            b8[...] = dot_nn(expand, block[0:DS].astype(f32), highest)
            c8[...] = dot_nn(expand, block[DS:].astype(f32), highest)
            db8[...] = jnp.zeros_like(db8)
            dc8[...] = jnp.zeros_like(dc8)

        def tile(ref, s):
            return ref[rows, t.cols(r, s)].reshape(1, CT, 8, LANES)

        def state(ref, s):
            return ref[nrows, slab(s)].reshape(NG, 1, 8, LANES)

        dec = decb[pl.ds(g * NG, NG), rows, :].reshape(NG, CT, 8, LANES)
        h = h0[pl.ds(r * DS + g * NG, NG), rows, :].reshape(NG, CT, 8, LANES)
        for s in range(SLABS):
            stepk = jnp.where(mask[0:1, t.cols(r, s)] > 0.0, HUGE, step_ref[rows, t.cols(r, s)])
            a = jnp.exp2(dec * stepk.reshape(1, CT, 8, LANES))
            a_scr[s] = a
            ah = a * h
            ah_scr[s] = ah
            h = ah + state(b8, s) * tile(du, s)
            dc8[nrows, slab(s)] += jnp.sum(tile(dy, s) * h, axis=1).reshape(NG * 8, LANES)
        p = jnp.zeros((NG, CT, 8, LANES), f32)
        for s in reversed(range(SLABS)):
            p = a_scr[s] * (tile(dy, s) * state(c8, s) + p)
        at = pl.ds(pl.multiple_of(r * channels + i * t.span, t.span), t.span)
        for k in range(7):
            gain = jnp.exp2(dec * wb[k, at, :].reshape(1, CT, 8, LANES))
            p = p + gain * pltpu.roll(p, LANES - (1 << k), 3)
        p = pltpu.roll(p, LANES - 1, 3)
        rate = jnp.zeros((NG, CT, 8, LANES), f32)
        for s in reversed(range(SLABS)):
            lam = tile(dy, s) * state(c8, s) + p
            p = a_scr[s] * lam
            s1[rows, t.cols(r, s)] += jnp.sum(lam * state(b8, s), axis=0).reshape(t.span, LANES)
            db8[nrows, slab(s)] += jnp.sum(lam * tile(du, s), axis=1).reshape(NG * 8, LANES)
            q = lam * ah_scr[s]
            ds2[rows, t.cols(r, s)] += jnp.sum(dec * q, axis=0).reshape(t.span, LANES)
            rate = rate + q * tile(step_ref, s)
        for n in range(NG):
            cols = pl.ds(pl.multiple_of((g * NG + n) * LANES, LANES), LANES)
            red[rows, cols] += rate[n].reshape(t.span, LANES)

        @pl.when(j == t.per_row - 1)
        def _():
            pback[DR : DR + DS, whole_row] = dot_tn(expand, db8[...], highest).astype(bf16)
            pback[DR + DS :, whole_row] = dot_tn(expand, dc8[...], highest).astype(bf16)

        return carry

    levels = seq_size.bit_length() - 1
    for segment in range(SEGMENTS):
        t.loop(segment, group)
        if segment == 1:
            sum_a.step(0)
            sum_b.step(0)
        if segment + 1 == SEGMENTS:
            for i in range(1, levels):
                sum_a.step(i)
                sum_b.step(i)
            mixed.finish(msum_ref)
    loads["x"].start()
    x_buf = du

    def adjoint_tile(index, carry):
        i = index // rows_n
        r = index % rows_n
        rows = pl.ds(pl.multiple_of(i * 16, 16), 16)
        skip = jnp.broadcast_to(table[rows, KC + 2 : KC + 3], (16, LANES))
        skip_sum = jnp.zeros((16, LANES), f32)
        bias_sum = jnp.zeros((16, LANES), f32)
        for s in range(SLABS):
            cols = t.cols(r, s)
            value = step_ref[rows, cols]
            lam_b = s1[rows, cols]
            d_y = dy[rows, cols]
            act_s = act[rows, cols].astype(f32)
            s1[rows, cols] = d_y * skip + lam_b * value
            small = value * (1.0 - value * (0.5 - value * (1.0 / 6.0)))
            slope = jnp.where(value < 0.01, small, 1.0 - jnp.exp(-value))
            back = ((lam_b * act_s + LN2 * ds2[rows, cols]) * slope).astype(bf16)
            dx[rows, cols] = back
            skip_sum = skip_sum + d_y * act_s
            bias_sum = bias_sum + back.astype(f32)
        red[rows, DS * LANES : (DS + 1) * LANES] += skip_sum
        red[rows, (DS + 1) * LANES :] += bias_sum
        return carry

    lax.fori_loop(0, tile_count, adjoint_tile, 0)
    low_table = table[...].astype(bf16)
    for r in range(rows_n):
        pback[0:DR, row_cols(r)] = dot_tn(low_table, dx[:, row_cols(r)])[DT_COL : DT_COL + DR].astype(bf16)
    reduce.step1()
    pick = jnp.where(iota(((DS + 2) * LANES, LANES), 0) // LANES == iota(((DS + 2) * LANES, LANES), 1), 1.0, 0.0)
    zc[0:channels, width + LANES :] = (dot_nn(red[...], pick, highest) + dot_nt(dx[...], padded[...])).astype(bf16)
    reduce.step2()
    reduce.step3()
    reduce.step4()
    saves = sum_a.finish(za_out, out_sem.at[0])
    saves += sum_b.finish(zb_out, out_sem.at[1])
    loads["x"].wait()
    x_low = xw_ref[...].astype(bf16)
    reduce.step5()
    for r in range(rows_n):
        s1[:, row_cols(r)] += dot_tn(x_low, pj[:, row_cols(r)])

    def conv_tile(index, carry):
        i = index // rows_n
        r = index % rows_n
        rows = pl.ds(pl.multiple_of(i * 16, 16), 16)
        taps = [jnp.broadcast_to(table[rows, k : k + 1], (16, LANES)) for k in range(KC + 1)]
        earlier = {s: pltpu.roll(x_buf[rows, t.cols(r, s)], 1, 1) for s in range(SLABS - KC + 1, SLABS)}
        sums = [jnp.zeros((16, LANES), f32) for _ in range(KC + 1)]
        for s in range(SLABS):
            cols = t.cols(r, s)
            inputs = []
            conv = taps[KC]
            for j in range(KC):
                value = x_buf[rows, t.cols(r, s - j)] if s >= j else earlier[SLABS + s - j]
                if j > 0:
                    value = value * mask[j : j + 1, cols]
                inputs.append(value)
                conv = conv + taps[KC - 1 - j] * value
            sig = jax.nn.sigmoid(conv)
            d_conv = s1[rows, cols] * (sig * (1.0 + conv * (1.0 - sig)))
            dc[:, slab(s)] = d_conv
            for j in range(KC):
                sums[KC - 1 - j] = sums[KC - 1 - j] + d_conv * inputs[j]
            sums[KC] = sums[KC] + d_conv
        wrapped = {}
        for s in range(KC - 1):
            for j in range(s + 1, KC):
                wrapped[s, j] = pltpu.roll(dc[:, slab(s)] * mask[j : j + 1, t.cols(r, s)], LANES - 1, 1)
        for s in range(SLABS):
            d_x = taps[KC - 1] * dc[:, slab(s)]
            for j in range(1, KC):
                if s + j < SLABS:
                    value = dc[:, slab(s + j)] * mask[j : j + 1, t.cols(r, s + j)]
                else:
                    value = wrapped[s + j - SLABS, j]
                d_x = d_x + taps[KC - 1 - j] * value
            dx[rows, t.cols(r, s)] = d_x.astype(bf16)
        for k in range(KC + 1):
            @pl.when(r == 0)
            def _():
                taps_red[rows, slab(k)] = sums[k]

            @pl.when(r > 0)
            def _():
                taps_red[rows, slab(k)] += sums[k]
        return carry

    lax.fori_loop(0, tile_count, conv_tile, 0)

    normed_grad.produce(
        lambda r, s: dot_tn(dx[:, cols_of(r, s)], low[0]) + dot_tn(dgate[:, cols_of(r, s)], low[1])
    )
    normed_grad.send()

    if rows_n > 1:
        fetch(normed_in, 0, 1, "normed").wait()
    in_grad = dot_nn(dx[:, row_cols(0)], row_block(1))
    for r in range(1, rows_n):
        fetch(normed_in, r, 1, "normed").wait()
        in_grad = in_grad + dot_nn(dx[:, row_cols(r)], row_block(1))
    zc[0:channels, 0:width] = in_grad.astype(bf16)
    x_grad = dot_nt(act[...], pj[...])
    x_grad = jnp.concatenate([x_grad, jnp.zeros((channels, LANES - project), f32)], axis=1)
    k_i = iota(((KC + 1) * LANES, LANES), 0)
    pick = jnp.where(k_i // LANES + project == iota(((KC + 1) * LANES, LANES), 1), 1.0, 0.0)
    zc[0:channels, width : width + LANES] = (x_grad + dot_nn(taps_red[...], pick, highest)).astype(bf16)
    sum_c.start()

    both = low[0].astype(f32) * in_grad + low[1].astype(f32) * gin1[...]
    gp[...] = jnp.sum(both.reshape(channels // 8, 8, width), axis=0)

    def gain_seq(k):
        return pltpu.make_async_remote_copy(
            src_ref=gp, dst_ref=gz.at[k - 1], send_sem=gz_send.at[k - 1], recv_sem=gz_recv.at[k - 1],
            device_id=(flip(here.seq, k), here.chan), device_id_type=MESH,
        )

    def gain_chan(k):
        return here.copy(gz.at[seq_size - 1], gc.at[k - 1], gc_send.at[k - 1], gc_recv.at[k - 1], flip(here.chan, k))

    for k in range(1, seq_size):
        gain_seq(k).start()
    for k in range(1, seq_size):
        gain_seq(k).wait()
    total = gp[...]
    for k in range(1, seq_size):
        total = total + gz[k - 1]
    gz[seq_size - 1] = total
    for k in range(1, chan_size):
        gain_chan(k).start()
    for i in range(levels):
        sum_c.step(i)
    for k in range(1, chan_size):
        gain_chan(k).wait()
        total = total + gc[k - 1]
    gsum_ref[...] = total
    normed_grad.finish(dsum_ref)
    saves += sum_c.finish(zc_out, out_sem.at[2])
    reduce.close()
    for c in saves:
        c.wait()


def back_call(
    chan_size, seq_size, own_rows, table, masks, x_weight, gated, out_weight, cot_all, step, act, pj, decays, dy, h0,
    dgate, normed_all, in_weight, x_cols,
):
    channels, width = out_weight.shape
    count = masks.shape[1]
    chips = chan_size // 2
    rows = count // SEQ_LEN
    per_row = SEQ_LEN // own_rows // 2
    lanes = own_rows // SLABS
    project = DR + 2 * DS
    wide = (channels, count)
    padded = (channels + 31) // 32 * 32
    levels = seq_size.bit_length() - 1
    any_spec = pl.BlockSpec(memory_space=pl.ANY)
    vmem = pl.BlockSpec(memory_space=pltpu.VMEM)
    dma = pltpu.SemaphoreType.DMA
    sums = ((padded, width), (padded, width), (padded, width + 2 * LANES))
    states = (DS * 8, SEQ_LEN)
    loops = (SLABS, NG, CT, 8, LANES)
    outs = [
        ((own_rows, width), f32), ((own_rows, width), f32), (sums[0], bf16), (sums[1], bf16), (sums[2], bf16),
        ((8, width), f32),
    ]
    scratch = [
        (wide, bf16), ((channels, width), f32), (wide, f32), (wide, bf16), ((project, count), bf16),
        ((DS, channels, LANES), f32), (wide, f32), ((rows * DS, channels, LANES), f32), (wide, bf16),
        ((2, channels, width), f32), ((2, SLABS, 2 * per_row, lanes, width), bf16),
        ((2, channels, width), bf16), (wide, bf16), ((16, SEQ_LEN), f32), ((channels, (KC + 1) * LANES), f32),
        ((channels, width), f32),
        (wide, f32), (wide, f32), (wide, f32), ((7, rows * channels, LANES), f32),
        (states, f32), (states, f32), (states, f32), (states, f32), ((channels, (DS + 2) * LANES), f32),
        (loops, f32), (loops, f32), ((LANES, count), bf16), ((project, count), bf16),
        ((min(rows, 2), SLABS, per_row, 2, lanes, width), bf16), ((rows, SLABS, per_row, lanes, width), bf16),
        ((chips - 1, SLABS, lanes, width), bf16), ((project, count // 2), bf16), ((project, count // 2), bf16),
        ((chips - 1, project, count // 2 // chips), bf16), ((project, count), bf16),
        (sums[0], bf16), (sums[1], bf16), (sums[2], bf16),
    ]
    scratch += [((levels + 1, padded // 2, s[1]), bf16) for s in sums]
    scratch += [((8, width), f32), ((seq_size, 8, width), f32), ((chan_size - 1, 8, width), f32)]
    return pl.pallas_call(
        functools.partial(back_kernel, chan_size, seq_size),
        in_specs=[vmem] * 3 + [any_spec] * 13,
        out_specs=[vmem, vmem, any_spec, any_spec, any_spec, vmem],
        out_shape=[jax.ShapeDtypeStruct(*o) for o in outs],
        scratch_shapes=[pltpu.VMEM(*s) for s in scratch]
        + [dma((13,)), dma((3, 2))]
        + ([dma((rows * PIECES,))] * 2 + [dma((chips * PIECES,))] * 2) * 2
        + [dma((2 * chips,))] * 2
        + [dma((3, levels + 1))] * 2
        + [dma((seq_size,))] * 2
        + [dma((chan_size,))] * 2,
        compiler_params=pltpu.CompilerParams(collective_id=1, has_side_effects=True, vmem_limit_bytes=60 * MIB),
        name="back",
    )(
        table, masks, x_weight, gated, out_weight, cot_all, step, act, pj, decays, dy, h0, dgate, normed_all, in_weight, x_cols
    )


def update(grad, master, first, second, rate, outs):
    new = adamw_core(master, first, second, grad, rate)
    for ref, value in zip(outs, new):
        ref[...] = value
    outs[3][...] = new[0].astype(bf16)


def finish_kernel(
    tok_ref, cot_ref, msum_ref, dsum_ref, za_ref, zb_ref, zc_ref, zb_all, zc_all, gsum_ref,
    gain_m, gain_f, gain_s, in_m, in_f, in_s, x_m, x_f, x_s, dt_m, dt_f, dt_s, out_m, out_f, out_s, ch_m, ch_f, ch_s,
    mixed_ref, tgrad_ref, *rest,
):
    gain_o, in_o, x_o, dt_o, out_o, ch_o = (rest[i * 4 : i * 4 + 4] for i in range(6))
    ch_grad = rest[24]
    i = pl.program_id(0)
    width = tok_ref.shape[1]
    own_rows = msum_ref.shape[0]
    block = tok_ref.shape[0]
    lanes = own_rows // SLABS
    channels = x_m.shape[1]

    r = lax.broadcasted_iota(jnp.int32, (block, own_rows), 0) + i * block
    q = lax.broadcasted_iota(jnp.int32, (block, own_rows), 1)
    order = jnp.where(r == (q % lanes) * SLABS + q // lanes, 1.0, 0.0).astype(bf16)

    def in_order(ref):
        values = ref[...]
        high = values.astype(bf16)
        return dot_nn(order, high) + dot_nn(order, (values - high.astype(f32)).astype(bf16))

    values = tok_ref[...].astype(f32)
    mixed_ref[...] = (values + in_order(msum_ref)).astype(bf16)
    d_normed = in_order(dsum_ref)
    rstd = lax.rsqrt(jnp.mean(values * values, axis=-1, keepdims=True) + norm_epsilon)
    scaled = gain_m[...] * d_normed
    mean = jnp.mean(scaled * values, axis=-1, keepdims=True)
    tgrad_ref[...] = cot_ref[...].astype(f32) + rstd * scaled - values * (rstd * rstd * rstd * mean)

    out_grad = za_ref[...].astype(f32)
    update(out_grad, out_m[...], out_f[...], out_s[...], rate_output, out_o)
    for k, ref in ((0, zc_ref), (1, zb_ref)):
        grad = ref[:, 0:width].astype(f32)
        new = adamw_core(in_m[k], in_f[k], in_s[k], grad, rate_inner)
        for o, value in zip(in_o, new):
            o[k] = value
        in_o[3][k] = new[0].astype(bf16)

    @pl.when(i == 0)
    def _():
        grad_b = zb_all[...].astype(f32).T
        grad_c = zc_all[...].astype(f32).T
        update(grad_b[64 : 64 + DR, 0:channels], dt_m[...], dt_f[...], dt_s[...], rate_step, dt_o)
        project = x_m.shape[0]
        update(grad_c[0:project, 0:channels], x_m[...], x_f[...], x_s[...], rate_project, x_o)
        ch_grad[0 : KC + 1, :] = grad_c[project : project + KC + 1, 0:channels]
        ch_grad[KC + 1 : KC + 2, :] = grad_b[DS + 1 : DS + 2, 0:channels]
        ch_grad[KC + 2 : KC + 3, :] = grad_b[DS : DS + 1, 0:channels]
        ch_grad[KC + 3 :, :] = grad_b[0:DS, 0:channels] * -jnp.exp(ch_m[KC + 3 :, :])
        update(ch_grad[...], ch_m[...], ch_f[...], ch_s[...], rate_channel, ch_o)
        gain_grad = jnp.sum(gsum_ref[...], axis=0, keepdims=True) / gain_m[...]
        update(gain_grad, gain_m[...], gain_f[...], gain_s[...], rate_gain, gain_o)


def finish_call(tokens, cotangent, msum, dsum, za, zb, zc, gsum, gains, inners, projects, steps, outputs, chans):
    own_rows, width = tokens.shape
    channels = outputs[0].shape[0]
    cb = 48 if channels % 48 == 0 else channels
    grid = channels // cb
    block = own_rows // grid
    row = pl.BlockSpec((block, width), lambda i: (i, 0))

    def full(shape):
        return pl.BlockSpec(shape, lambda i: (0,) * len(shape))

    inner = pl.BlockSpec((2, cb, width), lambda i: (0, i, 0))
    outer = pl.BlockSpec((cb, width), lambda i: (i, 0))
    tails = [pl.BlockSpec((zc.shape[0], LANES), lambda i, k=k: (0, width // LANES + k)) for k in (1, 0)]
    zed = pl.BlockSpec((cb, width), lambda i: (i, 0))
    groups = (gains, inners, projects, steps, outputs, chans)
    specs = (full(gains[0].shape), inner, full(projects[0].shape), full(steps[0].shape), outer, full(chans[0].shape))
    in_specs = [row, row, full(msum.shape), full(dsum.shape), zed, zed, zed, *tails, full(gsum.shape)]
    out_specs = [row, row]
    out_shape = [jax.ShapeDtypeStruct(tokens.shape, bf16), jax.ShapeDtypeStruct(tokens.shape, f32)]
    args = [tokens, cotangent, msum, dsum, za, zb, zc, zc, zc, gsum]
    for arrays, spec in zip(groups, specs):
        in_specs += [spec] * 3
        out_specs += [spec] * 4
        out_shape += [jax.ShapeDtypeStruct(arrays[0].shape, f32)] * 3 + [jax.ShapeDtypeStruct(arrays[0].shape, bf16)]
        args += list(arrays)
    return pl.pallas_call(
        finish_kernel,
        grid=(grid,),
        in_specs=in_specs,
        out_specs=out_specs,
        out_shape=out_shape,
        scratch_shapes=[pltpu.VMEM(chans[0].shape, f32)],
        compiler_params=pltpu.CompilerParams(dimension_semantics=("arbitrary",), vmem_limit_bytes=60 * MIB),
        name="finish",
    )(*args)


def per_device(
    tokens,
    resets,
    cotangent,
    norm_gain,
    in_weight,
    x_weight,
    dt_weight,
    out_weight,
    chan_params,
    gain_first,
    gain_second,
    in_first,
    in_second,
    x_first,
    x_second,
    dt_first,
    dt_second,
    out_first,
    out_second,
    chan_first,
    chan_second,
):
    own_count = tokens.shape[0]
    chan_size = lax.axis_size("chan")
    seq_size = lax.axis_size("seq")
    inners = [jnp.swapaxes(a, 1, 2) for a in (in_weight, in_first, in_second)]
    projects = [a.T for a in (x_weight, x_first, x_second)]
    x_cols, act, step, dy, gated, dgate, pj, normed_all, cot_all, h0, decays, masks, table = front_call(
        chan_size, tokens, cotangent, norm_gain[None], inners[0], projects[0], out_weight, chan_params, dt_weight,
        resets.reshape(-1, LANES),
    )
    msum, dsum, za, zb, zc, gsum = back_call(
        chan_size, seq_size, own_count, table, masks, projects[0], gated, out_weight, cot_all, step, act, pj, decays, dy, h0,
        dgate, normed_all, inners[0], x_cols,
    )
    result = finish_call(
        tokens, cotangent, msum, dsum, za, zb, zc, gsum,
        [a[None] for a in (norm_gain, gain_first, gain_second)],
        inners,
        projects,
        (dt_weight, dt_first, dt_second),
        (out_weight, out_first, out_second),
        (chan_params, chan_first, chan_second),
    )
    result = list(result)
    result[2:6] = [a[0] for a in result[2:6]]
    result[6:10] = [jnp.swapaxes(a, 1, 2) for a in result[6:10]]
    result[10:14] = [a.T for a in result[10:14]]
    return tuple(result)


def solution(mesh):
    rows = P(("seq", "chan"), None)
    inner = P(None, None, "chan")
    by_row = P("chan", None)
    by_col = P(None, "chan")
    placed = (rows, P("seq"), rows, P(), inner, by_row, by_col, by_row, by_col, P(), P())
    placed += (inner, inner, by_row, by_row, by_col, by_col, by_row, by_row, by_col, by_col)
    return jax.shard_map(
        per_device,
        mesh=mesh,
        in_specs=placed,
        out_specs=(rows, rows)
        + (P(),) * 4
        + (inner,) * 4
        + (by_row,) * 4
        + (by_col,) * 4
        + (by_row,) * 4
        + (by_col,) * 4,
        check_vma=False,
    )
```

```python
import functools

import jax
import jax.numpy as jnp
from jax import lax
from jax.experimental import pallas as pl
from jax.experimental.pallas import tpu as pltpu
from jax.sharding import PartitionSpec as P

DS = 16
DR = 48
KC = 4
SEQ_LEN = 2048
STEP = 10
SLABS = 16
LANES = 128
NG = 16
CT = 2
SEGMENTS = 4
PIECES = 4
MIB = 1024 * 1024
MESH = pl.DeviceIdType.MESH

highest = lax.Precision.HIGHEST
norm_epsilon = 1e-05
beta_first = 0.9
beta_second = 0.999
adam_epsilon = 1e-08
weight_decay = 0.1
rate_gain = 0.4
rate_inner = 0.05
rate_project = 0.04
rate_step = 0.1
rate_output = 0.08
rate_channel = 0.5
LOG2E = 1.4426950408889634
LN2 = 0.6931471805599453
HUGE = 1e30
f32 = jnp.float32
bf16 = jnp.bfloat16


def adamw_core(master, moment_one, moment_two, gradient, rate_value):
    first_new = beta_first * moment_one + (1.0 - beta_first) * gradient
    second_new = beta_second * moment_two + (1.0 - beta_second) * gradient * gradient
    scale = jnp.sqrt(second_new * (1.0 / (1.0 - beta_second**STEP))) + adam_epsilon
    corrected = first_new * (rate_value / (1.0 - beta_first**STEP)) / scale
    master_new = master * (1.0 - rate_value * weight_decay) - corrected
    return (master_new, first_new, second_new)


def dot_nn(a, b, precision=None):
    return lax.dot_general(a, b, (((1,), (0,)), ((), ())), precision=precision, preferred_element_type=f32)


def dot_nt(a, b, precision=None):
    return lax.dot_general(a, b, (((1,), (1,)), ((), ())), precision=precision, preferred_element_type=f32)


def dot_tn(a, b, precision=None):
    return lax.dot_general(a, b, (((0,), (0,)), ((), ())), precision=precision, preferred_element_type=f32)


def slab(s):
    return slice(s * LANES, (s + 1) * LANES)


def flip(index, bits):
    result = index
    place = 1
    while place <= bits:
        if bits & place:
            result = result + place * (1 - 2 * ((index // place) % 2))
        place *= 2
    return result


class Here:
    def __init__(self, chan_size):
        self.seq = lax.axis_index("seq")
        self.chan = lax.axis_index("chan")
        self.chips = chan_size // 2
        self.core = self.chan % 2
        self.chip = self.chan // 2
        self.partner = self.chan + 1 - 2 * self.core

    def same_core(self, k):
        return flip(self.chip, k) * 2 + self.core

    def other_core(self, k):
        return flip(self.chip, k) * 2 + 1 - self.core

    def copy(self, src, dst, send, recv, chan):
        return pltpu.make_async_remote_copy(
            src_ref=src, dst_ref=dst, send_sem=send, recv_sem=recv,
            device_id=(self.seq, chan), device_id_type=MESH,
        )


class Gather:
    def __init__(self, here, buf, hop, send, recv, rsend, rrecv, fsend, frecv):
        self.here, self.buf, self.hop = here, buf, hop
        self.send, self.recv, self.rsend, self.rrecv = send, recv, rsend, rrecv
        self.fsend, self.frecv = fsend, frecv
        self.half = PIECES // 2

    def place(self, j, q):
        per_row = self.buf.shape[2]
        step = SLABS // PIECES
        return self.buf.at[j // per_row, pl.ds(q * step, step), j % per_row]

    def direct(self, k, q, shard):
        h = self.here
        to = h.partner if k == 0 else h.same_core(k)
        return h.copy(self.place(shard, q), self.place(shard, q), self.send.at[k, q], self.recv.at[k, q], to)

    def relay(self, k, q, shard):
        return self.here.copy(
            self.place(shard, q), self.place(shard, q), self.rsend.at[k, q], self.rrecv.at[k, q], self.here.partner
        )

    def onward(self, q, shard, k):
        return self.here.copy(
            self.place(shard, q), self.place(shard, q), self.fsend.at[q], self.frecv.at[q], self.here.same_core(k)
        )

    def pieces(self, k):
        every = list(range(PIECES))
        return every[self.half :] + every[: self.half] if k == 1 else every

    def start(self):
        h = self.here
        for i in range(PIECES):
            for k in range(1, 3 if self.hop else h.chips):
                self.direct(k, self.pieces(k)[i] if self.hop else i, h.chan).start()
        for q in range(PIECES):
            self.direct(0, q, h.chan).start()

    def take(self, k, q):
        shard = self.here.same_core(k)
        self.direct(k, q, shard).wait_recv()
        if self.hop and (q >= self.half) == (k == 1):
            self.onward(q, shard, 3 - k).start()
        self.relay(k, q, shard).start()

    def take_across(self, q):
        shard = self.here.same_core(3)
        self.onward(q, shard, 1).wait_recv()
        self.relay(3, q, shard).start()

    def pass_on(self, i):
        if not self.hop:
            if i < PIECES:
                for k in range(1, self.here.chips):
                    self.take(k, i)
        elif i < PIECES:
            self.take(1, self.pieces(1)[i])
            self.take(2, self.pieces(2)[i])
        else:
            for q in range(self.half):
                self.take_across(q)
                self.take_across(self.half + q)

    def arrive(self, q):
        self.direct(0, q, self.here.partner).wait_recv()
        for k in range(1, self.here.chips):
            self.relay(k, q, self.here.other_core(k)).wait_recv()

    def close(self):
        for q in range(PIECES):
            for k in range(3 if self.hop else self.here.chips):
                self.direct(k, q, self.here.chan).wait_send()
            if self.hop:
                k = 1 if q >= self.half else 2
                self.onward(q, self.here.same_core(k), 3 - k).wait_send()
            for k in range(1, self.here.chips):
                self.relay(k, q, self.here.same_core(k)).wait_send()


class Reduce:
    def __init__(self, here, part, from_pair, pair, from_chips, total, send, recv):
        self.here, self.part, self.from_pair, self.pair = here, part, from_pair, pair
        self.from_chips, self.total, self.send, self.recv = from_chips, total, send, recv
        self.half = part.shape[1] // 2
        self.own = self.half // here.chips

    def half_cols(self, core):
        return pl.ds(pl.multiple_of(core * self.half, LANES), self.half)

    def own_cols(self, chip):
        return pl.ds(pl.multiple_of(chip * self.own, LANES), self.own)

    def own_total(self, chip):
        start = pl.multiple_of(self.here.core * self.half + chip * self.own, LANES)
        return self.total.at[:, pl.ds(start, self.own)]

    def swap(self):
        h = self.here
        return h.copy(
            self.part.at[:, self.half_cols(1 - h.core)], self.from_pair, self.send.at[0], self.recv.at[0], h.partner
        )

    def scatter(self, k):
        h = self.here
        return h.copy(
            self.pair.at[:, self.own_cols(flip(h.chip, k))], self.from_chips.at[k - 1],
            self.send.at[k], self.recv.at[k], h.same_core(k),
        )

    def spread(self, k, chip):
        h = self.here
        index = h.chips + k
        return h.copy(
            self.own_total(chip), self.own_total(chip), self.send.at[index], self.recv.at[index], h.same_core(k)
        )

    def share(self, core):
        h = self.here
        cols = self.total.at[:, self.half_cols(core)]
        return h.copy(cols, cols, self.send.at[h.chips], self.recv.at[h.chips], h.partner)

    def step1(self):
        self.swap().start()

    def step2(self):
        self.swap().wait()
        pair = self.part[:, self.half_cols(self.here.core)].astype(f32) + self.from_pair[...].astype(f32)
        self.from_pair[...] = pair.astype(self.from_pair.dtype)
        self.pair[...] = pair.astype(bf16)
        for k in range(1, self.here.chips):
            self.scatter(k).start()

    def step3(self):
        total = self.from_pair[:, self.own_cols(self.here.chip)].astype(f32)
        for k in range(1, self.here.chips):
            self.scatter(k).wait_recv()
            total = total + self.from_chips[k - 1].astype(f32)
        start = pl.multiple_of(self.here.core * self.half + self.here.chip * self.own, LANES)
        self.total[:, pl.ds(start, self.own)] = total.astype(bf16)
        for k in range(1, self.here.chips):
            self.spread(k, self.here.chip).start()

    def step4(self):
        for k in range(1, self.here.chips):
            self.spread(k, flip(self.here.chip, k)).wait_recv()
        self.share(self.here.core).start()

    def step5(self):
        self.share(1 - self.here.core).wait_recv()

    def close(self):
        for k in range(1, self.here.chips):
            self.scatter(k).wait_send()
            self.spread(k, self.here.chip).wait_send()
        self.share(self.here.core).wait_send()


def reorder(own_rows):
    lanes = own_rows // SLABS
    r = lax.broadcasted_iota(jnp.int32, (own_rows, own_rows), 0)
    q = lax.broadcasted_iota(jnp.int32, (own_rows, own_rows), 1)
    return jnp.where(q == (r % lanes) * SLABS + r // lanes, 1.0, 0.0)


class Scatter:
    def __init__(self, here, part, pair, landed, send1, recv1, send2, recv2):
        self.here, self.part, self.pair, self.landed = here, part, pair, landed
        self.send1, self.recv1, self.send2, self.recv2 = send1, recv1, send2, recv2
        self.slots, self.rows, self.per_row = part.shape[0], pair.shape[0], pair.shape[2]

    def slabs(self, q):
        step = SLABS // PIECES
        return pl.ds(q * step, step)

    def swap(self, r, q):
        h = self.here
        index = r * PIECES + q
        return h.copy(
            self.part.at[r % self.slots, self.slabs(q), :, 1 - h.core], self.pair.at[r, self.slabs(q)],
            self.send1.at[index], self.recv1.at[index], h.partner,
        )

    def out(self, k, q):
        h = self.here
        chip = flip(h.chip, k)
        index = (k - 1) * PIECES + q
        return h.copy(
            self.pair.at[chip // self.per_row, self.slabs(q), chip % self.per_row],
            self.landed.at[k - 1, self.slabs(q)],
            self.send2.at[index], self.recv2.at[index], h.same_core(k),
        )

    def add(self, r, q):
        step = SLABS // PIECES
        self.swap(r, q).wait()
        for s in range(q * step, (q + 1) * step):
            mine = self.part[r % self.slots, s, :, self.here.core].astype(f32)
            self.pair[r, s] = (self.pair[r, s].astype(f32) + mine).astype(bf16)

    def produce(self, partial, pipelined, between):
        step = SLABS // PIECES
        _, _, per_row, _, lanes, width = self.part.shape
        for r in range(self.rows):
            for q in range(PIECES):
                start = (r * SLABS + q * step) * LANES
                rows = partial(slice(start, start + step * LANES)).astype(bf16)
                self.part[r % self.slots, q * step : (q + 1) * step] = rows.reshape(step, per_row, 2, lanes, width)
                self.swap(r, q).start()
                if pipelined and r + 1 == self.rows and q > 0:
                    self.send(q - 1)
                    if q == 1:
                        between()
            if r + 1 < self.rows:
                for q in range(PIECES):
                    self.add(r, q)

    def send(self, q):
        self.add(self.rows - 1, q)
        for k in range(1, self.here.chips):
            self.out(k, q).start()

    def finish(self, result):
        h = self.here
        lanes = self.part.shape[4]
        for q in range(PIECES):
            for k in range(1, h.chips):
                self.out(k, q).wait()
        for s in range(SLABS):
            total = self.pair[h.chip // self.per_row, s, h.chip % self.per_row].astype(f32)
            for k in range(1, h.chips):
                total = total + self.landed[k - 1, s].astype(f32)
            result[s * lanes : (s + 1) * lanes, :] = total


class SeqSum:
    def __init__(self, here, seq_size, buf, half_in, send, recv):
        self.here, self.size, self.buf, self.half_in = here, seq_size, buf, half_in
        self.send, self.recv = send, recv
        self.half = buf.shape[0] // 2
        self.levels = seq_size.bit_length() - 1

    def rows(self, side):
        return pl.ds(pl.multiple_of(side * self.half, 16), self.half)

    def copy(self, index, src, dst, bit):
        h = self.here
        return pltpu.make_async_remote_copy(
            src_ref=src, dst_ref=dst, send_sem=self.send.at[index], recv_sem=self.recv.at[index],
            device_id=(flip(h.seq, bit), h.chan), device_id_type=MESH,
        )

    def level(self, i):
        side = self.here.seq % 2
        rows = self.rows(1 - side) if i == 0 else self.rows(side)
        return self.copy(i, self.buf.at[rows], self.half_in.at[i], 1 << i)

    def back(self):
        return self.copy(self.levels, self.buf.at[self.rows(self.here.seq % 2)], self.half_in.at[self.levels], 1)

    def start(self):
        self.level(0).start()

    def step(self, i):
        side = self.here.seq % 2
        self.level(i).wait()
        rows = self.rows(side)
        total = self.buf[rows, :].astype(f32) + self.half_in[i].astype(f32)
        self.buf[rows, :] = total.astype(bf16)
        if i + 1 < self.levels:
            self.level(i + 1).start()
        else:
            self.back().start()

    def finish(self, out, sems):
        side = self.here.seq % 2
        self.back().wait()
        copies = [
            pltpu.make_async_copy(self.buf.at[self.rows(side)], out.at[self.rows(side)], sems.at[0]),
            pltpu.make_async_copy(self.half_in.at[self.levels], out.at[self.rows(1 - side)], sems.at[1]),
        ]
        for c in copies:
            c.start()
        return copies


def iota(shape, dim):
    return lax.broadcasted_iota(jnp.int32, shape, dim)


def row_masks(resets_ref, mask_ref):
    per_row = SEQ_LEN // LANES
    chunk, place = iota((SLABS, LANES), 1), iota((SLABS, LANES), 0)
    group = LANES // SLABS
    pick_row = jnp.where(iota((LANES, per_row), 0) // group == iota((LANES, per_row), 1), 1.0, 0.0).astype(bf16)
    pick_place = jnp.where(iota((SLABS, LANES), 1) % SLABS == iota((SLABS, LANES), 0), 1.0, 0.0).astype(bf16)
    own_chunk = iota((LANES, LANES), 1) // SLABS == iota((LANES, LANES), 0) % group

    def before(values):
        moved = pltpu.roll(values, 1, 0)
        return jnp.where(place == 0, pltpu.roll(moved, 1, 1), moved)

    for r in range(mask_ref.shape[1] // SEQ_LEN):
        block = resets_ref[r * per_row : (r + 1) * per_row, :].astype(f32).astype(bf16)
        spread = jnp.where(own_chunk, dot_nn(pick_row, block), 0.0).astype(bf16)
        start = dot_nt(pick_place, spread)
        start = jnp.where((place == 0) & (chunk == 0), 1.0, start)
        keep1 = 1.0 - start
        keep2 = keep1 * before(keep1)
        keep3 = keep2 * before(before(keep1))
        for s in range(SLABS):
            cols = slice(r * SEQ_LEN + s * LANES, r * SEQ_LEN + (s + 1) * LANES)
            for j, values in enumerate((start, keep1, keep2, keep3)):
                mask_ref[j : j + 1, cols] = values[s : s + 1, :]


DECAY_COL = 8
DT_COL = 64


def softplus(values):
    e = jnp.exp(-jnp.abs(values))
    return jnp.maximum(values, 0.0) + jnp.where(e < 1e-3, e * (1.0 - e * (0.5 - e * (1.0 / 3.0))), jnp.log(1.0 + e))


def tall(channels):
    return 48 if channels % 48 == 0 else 16


def windows(total_ref, window_ref, later):
    channels = total_ref.shape[0]
    part = 96 if channels % 96 == 0 else channels
    for start in range(0, channels, part):
        rows = slice(start, start + part)
        total = total_ref[rows, :]
        for k in range(7):
            window_ref[k, rows, :] = total
            if k < 6:
                total = total + pltpu.roll(total, LANES - (1 << k) if later else 1 << k, 1)


def expand_matrix():
    return jnp.where(iota((DS * 8, DS), 0) // 8 == iota((DS * 8, DS), 1), 1.0, 0.0)


class Tiles:
    def __init__(self, channels, rows_n):
        self.rows_n, self.span = rows_n, CT * 8
        self.tiles, self.groups = channels // self.span, DS // NG
        self.per_row = self.tiles * self.groups
        self.count = rows_n * self.per_row

    def split(self, index):
        r, j = (0, index) if self.rows_n == 1 else (index // self.per_row, index % self.per_row)
        return r, j, j // self.groups, j % self.groups

    def rows(self, i):
        return pl.ds(pl.multiple_of(i * self.span, self.span), self.span)

    def cols(self, r, s):
        if self.rows_n == 1:
            return slab(s)
        return pl.ds(pl.multiple_of(r * SEQ_LEN + s * LANES, LANES), LANES)

    def loop(self, segment, body):
        lo, hi = (self.count * k // SEGMENTS for k in (segment, segment + 1))
        lax.fori_loop(lo, hi, body, 0)


def front_kernel(
    chan_size,
    tok_ref, cot_ref, gain_ref, inw_ref, xw_ref, outw_ref, ch_ref, dtw_ref, resets_ref,
    x_out, act_out, step_out, dy_out, gated_out, dgate_out, pj_out, ng_out, cg_out, h0_out, dec_out, mask_out, ct_out,
    ng, cg, xs, gs, slope, acts, dgs, wxg, part, from_pair, pair, from_chips, pj,
    mask, table, rowf, padded, step_ref, du_ref, y_ref, sums, wf, b8, c8, decb, h0, a_scr, gated, dgate,
    ag_send, ag_recv, ag_rsend, ag_rrecv, ag_fsend, ag_frecv, rd_send, rd_recv, out_sem,
):
    here = Here(chan_size)
    chips = here.chips
    own_rows, width = tok_ref.shape
    lanes = own_rows // SLABS
    rows_n, _, per_row = ng.shape[:3]
    channels, tokens = xs.shape
    t = Tiles(channels, rows_n)
    copies = []

    def save(src, dst):
        c = pltpu.make_async_copy(src, dst, out_sem.at[len(copies)])
        c.start()
        copies.append(c)

    barrier = pltpu.get_barrier_semaphore()
    for k in range(1, chips):
        pl.semaphore_signal(barrier, inc=1, device_id=(here.seq, here.same_core(k)), device_id_type=MESH)
    pl.semaphore_signal(barrier, inc=1, device_id=(here.seq, here.partner), device_id_type=MESH)

    order = reorder(own_rows).astype(bf16)
    values = tok_ref[...].astype(f32)
    normed = values * lax.rsqrt(jnp.mean(values * values, axis=-1, keepdims=True) + norm_epsilon) * gain_ref[...].reshape(1, width)
    shape = (SLABS, lanes, width)
    ng[here.chan // per_row, :, here.chan % per_row] = (
        dot_nn(order, normed.astype(bf16)).astype(bf16).reshape(shape)
    )
    pl.semaphore_wait(barrier, chips)
    first = Gather(
        here, ng, chips == 4, ag_send.at[0], ag_recv.at[0], ag_rsend.at[0], ag_rrecv.at[0], ag_fsend, ag_frecv
    )
    second = Gather(here, cg, False, ag_send.at[1], ag_recv.at[1], ag_rsend.at[1], ag_rrecv.at[1], None, None)
    first.start()

    cg[here.chan // per_row, :, here.chan % per_row] = dot_nn(order, cot_ref[...]).astype(bf16).reshape(shape)
    wxg[0:channels, :] = inw_ref[0].astype(bf16)
    wxg[channels:, :] = inw_ref[1].astype(bf16)
    row_masks(resets_ref, mask)
    rowf[...] = jnp.zeros_like(rowf)
    rowf[0 : KC + 3, :] = ch_ref[0 : KC + 3, :]
    rowf[DECAY_COL : DECAY_COL + DS, :] = -jnp.exp(ch_ref[KC + 3 :, :]) * LOG2E
    rowf[DT_COL : DT_COL + DR, :] = dtw_ref[...]
    table[...] = rowf[...].T
    for n in range(DS):
        decb[n] = jnp.broadcast_to(table[:, DECAY_COL + n : DECAY_COL + n + 1], (channels, LANES))
    padded[...] = jnp.zeros_like(padded)
    save(mask, mask_out)
    save(table, ct_out)
    save(decb, dec_out)

    step = SLABS // PIECES
    span = step * per_row * lanes

    def project(q):
        first.arrive(q)
        for r in range(rows_n):
            block = ng[r, q * step : (q + 1) * step].reshape(span, width)
            cols = slice((r * PIECES + q) * span, (r * PIECES + q + 1) * span)
            both = dot_nt(wxg[...], block)
            xs[:, cols] = both[0:channels]
            gs[:, cols] = both[channels:]

    if first.hop:
        for i in range(PIECES + 1):
            first.pass_on(i)
        for q in range(PIECES):
            project(q)
    else:
        first.pass_on(0)
        for q in range(PIECES):
            if q + 1 < PIECES:
                first.pass_on(q + 1)
            project(q)
    save(xs, x_out)
    save(ng, ng_out)

    high = tall(channels)

    def conv_tile(index, carry):
        i = index // rows_n
        r = index % rows_n
        rows = pl.ds(pl.multiple_of(i * high, high), high)
        taps = [jnp.broadcast_to(table[rows, k : k + 1], (high, LANES)) for k in range(KC + 1)]
        earlier = {s: pltpu.roll(xs[rows, t.cols(r, s)], 1, 1) for s in range(SLABS - KC + 1, SLABS)}
        for s in range(SLABS):
            conv = taps[KC]
            for j in range(KC):
                value = xs[rows, t.cols(r, s - j)] if s >= j else earlier[SLABS + s - j]
                if j > 0:
                    value = value * mask[j : j + 1, t.cols(r, s)]
                conv = conv + taps[KC - 1 - j] * value
            acts[rows, t.cols(r, s)] = (conv * jax.nn.sigmoid(conv)).astype(bf16)
        return carry

    lax.fori_loop(0, channels // high * rows_n, conv_tile, 0)
    part[...] = dot_nn(xw_ref[...].astype(bf16), acts[...])
    reduce = Reduce(here, part, from_pair, pair, from_chips, pj, rd_send, rd_recv)
    reduce.step1()
    save(acts, act_out)
    reduce.step2()

    def gate_tile(index, carry):
        i = index // rows_n
        r = index % rows_n
        rows = pl.ds(pl.multiple_of(i * 16, 16), 16)
        for s in range(SLABS):
            gate = gs[rows, t.cols(r, s)]
            sig = jax.nn.sigmoid(gate)
            gs[rows, t.cols(r, s)] = gate * sig
            slope[rows, t.cols(r, s)] = sig * (1.0 + gate * (1.0 - sig))
        return carry

    lax.fori_loop(0, channels // 16 * rows_n, gate_tile, 0)
    reduce.step3()
    reduce.step4()
    reduce.step5()
    second.start()
    save(pj, pj_out)

    padded[DT_COL : DT_COL + DR, :] = pj[0:DR, :]
    step_ref[...] = dot_nn(table[...].astype(bf16), padded[...])

    def prelude(index, carry):
        i = index // rows_n
        r = index % rows_n
        rows = pl.ds(pl.multiple_of(i * 16, 16), 16)
        bias = jnp.broadcast_to(table[rows, KC + 1 : KC + 2], (16, LANES))
        total = jnp.zeros((16, LANES), f32)
        for s in range(SLABS):
            cols = t.cols(r, s)
            value = softplus(step_ref[rows, cols] + bias)
            step_ref[rows, cols] = value
            du_ref[rows, cols] = value * acts[rows, cols].astype(f32)
            y_ref[rows, cols] = jnp.zeros((16, LANES), f32)
            total = total + jnp.where(mask[0:1, cols] > 0.0, HUGE, value)
        sums[pl.ds(pl.multiple_of(r * channels + i * 16, 16), 16), :] = total
        return carry

    lax.fori_loop(0, channels // 16 * rows_n, prelude, 0)
    windows(sums, wf, False)
    save(step_ref, step_out)
    expand = expand_matrix()

    def group(index, carry):
        r, j, i, g = t.split(index)
        rows = t.rows(i)
        nrows = pl.ds(pl.multiple_of(g * (NG * 8), NG * 8), NG * 8)

        @pl.when(j == 0)
        def _():
            if rows_n == 1:
                block = pj[DR:, :]
            else:
                block = pj[DR:, pl.ds(pl.multiple_of(r * SEQ_LEN, SEQ_LEN), SEQ_LEN)]
            b8[...] = dot_nn(expand, block[0:DS].astype(f32), highest)
            c8[...] = dot_nn(expand, block[DS:].astype(f32), highest)

        def tile(ref, s):
            return ref[rows, t.cols(r, s)].reshape(1, CT, 8, LANES)

        def state(ref, s):
            return ref[nrows, slab(s)].reshape(NG, 1, 8, LANES)

        dec = decb[pl.ds(g * NG, NG), rows, :].reshape(NG, CT, 8, LANES)
        h = jnp.zeros((NG, CT, 8, LANES), f32)
        for s in range(SLABS):
            stepk = jnp.where(mask[0:1, t.cols(r, s)] > 0.0, HUGE, step_ref[rows, t.cols(r, s)])
            a = jnp.exp2(dec * stepk.reshape(1, CT, 8, LANES))
            a_scr[s] = a
            h = a * h + state(b8, s) * tile(du_ref, s)
        at = pl.ds(pl.multiple_of(r * channels + i * t.span, t.span), t.span)
        for k in range(7):
            gain = jnp.exp2(dec * wf[k, at, :].reshape(1, CT, 8, LANES))
            h = h + gain * pltpu.roll(h, 1 << k, 3)
        h = pltpu.roll(h, 1, 3)
        h0[pl.ds(r * DS + g * NG, NG), rows, :] = h.reshape(NG, t.span, LANES)
        for s in range(SLABS):
            h = a_scr[s] * h + state(b8, s) * tile(du_ref, s)
            y_ref[rows, t.cols(r, s)] += jnp.sum(state(c8, s) * h, axis=0).reshape(t.span, LANES)
        return carry

    for segment in range(SEGMENTS):
        t.loop(segment, group)
        if segment + 2 >= SEGMENTS:
            for q in range(PIECES // 2):
                second.pass_on(q + (segment + 2 - SEGMENTS) * PIECES // 2)
    save(h0, h0_out)

    def skip_tile(index, carry):
        i = index // rows_n
        r = index % rows_n
        rows = pl.ds(pl.multiple_of(i * 16, 16), 16)
        skip = jnp.broadcast_to(table[rows, KC + 2 : KC + 3], (16, LANES))
        for s in range(SLABS):
            cols = t.cols(r, s)
            y = y_ref[rows, cols] + skip * acts[rows, cols].astype(f32)
            gated[rows, cols] = (y * gs[rows, cols]).astype(bf16)
            y_ref[rows, cols] = y * slope[rows, cols]
        return carry

    lax.fori_loop(0, channels // 16 * rows_n, skip_tile, 0)
    save(gated, gated_out)
    low = outw_ref[...].astype(bf16)
    for q in range(PIECES):
        second.arrive(q)
        for r in range(rows_n):
            block = cg[r, q * step : (q + 1) * step].reshape(span, width)
            cols = slice((r * PIECES + q) * span, (r * PIECES + q + 1) * span)
            dgs[:, cols] = dot_nt(low, block)
    save(cg, cg_out)

    def grad_tile(index, carry):
        i = index // rows_n
        r = index % rows_n
        rows = pl.ds(pl.multiple_of(i * 16, 16), 16)
        for s in range(SLABS):
            cols = t.cols(r, s)
            dg = dgs[rows, cols]
            dgate[rows, cols] = (dg * y_ref[rows, cols]).astype(bf16)
            dgs[rows, cols] = dg * gs[rows, cols]
        return carry

    lax.fori_loop(0, channels // 16 * rows_n, grad_tile, 0)
    save(dgs, dy_out)
    save(dgate, dgate_out)
    first.close()
    second.close()
    reduce.close()
    for c in copies:
        c.wait()


def front_call(chan_size, tokens, cotangent, gain, in_weight, x_weight, out_weight, chan_params, dt_weight, resets):
    own_rows, width = tokens.shape
    count = resets.shape[0] * LANES
    channels = out_weight.shape[0]
    chips = chan_size // 2
    rows = count // SEQ_LEN
    wide = (channels, count)
    whole = (rows, SLABS, SEQ_LEN // own_rows, own_rows // SLABS, width)
    project = DR + 2 * DS
    any_spec = pl.BlockSpec(memory_space=pl.ANY)
    vmem = pl.BlockSpec(memory_space=pltpu.VMEM)
    dma = pltpu.SemaphoreType.DMA
    gather_sems = (2, chips, PIECES)
    states = (rows * DS, channels, LANES)
    decays = (DS, channels, LANES)
    outs = [
        (wide, f32), (wide, bf16), (wide, f32), (wide, f32), (wide, bf16), (wide, bf16), ((project, count), bf16),
        (whole, bf16), (whole, bf16), (states, f32), (decays, f32), ((4, count), f32), ((channels, LANES), f32),
    ]
    scratch = [
        (whole, bf16), (whole, bf16), (wide, f32), (wide, f32), (wide, f32), (wide, bf16), (wide, f32),
        ((2 * channels, width), bf16),
        ((project, count), f32), ((project, count // 2), f32), ((project, count // 2), bf16),
        ((chips - 1, project, count // 2 // chips), bf16), ((project, count), bf16),
        ((4, count), f32), ((channels, LANES), f32), ((LANES, channels), f32), ((LANES, count), bf16),
        (wide, f32), (wide, f32), (wide, f32), ((rows * channels, LANES), f32), ((7, rows * channels, LANES), f32),
        ((DS * 8, SEQ_LEN), f32), ((DS * 8, SEQ_LEN), f32), (decays, f32), (states, f32),
        ((SLABS, NG, CT, 8, LANES), f32), (wide, bf16), (wide, bf16),
    ]
    return pl.pallas_call(
        functools.partial(front_kernel, chan_size),
        in_specs=[vmem] * 9,
        out_specs=[any_spec] * len(outs),
        out_shape=[jax.ShapeDtypeStruct(*o) for o in outs],
        scratch_shapes=[pltpu.VMEM(*s) for s in scratch]
        + [dma(gather_sems)] * 4
        + [dma((PIECES,))] * 2
        + [dma((2 * chips,))] * 2
        + [dma((len(outs),))],
        compiler_params=pltpu.CompilerParams(collective_id=0, has_side_effects=True, vmem_limit_bytes=60 * MIB),
        name="front",
    )(tokens, cotangent, gain, in_weight, x_weight, out_weight, chan_params, dt_weight, resets)


def back_kernel(
    chan_size, seq_size,
    table, mask, xw_ref,
    gated_in, outw_in, cot_in, step_in, act_in, pj_in, dec_in, dy_in, h0_in, dgate_in, normed_in, inw_in, x_in,
    msum_ref, dsum_ref, za_out, zb_out, zc_out, gsum_ref,
    gated, outw, step_ref, act, pjf, decb, dy, h0, dgate, inw, rows_buf, low, dx, dc, taps_red, gin1,
    du, s1, ds2, totals, wb, b8, c8, db8, dc8, red, a_scr, ah_scr, pback,
    part, pair_buf, land, from_pair, pair, from_chips, pj,
    za, zb, zc, zha, zhb, zhc, gp, gz, gc,
    in_sem, out_sem, m_s1, m_r1, m_s2, m_r2, d_s1, d_r1, d_s2, d_r2,
    rd_send, rd_recv, z_send, z_recv, gz_send, gz_recv, gc_send, gc_recv,
):
    here = Here(chan_size)
    channels, tokens = gated.shape
    rows_n = pair_buf.shape[0]
    width = outw.shape[1]
    project = pj.shape[0]
    t = Tiles(channels, rows_n)
    tile_count = channels // 16 * rows_n

    loads = {}
    for index, (name, src, dst) in enumerate(
        (
            ("gated", gated_in, gated), ("outw", outw_in, outw), ("cot", cot_in.at[0], rows_buf.at[0]),
            ("step", step_in, step_ref), ("act", act_in, act), ("pj", pj_in, pjf), ("dec", dec_in, decb),
            ("dy", dy_in, dy), ("h0", h0_in, h0), ("dgate", dgate_in, dgate),
            ("normed", normed_in.at[0], rows_buf.at[1]), ("inw", inw_in, inw), ("x", x_in, du),
        )
    ):
        loads[name] = pltpu.make_async_copy(src, dst, in_sem.at[index])
    early = ("gated", "outw", "cot")
    for name in early:
        loads[name].start()

    barrier = pltpu.get_barrier_semaphore()
    for k in range(1, chan_size):
        pl.semaphore_signal(barrier, inc=1, device_id=(here.seq, flip(here.chan, k)), device_id_type=MESH)
    for k in range(1, seq_size):
        pl.semaphore_signal(barrier, inc=1, device_id=(flip(here.seq, k), here.chan), device_id_type=MESH)

    reduce = Reduce(here, pback, from_pair, pair, from_chips, pj, rd_send, rd_recv)
    mixed = Scatter(here, part, pair_buf, land, m_s1, m_r1, m_s2, m_r2)
    normed_grad = Scatter(here, part, pair_buf, land, d_s1, d_r1, d_s2, d_r2)
    sum_a = SeqSum(here, seq_size, za, zha, z_send.at[0], z_recv.at[0])
    sum_b = SeqSum(here, seq_size, zb, zhb, z_send.at[1], z_recv.at[1])
    sum_c = SeqSum(here, seq_size, zc, zhc, z_send.at[2], z_recv.at[2])
    if za.shape[0] > channels:
        for buf in (za, zb, zc):
            buf[channels:, :] = jnp.zeros((buf.shape[0] - channels, buf.shape[1]), bf16)

    def row_block(slot):
        return rows_buf[slot].reshape(SEQ_LEN, width)

    def row_cols(r):
        return slice(r * SEQ_LEN, (r + 1) * SEQ_LEN)

    def fetch(src, r, slot, name):
        index = list(loads).index(name)
        c = pltpu.make_async_copy(src.at[r], rows_buf.at[slot], in_sem.at[index])
        c.start()
        return c

    loads["gated"].wait()
    loads["outw"].wait()
    for name in loads:
        if name not in early and name != "x":
            loads[name].start()
    low[0] = outw[...].astype(bf16)
    pl.semaphore_wait(barrier, chan_size - 1 + seq_size - 1)
    mixed.produce(lambda cols: dot_tn(gated[:, cols], low[0]), False, None)
    loads["cot"].wait()
    out_grad = dot_nn(gated[:, row_cols(0)], row_block(0))
    for r in range(1, rows_n):
        fetch(cot_in, r, 0, "cot").wait()
        out_grad = out_grad + dot_nn(gated[:, row_cols(r)], row_block(0))
    za[0:channels, :] = out_grad.astype(bf16)
    sum_a.start()
    loads["dgate"].wait()
    loads["normed"].wait()
    in_grad = dot_nn(dgate[:, row_cols(0)], row_block(1))
    for r in range(1, rows_n):
        fetch(normed_in, r, 1, "normed").wait()
        in_grad = in_grad + dot_nn(dgate[:, row_cols(r)], row_block(1))
    gin1[...] = in_grad
    zb[0:channels, :] = in_grad.astype(bf16)
    sum_b.start()
    loads["inw"].wait()
    low[0] = inw[0].astype(bf16)
    low[1] = inw[1].astype(bf16)

    for name in ("step", "act", "pj", "dec", "dy", "h0"):
        loads[name].wait()
    red[...] = jnp.zeros_like(red)

    def prelude(index, carry):
        i = index // rows_n
        r = index % rows_n
        rows = pl.ds(pl.multiple_of(i * 16, 16), 16)
        total = jnp.zeros((16, LANES), f32)
        for s in range(SLABS):
            cols = t.cols(r, s)
            value = step_ref[rows, cols]
            du[rows, cols] = value * act[rows, cols].astype(f32)
            s1[rows, cols] = jnp.zeros((16, LANES), f32)
            ds2[rows, cols] = jnp.zeros((16, LANES), f32)
            total = total + jnp.where(mask[0:1, cols] > 0.0, HUGE, value)
        totals[pl.ds(pl.multiple_of(r * channels + i * 16, 16), 16), :] = total
        return carry

    lax.fori_loop(0, tile_count, prelude, 0)
    windows(totals, wb, True)
    for q in range(PIECES):
        mixed.send(q)
    expand = expand_matrix()

    def group(index, carry):
        r, j, i, g = t.split(index)
        rows = t.rows(i)
        nrows = pl.ds(pl.multiple_of(g * (NG * 8), NG * 8), NG * 8)
        whole_row = slice(0, SEQ_LEN) if rows_n == 1 else pl.ds(pl.multiple_of(r * SEQ_LEN, SEQ_LEN), SEQ_LEN)

        @pl.when(j == 0)
        def _():
            block = pjf[DR:, whole_row]
            b8[...] = dot_nn(expand, block[0:DS].astype(f32), highest)
            c8[...] = dot_nn(expand, block[DS:].astype(f32), highest)
            db8[...] = jnp.zeros_like(db8)
            dc8[...] = jnp.zeros_like(dc8)

        def tile(ref, s):
            return ref[rows, t.cols(r, s)].reshape(1, CT, 8, LANES)

        def state(ref, s):
            return ref[nrows, slab(s)].reshape(NG, 1, 8, LANES)

        dec = decb[pl.ds(g * NG, NG), rows, :].reshape(NG, CT, 8, LANES)
        h = h0[pl.ds(r * DS + g * NG, NG), rows, :].reshape(NG, CT, 8, LANES)
        for s in range(SLABS):
            stepk = jnp.where(mask[0:1, t.cols(r, s)] > 0.0, HUGE, step_ref[rows, t.cols(r, s)])
            a = jnp.exp2(dec * stepk.reshape(1, CT, 8, LANES))
            a_scr[s] = a
            ah = a * h
            ah_scr[s] = ah
            h = ah + state(b8, s) * tile(du, s)
            dc8[nrows, slab(s)] += jnp.sum(tile(dy, s) * h, axis=1).reshape(NG * 8, LANES)
        p = jnp.zeros((NG, CT, 8, LANES), f32)
        for s in reversed(range(SLABS)):
            p = a_scr[s] * (tile(dy, s) * state(c8, s) + p)
        at = pl.ds(pl.multiple_of(r * channels + i * t.span, t.span), t.span)
        for k in range(7):
            gain = jnp.exp2(dec * wb[k, at, :].reshape(1, CT, 8, LANES))
            p = p + gain * pltpu.roll(p, LANES - (1 << k), 3)
        p = pltpu.roll(p, LANES - 1, 3)
        rate = jnp.zeros((NG, CT, 8, LANES), f32)
        for s in reversed(range(SLABS)):
            lam = tile(dy, s) * state(c8, s) + p
            p = a_scr[s] * lam
            s1[rows, t.cols(r, s)] += jnp.sum(lam * state(b8, s), axis=0).reshape(t.span, LANES)
            db8[nrows, slab(s)] += jnp.sum(lam * tile(du, s), axis=1).reshape(NG * 8, LANES)
            q = lam * ah_scr[s]
            ds2[rows, t.cols(r, s)] += jnp.sum(dec * q, axis=0).reshape(t.span, LANES)
            rate = rate + q * tile(step_ref, s)
        for n in range(NG):
            cols = pl.ds(pl.multiple_of((g * NG + n) * LANES, LANES), LANES)
            red[rows, cols] += rate[n].reshape(t.span, LANES)

        @pl.when(j == t.per_row - 1)
        def _():
            pback[DR : DR + DS, whole_row] = dot_tn(expand, db8[...], highest).astype(bf16)
            pback[DR + DS :, whole_row] = dot_tn(expand, dc8[...], highest).astype(bf16)

        return carry

    levels = seq_size.bit_length() - 1
    for segment in range(SEGMENTS):
        t.loop(segment, group)
        if segment == 1:
            sum_a.step(0)
            sum_b.step(0)
        if segment + 1 == SEGMENTS:
            for i in range(1, levels):
                sum_a.step(i)
                sum_b.step(i)
            mixed.finish(msum_ref)
    loads["x"].start()
    x_buf = du

    def adjoint_tile(index, carry):
        i = index // rows_n
        r = index % rows_n
        rows = pl.ds(pl.multiple_of(i * 16, 16), 16)
        skip = jnp.broadcast_to(table[rows, KC + 2 : KC + 3], (16, LANES))
        skip_sum = jnp.zeros((16, LANES), f32)
        bias_sum = jnp.zeros((16, LANES), f32)
        for s in range(SLABS):
            cols = t.cols(r, s)
            value = step_ref[rows, cols]
            lam_b = s1[rows, cols]
            d_y = dy[rows, cols]
            act_s = act[rows, cols].astype(f32)
            s1[rows, cols] = d_y * skip + lam_b * value
            small = value * (1.0 - value * (0.5 - value * (1.0 / 6.0)))
            slope = jnp.where(value < 0.01, small, 1.0 - jnp.exp(-value))
            back = ((lam_b * act_s + LN2 * ds2[rows, cols]) * slope).astype(bf16)
            dx[rows, cols] = back
            skip_sum = skip_sum + d_y * act_s
            bias_sum = bias_sum + back.astype(f32)
        red[rows, DS * LANES : (DS + 1) * LANES] += skip_sum
        red[rows, (DS + 1) * LANES :] += bias_sum
        return carry

    lax.fori_loop(0, tile_count, adjoint_tile, 0)
    low_table = table[...].astype(bf16)
    for r in range(rows_n):
        pback[0:DR, row_cols(r)] = dot_tn(low_table, dx[:, row_cols(r)])[DT_COL : DT_COL + DR].astype(bf16)
    reduce.step1()
    pick = jnp.where(iota(((DS + 2) * LANES, LANES), 0) // LANES == iota(((DS + 2) * LANES, LANES), 1), 1.0, 0.0)
    dt_grad = jnp.concatenate(
        [
            jnp.zeros((channels, DT_COL), f32),
            dot_nt(dx[...], pjf[0:DR, :]),
            jnp.zeros((channels, LANES - DT_COL - DR), f32),
        ],
        axis=1,
    )
    zc[0:channels, width + LANES :] = (dot_nn(red[...], pick, highest) + dt_grad).astype(bf16)
    reduce.step2()
    reduce.step3()
    reduce.step4()
    saves = sum_a.finish(za_out, out_sem.at[0])
    saves += sum_b.finish(zb_out, out_sem.at[1])
    loads["x"].wait()
    x_low = xw_ref[...].astype(bf16)
    reduce.step5()
    for r in range(rows_n):
        s1[:, row_cols(r)] += dot_tn(x_low, pj[:, row_cols(r)])

    high = tall(channels)

    def conv_tile(index, carry):
        i = index // rows_n
        r = index % rows_n
        rows = pl.ds(pl.multiple_of(i * high, high), high)
        taps = [jnp.broadcast_to(table[rows, k : k + 1], (high, LANES)) for k in range(KC + 1)]
        earlier = {s: pltpu.roll(x_buf[rows, t.cols(r, s)], 1, 1) for s in range(SLABS - KC + 1, SLABS)}
        sums = [jnp.zeros((high, LANES), f32) for _ in range(KC + 1)]
        for s in range(SLABS):
            cols = t.cols(r, s)
            inputs = []
            conv = taps[KC]
            for j in range(KC):
                value = x_buf[rows, t.cols(r, s - j)] if s >= j else earlier[SLABS + s - j]
                if j > 0:
                    value = value * mask[j : j + 1, cols]
                inputs.append(value)
                conv = conv + taps[KC - 1 - j] * value
            sig = jax.nn.sigmoid(conv)
            d_conv = s1[rows, cols] * (sig * (1.0 + conv * (1.0 - sig)))
            dc[:, slab(s)] = d_conv
            for j in range(KC):
                sums[KC - 1 - j] = sums[KC - 1 - j] + d_conv * inputs[j]
            sums[KC] = sums[KC] + d_conv
        wrapped = {}
        for s in range(KC - 1):
            for j in range(s + 1, KC):
                wrapped[s, j] = pltpu.roll(dc[:, slab(s)] * mask[j : j + 1, t.cols(r, s)], LANES - 1, 1)
        for s in range(SLABS):
            d_x = taps[KC - 1] * dc[:, slab(s)]
            for j in range(1, KC):
                if s + j < SLABS:
                    value = dc[:, slab(s + j)] * mask[j : j + 1, t.cols(r, s + j)]
                else:
                    value = wrapped[s + j - SLABS, j]
                d_x = d_x + taps[KC - 1 - j] * value
            dx[rows, t.cols(r, s)] = d_x.astype(bf16)
        for k in range(KC + 1):
            @pl.when(r == 0)
            def _():
                taps_red[rows, slab(k)] = sums[k]

            @pl.when(r > 0)
            def _():
                taps_red[rows, slab(k)] += sums[k]
        return carry

    lax.fori_loop(0, channels // high * rows_n, conv_tile, 0)

    def weight_sums():
        if rows_n > 1:
            fetch(normed_in, 0, 1, "normed").wait()
        in_grad = dot_nn(dx[:, row_cols(0)], row_block(1))
        for r in range(1, rows_n):
            fetch(normed_in, r, 1, "normed").wait()
            in_grad = in_grad + dot_nn(dx[:, row_cols(r)], row_block(1))
        zc[0:channels, 0:width] = in_grad.astype(bf16)
        x_grad = dot_nt(act[...], pj[...])
        x_grad = jnp.concatenate([x_grad, jnp.zeros((channels, LANES - project), f32)], axis=1)
        k_i = iota(((KC + 1) * LANES, LANES), 0)
        pick = jnp.where(k_i // LANES + project == iota(((KC + 1) * LANES, LANES), 1), 1.0, 0.0)
        zc[0:channels, width : width + LANES] = (x_grad + dot_nn(taps_red[...], pick, highest)).astype(bf16)
        sum_c.start()

        both = low[0].astype(f32) * in_grad + low[1].astype(f32) * gin1[...]
        gp[...] = jnp.sum(both.reshape(channels // 8, 8, width), axis=0)

    normed_grad.produce(
        lambda cols: dot_tn(dx[:, cols], low[0]) + dot_tn(dgate[:, cols], low[1]), True, weight_sums
    )
    normed_grad.send(PIECES - 1)

    def gain_seq(k):
        return pltpu.make_async_remote_copy(
            src_ref=gp, dst_ref=gz.at[k - 1], send_sem=gz_send.at[k - 1], recv_sem=gz_recv.at[k - 1],
            device_id=(flip(here.seq, k), here.chan), device_id_type=MESH,
        )

    def gain_chan(k):
        return here.copy(gz.at[seq_size - 1], gc.at[k - 1], gc_send.at[k - 1], gc_recv.at[k - 1], flip(here.chan, k))

    for k in range(1, seq_size):
        gain_seq(k).start()
    for k in range(1, seq_size):
        gain_seq(k).wait()
    total = gp[...]
    for k in range(1, seq_size):
        total = total + gz[k - 1]
    gz[seq_size - 1] = total
    for k in range(1, chan_size):
        gain_chan(k).start()
    for i in range(levels):
        sum_c.step(i)
    for k in range(1, chan_size):
        gain_chan(k).wait()
        total = total + gc[k - 1]
    gsum_ref[...] = total
    normed_grad.finish(dsum_ref)
    saves += sum_c.finish(zc_out, out_sem.at[2])
    reduce.close()
    for c in saves:
        c.wait()


def back_call(
    chan_size, seq_size, own_rows, table, masks, x_weight, gated, out_weight, cot_all, step, act, pj, decays, dy, h0,
    dgate, normed_all, in_weight, x_cols,
):
    channels, width = out_weight.shape
    count = masks.shape[1]
    chips = chan_size // 2
    rows = count // SEQ_LEN
    per_row = SEQ_LEN // own_rows // 2
    lanes = own_rows // SLABS
    project = DR + 2 * DS
    wide = (channels, count)
    padded = (channels + 31) // 32 * 32
    levels = seq_size.bit_length() - 1
    any_spec = pl.BlockSpec(memory_space=pl.ANY)
    vmem = pl.BlockSpec(memory_space=pltpu.VMEM)
    dma = pltpu.SemaphoreType.DMA
    sums = ((padded, width), (padded, width), (padded, width + 2 * LANES))
    states = (DS * 8, SEQ_LEN)
    loops = (SLABS, NG, CT, 8, LANES)
    outs = [
        ((own_rows, width), f32), ((own_rows, width), f32), (sums[0], bf16), (sums[1], bf16), (sums[2], bf16),
        ((8, width), f32),
    ]
    scratch = [
        (wide, bf16), ((channels, width), f32), (wide, f32), (wide, bf16), ((project, count), bf16),
        ((DS, channels, LANES), f32), (wide, f32), ((rows * DS, channels, LANES), f32), (wide, bf16),
        ((2, channels, width), f32), ((2, SLABS, 2 * per_row, lanes, width), bf16),
        ((2, channels, width), bf16), (wide, bf16), ((tall(channels), SEQ_LEN), f32), ((channels, (KC + 1) * LANES), f32),
        ((channels, width), f32),
        (wide, f32), (wide, f32), (wide, f32), ((rows * channels, LANES), f32), ((7, rows * channels, LANES), f32),
        (states, f32), (states, f32), (states, f32), (states, f32), ((channels, (DS + 2) * LANES), f32),
        (loops, f32), (loops, f32), ((project, count), bf16),
        ((min(rows, 2), SLABS, per_row, 2, lanes, width), bf16), ((rows, SLABS, per_row, lanes, width), bf16),
        ((chips - 1, SLABS, lanes, width), bf16), ((project, count // 2), bf16), ((project, count // 2), bf16),
        ((chips - 1, project, count // 2 // chips), bf16), ((project, count), bf16),
        (sums[0], bf16), (sums[1], bf16), (sums[2], bf16),
    ]
    scratch += [((levels + 1, padded // 2, s[1]), bf16) for s in sums]
    scratch += [((8, width), f32), ((seq_size, 8, width), f32), ((chan_size - 1, 8, width), f32)]
    return pl.pallas_call(
        functools.partial(back_kernel, chan_size, seq_size),
        in_specs=[vmem] * 3 + [any_spec] * 13,
        out_specs=[vmem, vmem, any_spec, any_spec, any_spec, vmem],
        out_shape=[jax.ShapeDtypeStruct(*o) for o in outs],
        scratch_shapes=[pltpu.VMEM(*s) for s in scratch]
        + [dma((13,)), dma((3, 2))]
        + ([dma((rows * PIECES,))] * 2 + [dma((chips * PIECES,))] * 2) * 2
        + [dma((2 * chips,))] * 2
        + [dma((3, levels + 1))] * 2
        + [dma((seq_size,))] * 2
        + [dma((chan_size,))] * 2,
        compiler_params=pltpu.CompilerParams(collective_id=1, has_side_effects=True, vmem_limit_bytes=60 * MIB),
        name="back",
    )(
        table, masks, x_weight, gated, out_weight, cot_all, step, act, pj, decays, dy, h0, dgate, normed_all, in_weight, x_cols
    )


def update(grad, master, first, second, rate, outs):
    new = adamw_core(master, first, second, grad, rate)
    for ref, value in zip(outs, new):
        ref[...] = value
    outs[3][...] = new[0].astype(bf16)


def finish_kernel(
    tok_ref, cot_ref, msum_ref, dsum_ref, za_ref, zb_ref, zc_ref, zb_all, zc_all, gsum_ref,
    gain_m, gain_f, gain_s, in_m, in_f, in_s, x_m, x_f, x_s, dt_m, dt_f, dt_s, out_m, out_f, out_s, ch_m, ch_f, ch_s,
    mixed_ref, tgrad_ref, *rest,
):
    gain_o, in_o, x_o, dt_o, out_o, ch_o = (rest[i * 4 : i * 4 + 4] for i in range(6))
    ch_grad = rest[24]
    i = pl.program_id(0)
    width = tok_ref.shape[1]
    own_rows = msum_ref.shape[0]
    block = tok_ref.shape[0]
    lanes = own_rows // SLABS
    channels = x_m.shape[1]

    r = lax.broadcasted_iota(jnp.int32, (block, own_rows), 0) + i * block
    q = lax.broadcasted_iota(jnp.int32, (block, own_rows), 1)
    order = jnp.where(r == (q % lanes) * SLABS + q // lanes, 1.0, 0.0).astype(bf16)

    def in_order(ref):
        values = ref[...]
        high = values.astype(bf16)
        return dot_nn(order, high) + dot_nn(order, (values - high.astype(f32)).astype(bf16))

    values = tok_ref[...].astype(f32)
    mixed_ref[...] = (values + in_order(msum_ref)).astype(bf16)
    d_normed = in_order(dsum_ref)
    rstd = lax.rsqrt(jnp.mean(values * values, axis=-1, keepdims=True) + norm_epsilon)
    gain_row = gain_m[...].reshape(1, width)
    scaled = gain_row * d_normed
    mean = jnp.mean(scaled * values, axis=-1, keepdims=True)
    tgrad_ref[...] = cot_ref[...].astype(f32) + rstd * scaled - values * (rstd * rstd * rstd * mean)

    out_grad = za_ref[...].astype(f32)
    update(out_grad, out_m[...], out_f[...], out_s[...], rate_output, out_o)
    for k, ref in ((0, zc_ref), (1, zb_ref)):
        grad = ref[:, 0:width].astype(f32)
        new = adamw_core(in_m[k], in_f[k], in_s[k], grad, rate_inner)
        for o, value in zip(in_o, new):
            o[k] = value
        in_o[3][k] = new[0].astype(bf16)

    @pl.when(i == 0)
    def _():
        grad_b = zb_all[...].astype(f32).T
        grad_c = zc_all[...].astype(f32).T
        update(grad_b[64 : 64 + DR, 0:channels], dt_m[...], dt_f[...], dt_s[...], rate_step, dt_o)
        project = x_m.shape[0]
        update(grad_c[0:project, 0:channels], x_m[...], x_f[...], x_s[...], rate_project, x_o)
        ch_grad[0 : KC + 1, :] = grad_c[project : project + KC + 1, 0:channels]
        ch_grad[KC + 1 : KC + 2, :] = grad_b[DS + 1 : DS + 2, 0:channels]
        ch_grad[KC + 2 : KC + 3, :] = grad_b[DS : DS + 1, 0:channels]
        ch_grad[KC + 3 :, :] = grad_b[0:DS, 0:channels] * -jnp.exp(ch_m[KC + 3 :, :])
        update(ch_grad[...], ch_m[...], ch_f[...], ch_s[...], rate_channel, ch_o)
        gain_grad = jnp.sum(gsum_ref[...], axis=0, keepdims=True) / gain_row
        moments = (ref[...].reshape(1, width) for ref in (gain_f, gain_s))
        new = adamw_core(gain_row, *moments, gain_grad, rate_gain)
        for ref, value in zip(gain_o, (*new, new[0].astype(bf16))):
            ref[...] = value.reshape(width)


def finish_call(tokens, cotangent, msum, dsum, za, zb, zc, gsum, gains, inners, projects, steps, outputs, chans):
    own_rows, width = tokens.shape
    channels = outputs[0].shape[0]
    cb = 96 if channels % 96 == 0 else channels
    grid = channels // cb
    block = own_rows // grid
    row = pl.BlockSpec((block, width), lambda i: (i, 0))

    def full(shape):
        return pl.BlockSpec(shape, lambda i: (0,) * len(shape))

    inner = pl.BlockSpec((2, cb, width), lambda i: (0, i, 0))
    outer = pl.BlockSpec((cb, width), lambda i: (i, 0))
    tails = [pl.BlockSpec((zc.shape[0], LANES), lambda i, k=k: (0, width // LANES + k)) for k in (1, 0)]
    zed = pl.BlockSpec((cb, width), lambda i: (i, 0))
    groups = (gains, inners, projects, steps, outputs, chans)
    specs = (full(gains[0].shape), inner, full(projects[0].shape), full(steps[0].shape), outer, full(chans[0].shape))
    in_specs = [row, row, full(msum.shape), full(dsum.shape), zed, zed, zed, *tails, full(gsum.shape)]
    out_specs = [row, row]
    out_shape = [jax.ShapeDtypeStruct(tokens.shape, bf16), jax.ShapeDtypeStruct(tokens.shape, f32)]
    args = [tokens, cotangent, msum, dsum, za, zb, zc, zc, zc, gsum]
    for arrays, spec in zip(groups, specs):
        in_specs += [spec] * 3
        out_specs += [spec] * 4
        out_shape += [jax.ShapeDtypeStruct(arrays[0].shape, f32)] * 3 + [jax.ShapeDtypeStruct(arrays[0].shape, bf16)]
        args += list(arrays)
    return pl.pallas_call(
        finish_kernel,
        grid=(grid,),
        in_specs=in_specs,
        out_specs=out_specs,
        out_shape=out_shape,
        scratch_shapes=[pltpu.VMEM(chans[0].shape, f32)],
        compiler_params=pltpu.CompilerParams(dimension_semantics=("arbitrary",), vmem_limit_bytes=60 * MIB),
        name="finish",
    )(*args)


def per_device(
    tokens,
    resets,
    cotangent,
    norm_gain,
    in_weight,
    x_weight,
    dt_weight,
    out_weight,
    chan_params,
    gain_first,
    gain_second,
    in_first,
    in_second,
    x_first,
    x_second,
    dt_first,
    dt_second,
    out_first,
    out_second,
    chan_first,
    chan_second,
):
    own_count = tokens.shape[0]
    chan_size = lax.axis_size("chan")
    seq_size = lax.axis_size("seq")
    inners = [jnp.swapaxes(a, 1, 2) for a in (in_weight, in_first, in_second)]
    projects = [a.T for a in (x_weight, x_first, x_second)]
    x_cols, act, step, dy, gated, dgate, pj, normed_all, cot_all, h0, decays, masks, table = front_call(
        chan_size, tokens, cotangent, norm_gain, inners[0], projects[0], out_weight, chan_params, dt_weight,
        resets.reshape(-1, LANES),
    )
    msum, dsum, za, zb, zc, gsum = back_call(
        chan_size, seq_size, own_count, table, masks, projects[0], gated, out_weight, cot_all, step, act, pj, decays, dy, h0,
        dgate, normed_all, inners[0], x_cols,
    )
    result = finish_call(
        tokens, cotangent, msum, dsum, za, zb, zc, gsum,
        (norm_gain, gain_first, gain_second),
        inners,
        projects,
        (dt_weight, dt_first, dt_second),
        (out_weight, out_first, out_second),
        (chan_params, chan_first, chan_second),
    )
    result = list(result)
    result[6:10] = [jnp.swapaxes(a, 1, 2) for a in result[6:10]]
    result[10:14] = [a.T for a in result[10:14]]
    return tuple(result)


def solution(mesh):
    rows = P(("seq", "chan"), None)
    inner = P(None, None, "chan")
    by_row = P("chan", None)
    by_col = P(None, "chan")
    placed = (rows, P("seq"), rows, P(), inner, by_row, by_col, by_row, by_col, P(), P())
    placed += (inner, inner, by_row, by_row, by_col, by_col, by_row, by_row, by_col, by_col)
    return jax.shard_map(
        per_device,
        mesh=mesh,
        in_specs=placed,
        out_specs=(rows, rows)
        + (P(),) * 4
        + (inner,) * 4
        + (by_row,) * 4
        + (by_col,) * 4
        + (by_row,) * 4
        + (by_col,) * 4,
        check_vma=False,
    )
```

```python
import functools

import jax
import jax.numpy as jnp
from jax import lax
from jax.experimental import pallas as pl
from jax.experimental.pallas import tpu as pltpu
from jax.sharding import PartitionSpec as P

DS = 16
DR = 48
KC = 4
SEQ_LEN = 2048
STEP = 10
SLABS = 16
LANES = 128
NG = 4
PIECES = 2
MIB = 1024 * 1024
MESH = pl.DeviceIdType.MESH

highest = lax.Precision.HIGHEST
norm_epsilon = 1e-05
beta_first = 0.9
beta_second = 0.999
adam_epsilon = 1e-08
weight_decay = 0.1
rate_gain = 0.4
rate_inner = 0.05
rate_project = 0.04
rate_step = 0.1
rate_output = 0.08
rate_channel = 0.5
LOG2E = 1.4426950408889634
LN2 = 0.6931471805599453
HUGE = 1e30
f32 = jnp.float32
bf16 = jnp.bfloat16


def adamw_core(master, moment_one, moment_two, gradient, rate_value):
    first_new = beta_first * moment_one + (1.0 - beta_first) * gradient
    second_new = beta_second * moment_two + (1.0 - beta_second) * gradient * gradient
    scale = jnp.sqrt(second_new * (1.0 / (1.0 - beta_second**STEP))) + adam_epsilon
    corrected = first_new * (rate_value / (1.0 - beta_first**STEP)) / scale
    master_new = master * (1.0 - rate_value * weight_decay) - corrected
    return (master_new, first_new, second_new)


def dot_nn(a, b, precision=None):
    return lax.dot_general(a, b, (((1,), (0,)), ((), ())), precision=precision, preferred_element_type=f32)


def dot_nt(a, b, precision=None):
    return lax.dot_general(a, b, (((1,), (1,)), ((), ())), precision=precision, preferred_element_type=f32)


def dot_tn(a, b, precision=None):
    return lax.dot_general(a, b, (((0,), (0,)), ((), ())), precision=precision, preferred_element_type=f32)


def slab(s):
    return slice(s * LANES, (s + 1) * LANES)


def flip(index, bits):
    result = index
    place = 1
    while place <= bits:
        if bits & place:
            result = result + place * (1 - 2 * ((index // place) % 2))
        place *= 2
    return result


class Here:
    def __init__(self, chan_size):
        self.seq = lax.axis_index("seq")
        self.chan = lax.axis_index("chan")
        self.chips = chan_size // 2
        self.core = self.chan % 2
        self.chip = self.chan // 2
        self.partner = self.chan + 1 - 2 * self.core

    def same_core(self, k):
        return flip(self.chip, k) * 2 + self.core

    def other_core(self, k):
        return flip(self.chip, k) * 2 + 1 - self.core

    def copy(self, src, dst, send, recv, chan):
        return pltpu.make_async_remote_copy(
            src_ref=src, dst_ref=dst, send_sem=send, recv_sem=recv,
            device_id=(self.seq, chan), device_id_type=MESH,
        )


class Gather:
    def __init__(self, here, buf, hop, send, recv, rsend, rrecv, fsend, frecv):
        self.here, self.buf, self.hop = here, buf, hop
        self.send, self.recv, self.rsend, self.rrecv = send, recv, rsend, rrecv
        self.fsend, self.frecv = fsend, frecv
        self.half = PIECES // 2

    def place(self, j, q):
        per_row = self.buf.shape[2]
        step = SLABS // PIECES
        return self.buf.at[j // per_row, pl.ds(q * step, step), j % per_row]

    def direct(self, k, q, shard):
        h = self.here
        to = h.partner if k == 0 else h.same_core(k)
        return h.copy(self.place(shard, q), self.place(shard, q), self.send.at[k, q], self.recv.at[k, q], to)

    def relay(self, k, q, shard):
        return self.here.copy(
            self.place(shard, q), self.place(shard, q), self.rsend.at[k, q], self.rrecv.at[k, q], self.here.partner
        )

    def onward(self, q, shard, k):
        return self.here.copy(
            self.place(shard, q), self.place(shard, q), self.fsend.at[q], self.frecv.at[q], self.here.same_core(k)
        )

    def pieces(self, k):
        every = list(range(PIECES))
        return every[self.half :] + every[: self.half] if k == 1 else every

    def start(self):
        h = self.here
        for i in range(PIECES):
            for k in range(1, 3 if self.hop else h.chips):
                self.direct(k, self.pieces(k)[i] if self.hop else i, h.chan).start()
        for q in range(PIECES):
            self.direct(0, q, h.chan).start()

    def take(self, k, q):
        shard = self.here.same_core(k)
        self.direct(k, q, shard).wait_recv()
        if self.hop and (q >= self.half) == (k == 1):
            self.onward(q, shard, 3 - k).start()
        self.relay(k, q, shard).start()

    def take_across(self, q):
        shard = self.here.same_core(3)
        self.onward(q, shard, 1).wait_recv()
        self.relay(3, q, shard).start()

    def pass_on(self, i):
        if not self.hop:
            if i < PIECES:
                for k in range(1, self.here.chips):
                    self.take(k, i)
        elif i < PIECES:
            self.take(1, self.pieces(1)[i])
            self.take(2, self.pieces(2)[i])
        else:
            for q in range(self.half):
                self.take_across(q)
                self.take_across(self.half + q)

    def arrive(self, q):
        self.direct(0, q, self.here.partner).wait_recv()
        for k in range(1, self.here.chips):
            self.relay(k, q, self.here.other_core(k)).wait_recv()

    def close(self):
        for q in range(PIECES):
            for k in range(3 if self.hop else self.here.chips):
                self.direct(k, q, self.here.chan).wait_send()
            if self.hop:
                k = 1 if q >= self.half else 2
                self.onward(q, self.here.same_core(k), 3 - k).wait_send()
            for k in range(1, self.here.chips):
                self.relay(k, q, self.here.same_core(k)).wait_send()


class Reduce:
    def __init__(self, here, part, from_pair, pair, from_chips, total, send, recv):
        self.here, self.part, self.from_pair, self.pair = here, part, from_pair, pair
        self.from_chips, self.total, self.send, self.recv = from_chips, total, send, recv
        self.half = part.shape[1] // 2
        self.own = self.half // here.chips

    def half_cols(self, core):
        return pl.ds(pl.multiple_of(core * self.half, LANES), self.half)

    def own_cols(self, chip):
        return pl.ds(pl.multiple_of(chip * self.own, LANES), self.own)

    def own_total(self, chip):
        start = pl.multiple_of(self.here.core * self.half + chip * self.own, LANES)
        return self.total.at[:, pl.ds(start, self.own)]

    def swap(self):
        h = self.here
        return h.copy(
            self.part.at[:, self.half_cols(1 - h.core)], self.from_pair, self.send.at[0], self.recv.at[0], h.partner
        )

    def scatter(self, k):
        h = self.here
        return h.copy(
            self.pair.at[:, self.own_cols(flip(h.chip, k))], self.from_chips.at[k - 1],
            self.send.at[k], self.recv.at[k], h.same_core(k),
        )

    def spread(self, k, chip):
        h = self.here
        index = h.chips + k
        return h.copy(
            self.own_total(chip), self.own_total(chip), self.send.at[index], self.recv.at[index], h.same_core(k)
        )

    def share(self, core):
        h = self.here
        cols = self.total.at[:, self.half_cols(core)]
        return h.copy(cols, cols, self.send.at[h.chips], self.recv.at[h.chips], h.partner)

    def step1(self):
        self.swap().start()

    def step2(self):
        self.swap().wait()
        pair = self.part[:, self.half_cols(self.here.core)].astype(f32) + self.from_pair[...].astype(f32)
        self.from_pair[...] = pair.astype(self.from_pair.dtype)
        self.pair[...] = pair.astype(bf16)
        for k in range(1, self.here.chips):
            self.scatter(k).start()

    def step3(self):
        total = self.from_pair[:, self.own_cols(self.here.chip)].astype(f32)
        for k in range(1, self.here.chips):
            self.scatter(k).wait_recv()
            total = total + self.from_chips[k - 1].astype(f32)
        start = pl.multiple_of(self.here.core * self.half + self.here.chip * self.own, LANES)
        self.total[:, pl.ds(start, self.own)] = total.astype(bf16)
        for k in range(1, self.here.chips):
            self.spread(k, self.here.chip).start()

    def step4(self):
        for k in range(1, self.here.chips):
            self.spread(k, flip(self.here.chip, k)).wait_recv()
        self.share(self.here.core).start()

    def step5(self):
        self.share(1 - self.here.core).wait_recv()

    def close(self):
        for k in range(1, self.here.chips):
            self.scatter(k).wait_send()
            self.spread(k, self.here.chip).wait_send()
        self.share(self.here.core).wait_send()


def reorder(own_rows):
    lanes = own_rows // SLABS
    r = lax.broadcasted_iota(jnp.int32, (own_rows, own_rows), 0)
    q = lax.broadcasted_iota(jnp.int32, (own_rows, own_rows), 1)
    return jnp.where(q == (r % lanes) * SLABS + r // lanes, 1.0, 0.0)


class Scatter:
    def __init__(self, here, part, pair, landed, send1, recv1, send2, recv2):
        self.here, self.part, self.pair, self.landed = here, part, pair, landed
        self.send1, self.recv1, self.send2, self.recv2 = send1, recv1, send2, recv2
        self.slots, self.rows, self.per_row = part.shape[0], pair.shape[0], pair.shape[2]

    def slabs(self, q):
        step = SLABS // PIECES
        return pl.ds(q * step, step)

    def swap(self, r, q):
        h = self.here
        index = r * PIECES + q
        return h.copy(
            self.part.at[r % self.slots, self.slabs(q), :, 1 - h.core], self.pair.at[r, self.slabs(q)],
            self.send1.at[index], self.recv1.at[index], h.partner,
        )

    def out(self, k, q):
        h = self.here
        chip = flip(h.chip, k)
        index = (k - 1) * PIECES + q
        return h.copy(
            self.pair.at[chip // self.per_row, self.slabs(q), chip % self.per_row],
            self.landed.at[k - 1, self.slabs(q)],
            self.send2.at[index], self.recv2.at[index], h.same_core(k),
        )

    def add(self, r, q):
        step = SLABS // PIECES
        self.swap(r, q).wait()
        for s in range(q * step, (q + 1) * step):
            mine = self.part[r % self.slots, s, :, self.here.core].astype(f32)
            self.pair[r, s] = (self.pair[r, s].astype(f32) + mine).astype(bf16)

    def produce(self, partial, pipelined, between):
        step = SLABS // PIECES
        _, _, per_row, _, lanes, width = self.part.shape
        for r in range(self.rows):
            for q in range(PIECES):
                start = (r * SLABS + q * step) * LANES
                rows = partial(slice(start, start + step * LANES)).astype(bf16)
                self.part[r % self.slots, q * step : (q + 1) * step] = rows.reshape(step, per_row, 2, lanes, width)
                self.swap(r, q).start()
                if pipelined and r + 1 == self.rows and q > 0:
                    self.send(q - 1)
                    if q == 1:
                        between()
            if r + 1 < self.rows:
                for q in range(PIECES):
                    self.add(r, q)

    def send(self, q):
        self.add(self.rows - 1, q)
        for k in range(1, self.here.chips):
            self.out(k, q).start()

    def finish(self, result):
        h = self.here
        lanes = self.part.shape[4]
        for q in range(PIECES):
            for k in range(1, h.chips):
                self.out(k, q).wait()
        for s in range(SLABS):
            total = self.pair[h.chip // self.per_row, s, h.chip % self.per_row].astype(f32)
            for k in range(1, h.chips):
                total = total + self.landed[k - 1, s].astype(f32)
            result[s * lanes : (s + 1) * lanes, :] = total


class SeqSum:
    def __init__(self, here, seq_size, buf, half_in, send, recv):
        self.here, self.size, self.buf, self.half_in = here, seq_size, buf, half_in
        self.send, self.recv = send, recv
        self.half = buf.shape[0] // 2
        self.levels = seq_size.bit_length() - 1

    def rows(self, side):
        return pl.ds(pl.multiple_of(side * self.half, 16), self.half)

    def copy(self, index, src, dst, bit):
        h = self.here
        return pltpu.make_async_remote_copy(
            src_ref=src, dst_ref=dst, send_sem=self.send.at[index], recv_sem=self.recv.at[index],
            device_id=(flip(h.seq, bit), h.chan), device_id_type=MESH,
        )

    def level(self, i):
        side = self.here.seq % 2
        rows = self.rows(1 - side) if i == 0 else self.rows(side)
        return self.copy(i, self.buf.at[rows], self.half_in.at[i], 1 << i)

    def back(self):
        return self.copy(self.levels, self.buf.at[self.rows(self.here.seq % 2)], self.half_in.at[self.levels], 1)

    def start(self):
        self.level(0).start()

    def step(self, i):
        side = self.here.seq % 2
        self.level(i).wait()
        rows = self.rows(side)
        total = self.buf[rows, :].astype(f32) + self.half_in[i].astype(f32)
        self.buf[rows, :] = total.astype(bf16)
        if i + 1 < self.levels:
            self.level(i + 1).start()
        else:
            self.back().start()

    def finish(self, out, sems):
        side = self.here.seq % 2
        self.back().wait()
        copies = [
            pltpu.make_async_copy(self.buf.at[self.rows(side)], out.at[self.rows(side)], sems.at[0]),
            pltpu.make_async_copy(self.half_in.at[self.levels], out.at[self.rows(1 - side)], sems.at[1]),
        ]
        for c in copies:
            c.start()
        return copies


def iota(shape, dim):
    return lax.broadcasted_iota(jnp.int32, shape, dim)


def row_masks(resets_ref, mask_ref):
    per_row = SEQ_LEN // LANES
    chunk, place = iota((SLABS, LANES), 1), iota((SLABS, LANES), 0)
    group = LANES // SLABS
    pick_row = jnp.where(iota((LANES, per_row), 0) // group == iota((LANES, per_row), 1), 1.0, 0.0).astype(bf16)
    pick_place = jnp.where(iota((SLABS, LANES), 1) % SLABS == iota((SLABS, LANES), 0), 1.0, 0.0).astype(bf16)
    own_chunk = iota((LANES, LANES), 1) // SLABS == iota((LANES, LANES), 0) % group

    def before(values):
        moved = pltpu.roll(values, 1, 0)
        return jnp.where(place == 0, pltpu.roll(moved, 1, 1), moved)

    for r in range(mask_ref.shape[1] // SEQ_LEN):
        block = resets_ref[r * per_row : (r + 1) * per_row, :].astype(f32).astype(bf16)
        spread = jnp.where(own_chunk, dot_nn(pick_row, block), 0.0).astype(bf16)
        start = dot_nt(pick_place, spread)
        start = jnp.where((place == 0) & (chunk == 0), 1.0, start)
        keep1 = 1.0 - start
        keep2 = keep1 * before(keep1)
        keep3 = keep2 * before(before(keep1))
        for s in range(SLABS):
            cols = slice(r * SEQ_LEN + s * LANES, r * SEQ_LEN + (s + 1) * LANES)
            for j, values in enumerate((start, keep1, keep2, keep3)):
                mask_ref[j : j + 1, cols] = values[s : s + 1, :]


DECAY_COL = 8
DT_COL = 64


def softplus(values):
    e = jnp.exp(-jnp.abs(values))
    return jnp.maximum(values, 0.0) + jnp.where(e < 1e-3, e * (1.0 - e * (0.5 - e * (1.0 / 3.0))), jnp.log(1.0 + e))


def tall(channels):
    return 48 if channels % 48 == 0 else 16


def windows(total_ref, window_ref, later):
    channels = total_ref.shape[0]
    part = 96 if channels % 96 == 0 else channels
    for start in range(0, channels, part):
        rows = slice(start, start + part)
        total = total_ref[rows, :]
        for k in range(7):
            window_ref[k, rows, :] = total
            if k < 6:
                total = total + pltpu.roll(total, LANES - (1 << k) if later else 1 << k, 1)


def expand_matrix():
    return jnp.where(iota((DS * 8, DS), 0) // 8 == iota((DS * 8, DS), 1), 1.0, 0.0)


def lane_scan(values, decay, window_ref, at, later):
    for k in range(7):
        gain = jnp.exp2(decay * window_ref[k, at, :][None])
        values = values + gain * pltpu.roll(values, LANES - (1 << k) if later else 1 << k, 2)
    return pltpu.roll(values, LANES - 1 if later else 1, 2)


def tile_depth(rows_n):
    return 2 if rows_n == 1 else 1


class Tiles:
    def __init__(self, channels, rows_n):
        self.ct = tile_depth(rows_n)
        self.rows_n, self.span = rows_n, self.ct * 8
        self.tiles = channels // self.span

    def rows(self, i):
        return pl.ds(pl.multiple_of(i * self.span, self.span), self.span)

    def cols(self, r, s):
        if self.rows_n == 1:
            return slab(s)
        return pl.ds(pl.multiple_of(r * SEQ_LEN + s * LANES, LANES), LANES)

    def row_cols(self, r):
        if self.rows_n == 1:
            return slice(0, SEQ_LEN)
        return pl.ds(pl.multiple_of(r * SEQ_LEN, SEQ_LEN), SEQ_LEN)

    def each_row(self, body):
        if self.rows_n == 1:
            body(0)
        else:
            lax.fori_loop(0, self.rows_n, lambda r, carry: (body(r), carry)[1], 0)


def front_kernel(
    chan_size,
    tok_ref, cot_ref, gain_ref, inw_ref, xw_ref, outw_ref, ch_ref, dtw_ref, resets_ref,
    x_out, act_out, step_out, dy_out, gated_out, dgate_out, pj_out, ng_out, cg_out, h0_out, dec_out, mask_out, ct_out,
    ng, cg, xs, gs, slope, acts, dgs, wxg, part, from_pair, pair, from_chips, pj,
    mask, table, rowf, padded, step_ref, du_ref, y_ref, sums, wf, b8, c8, decb, h0, gated, dgate, inw, outw,
    ag_send, ag_recv, ag_rsend, ag_rrecv, ag_fsend, ag_frecv, rd_send, rd_recv, out_sem,
):
    here = Here(chan_size)
    chips = here.chips
    own_rows, width = tok_ref.shape
    lanes = own_rows // SLABS
    rows_n, _, per_row = ng.shape[:3]
    channels, tokens = xs.shape
    t = Tiles(channels, rows_n)
    copies = []

    def save(src, dst):
        c = pltpu.make_async_copy(src, dst, out_sem.at[len(copies)])
        c.start()
        copies.append(c)

    barrier = pltpu.get_barrier_semaphore()
    for k in range(1, chips):
        pl.semaphore_signal(barrier, inc=1, device_id=(here.seq, here.same_core(k)), device_id_type=MESH)
    pl.semaphore_signal(barrier, inc=1, device_id=(here.seq, here.partner), device_id_type=MESH)

    inner_load = pltpu.make_async_copy(inw_ref, inw, out_sem.at[out_sem.shape[0] - 1])
    outer_load = pltpu.make_async_copy(outw_ref, outw, out_sem.at[out_sem.shape[0] - 2])
    inner_load.start()
    outer_load.start()
    order = reorder(own_rows).astype(bf16)
    values = tok_ref[...].astype(f32)
    normed = values * lax.rsqrt(jnp.mean(values * values, axis=-1, keepdims=True) + norm_epsilon) * gain_ref[...].reshape(1, width)
    shape = (SLABS, lanes, width)
    ng[here.chan // per_row, :, here.chan % per_row] = (
        dot_nn(order, normed.astype(bf16)).astype(bf16).reshape(shape)
    )
    pl.semaphore_wait(barrier, chips)
    first = Gather(
        here, ng, chips == 4, *(sems.at[0] for sems in (ag_send, ag_recv, ag_rsend, ag_rrecv, ag_fsend, ag_frecv))
    )
    second = Gather(
        here, cg, False, *(sems.at[1] for sems in (ag_send, ag_recv, ag_rsend, ag_rrecv, ag_fsend, ag_frecv))
    )
    first.start()

    cg[here.chan // per_row, :, here.chan % per_row] = dot_nn(order, cot_ref[...]).astype(bf16).reshape(shape)
    inner_load.wait()
    outer_load.wait()
    wxg[0:channels, :] = inw[0].astype(bf16)
    wxg[channels:, :] = inw[1].astype(bf16)
    row_masks(resets_ref, mask)
    rowf[...] = jnp.zeros_like(rowf)
    rowf[0 : KC + 3, :] = ch_ref[0 : KC + 3, :]
    rowf[DECAY_COL : DECAY_COL + DS, :] = -jnp.exp(ch_ref[KC + 3 :, :]) * LOG2E
    rowf[DT_COL : DT_COL + DR, :] = dtw_ref[...]
    table[...] = rowf[...].T
    for n in range(DS):
        decb[n] = jnp.broadcast_to(table[:, DECAY_COL + n : DECAY_COL + n + 1], (channels, LANES))
    padded[...] = jnp.zeros_like(padded)
    save(mask, mask_out)
    save(table, ct_out)
    save(decb, dec_out)

    step = SLABS // PIECES
    span = step * per_row * lanes

    def project(q):
        first.arrive(q)
        for r in range(rows_n):
            block = ng[r, q * step : (q + 1) * step].reshape(span, width)
            cols = slice((r * PIECES + q) * span, (r * PIECES + q + 1) * span)
            both = dot_nt(wxg[...], block)
            xs[:, cols] = both[0:channels]
            gs[:, cols] = both[channels:]

    if first.hop:
        for i in range(PIECES + 1):
            first.pass_on(i)
        for q in range(PIECES):
            project(q)
    else:
        first.pass_on(0)
        for q in range(PIECES):
            if q + 1 < PIECES:
                first.pass_on(q + 1)
            project(q)
    save(xs, x_out)
    save(ng, ng_out)

    high = tall(channels)

    def conv_tile(index, carry):
        i = index // rows_n
        r = index % rows_n
        rows = pl.ds(pl.multiple_of(i * high, high), high)
        taps = [jnp.broadcast_to(table[rows, k : k + 1], (high, LANES)) for k in range(KC + 1)]
        earlier = {s: pltpu.roll(xs[rows, t.cols(r, s)], 1, 1) for s in range(SLABS - KC + 1, SLABS)}
        for s in range(SLABS):
            conv = taps[KC]
            for j in range(KC):
                value = xs[rows, t.cols(r, s - j)] if s >= j else earlier[SLABS + s - j]
                if j > 0:
                    value = value * mask[j : j + 1, t.cols(r, s)]
                conv = conv + taps[KC - 1 - j] * value
            acts[rows, t.cols(r, s)] = (conv * jax.nn.sigmoid(conv)).astype(bf16)
        return carry

    lax.fori_loop(0, channels // high * rows_n, conv_tile, 0)
    part[...] = dot_nn(xw_ref[...].astype(bf16), acts[...])
    reduce = Reduce(here, part, from_pair, pair, from_chips, pj, rd_send, rd_recv)
    reduce.step1()
    save(acts, act_out)
    reduce.step2()

    def gate_tile(index, carry):
        i = index // rows_n
        r = index % rows_n
        rows = pl.ds(pl.multiple_of(i * 16, 16), 16)
        for s in range(SLABS):
            gate = gs[rows, t.cols(r, s)]
            sig = jax.nn.sigmoid(gate)
            gs[rows, t.cols(r, s)] = gate * sig
            slope[rows, t.cols(r, s)] = sig * (1.0 + gate * (1.0 - sig))
        return carry

    lax.fori_loop(0, channels // 16 * rows_n, gate_tile, 0)
    reduce.step3()
    second.start()
    reduce.step4()
    reduce.step5()
    save(pj, pj_out)

    padded[DT_COL : DT_COL + DR, :] = pj[0:DR, :]
    step_ref[...] = dot_nn(table[...].astype(bf16), padded[...])

    def prelude(index, carry):
        i = index // rows_n
        r = index % rows_n
        rows = pl.ds(pl.multiple_of(i * 16, 16), 16)
        bias = jnp.broadcast_to(table[rows, KC + 1 : KC + 2], (16, LANES))
        total = jnp.zeros((16, LANES), f32)
        for s in range(SLABS):
            cols = t.cols(r, s)
            value = softplus(step_ref[rows, cols] + bias)
            step_ref[rows, cols] = value
            du_ref[rows, cols] = value * acts[rows, cols].astype(f32)
            total = total + jnp.where(mask[0:1, cols] > 0.0, HUGE, value)
        sums[pl.ds(pl.multiple_of(r * channels + i * 16, 16), 16), :] = total
        return carry

    lax.fori_loop(0, channels // 16 * rows_n, prelude, 0)
    windows(sums, wf, False)
    save(step_ref, step_out)
    expand = expand_matrix()

    def scan_row(r):
        block = pj[DR:, t.row_cols(r)]
        b8[...] = dot_nn(expand, block[0:DS].astype(f32), highest)
        c8[...] = dot_nn(expand, block[DS:].astype(f32), highest)

        def tile(ref, rows, s):
            return ref[rows, t.cols(r, s)].reshape(1, t.ct, 8, LANES)

        def state(ref, s):
            return ref[:, slab(s)].reshape(DS, 1, 8, LANES)

        def keep(dec, rows, s):
            stepk = jnp.where(mask[0:1, t.cols(r, s)] > 0.0, HUGE, step_ref[rows, t.cols(r, s)])
            return jnp.exp2(dec * stepk.reshape(1, t.ct, 8, LANES))

        of_row = pl.ds(r * DS, DS)

        def chunk_ends(i, carry):
            rows = t.rows(i)
            dec = decb[:, rows, :].reshape(DS, t.ct, 8, LANES)
            h = jnp.zeros((DS, t.ct, 8, LANES), f32)
            for s in range(SLABS):
                h = keep(dec, rows, s) * h + state(b8, s) * tile(du_ref, rows, s)
            h0[of_row, rows, :] = h.reshape(DS, t.span, LANES)
            return carry

        def chunk_starts(i, carry):
            rows = pl.ds(pl.multiple_of(i * high, high), high)
            at = pl.ds(pl.multiple_of(r * channels + i * high, high), high)
            h0[of_row, rows, :] = lane_scan(h0[of_row, rows, :], decb[:, rows, :], wf, at, False)
            return carry

        def outputs(i, carry):
            rows = t.rows(i)
            dec = decb[:, rows, :].reshape(DS, t.ct, 8, LANES)
            h = h0[of_row, rows, :].reshape(DS, t.ct, 8, LANES)
            for s in range(SLABS):
                h = keep(dec, rows, s) * h + state(b8, s) * tile(du_ref, rows, s)
                y_ref[rows, t.cols(r, s)] = jnp.sum(state(c8, s) * h, axis=0).reshape(t.span, LANES)
            return carry

        lax.fori_loop(0, t.tiles, chunk_ends, 0)
        lax.fori_loop(0, channels // high, chunk_starts, 0)
        if rows_n == 1:
            second.pass_on(0)
        lax.fori_loop(0, t.tiles, outputs, 0)

    t.each_row(scan_row)
    for q in range(1 if rows_n == 1 else 0, PIECES):
        second.pass_on(q)
    save(h0, h0_out)

    def skip_tile(index, carry):
        i = index // rows_n
        r = index % rows_n
        rows = pl.ds(pl.multiple_of(i * 16, 16), 16)
        skip = jnp.broadcast_to(table[rows, KC + 2 : KC + 3], (16, LANES))
        for s in range(SLABS):
            cols = t.cols(r, s)
            y = y_ref[rows, cols] + skip * acts[rows, cols].astype(f32)
            gated[rows, cols] = (y * gs[rows, cols]).astype(bf16)
            y_ref[rows, cols] = y * slope[rows, cols]
        return carry

    lax.fori_loop(0, channels // 16 * rows_n, skip_tile, 0)
    save(gated, gated_out)
    low = outw[...].astype(bf16)
    for q in range(PIECES):
        second.arrive(q)
        save(cg.at[:, q * step : (q + 1) * step], cg_out.at[:, q * step : (q + 1) * step])
        for r in range(rows_n):
            block = cg[r, q * step : (q + 1) * step].reshape(span, width)
            cols = slice((r * PIECES + q) * span, (r * PIECES + q + 1) * span)
            dgs[:, cols] = dot_nt(low, block)

    def grad_tile(index, carry):
        i = index // rows_n
        r = index % rows_n
        rows = pl.ds(pl.multiple_of(i * 16, 16), 16)
        for s in range(SLABS):
            cols = t.cols(r, s)
            dg = dgs[rows, cols]
            dgate[rows, cols] = (dg * y_ref[rows, cols]).astype(bf16)
            dgs[rows, cols] = dg * gs[rows, cols]
        return carry

    lax.fori_loop(0, channels // 16 * rows_n, grad_tile, 0)
    save(dgs, dy_out)
    save(dgate, dgate_out)
    first.close()
    second.close()
    reduce.close()
    for c in copies:
        c.wait()


def front_call(chan_size, tokens, cotangent, gain, in_weight, x_weight, out_weight, chan_params, dt_weight, resets):
    own_rows, width = tokens.shape
    count = resets.shape[0] * LANES
    channels = out_weight.shape[0]
    chips = chan_size // 2
    rows = count // SEQ_LEN
    wide = (channels, count)
    whole = (rows, SLABS, SEQ_LEN // own_rows, own_rows // SLABS, width)
    project = DR + 2 * DS
    any_spec = pl.BlockSpec(memory_space=pl.ANY)
    vmem = pl.BlockSpec(memory_space=pltpu.VMEM)
    dma = pltpu.SemaphoreType.DMA
    gather_sems = (2, chips, PIECES)
    states = (rows * DS, channels, LANES)
    decays = (DS, channels, LANES)
    outs = [
        (wide, f32), (wide, bf16), (wide, f32), (wide, f32), (wide, bf16), (wide, bf16), ((project, count), bf16),
        (whole, bf16), (whole, bf16), (states, f32), (decays, f32), ((4, count), f32), ((channels, LANES), f32),
    ]
    scratch = [
        (whole, bf16), (whole, bf16), (wide, f32), (wide, f32), (wide, f32), (wide, bf16), (wide, f32),
        ((2 * channels, width), bf16),
        ((project, count), f32), ((project, count // 2), f32), ((project, count // 2), bf16),
        ((chips - 1, project, count // 2 // chips), bf16), ((project, count), bf16),
        ((4, count), f32), ((channels, LANES), f32), ((LANES, channels), f32), ((LANES, count), bf16),
        (wide, f32), (wide, f32), (wide, f32), ((rows * channels, LANES), f32), ((7, rows * channels, LANES), f32),
        ((DS * 8, SEQ_LEN), f32), ((DS * 8, SEQ_LEN), f32), (decays, f32), (states, f32),
        (wide, bf16), (wide, bf16),
        ((2, channels, width), f32), ((channels, width), f32),
    ]
    return pl.pallas_call(
        functools.partial(front_kernel, chan_size),
        in_specs=[vmem] * 3 + [any_spec, vmem, any_spec] + [vmem] * 3,
        out_specs=[any_spec] * len(outs),
        out_shape=[jax.ShapeDtypeStruct(*o) for o in outs],
        scratch_shapes=[pltpu.VMEM(*s) for s in scratch]
        + [dma(gather_sems)] * 4
        + [dma((2, PIECES))] * 2
        + [dma((2 * chips,))] * 2
        + [dma((len(outs) + PIECES + 2,))],
        compiler_params=pltpu.CompilerParams(collective_id=0, has_side_effects=True, vmem_limit_bytes=60 * MIB),
        name="front",
    )(tokens, cotangent, gain, in_weight, x_weight, out_weight, chan_params, dt_weight, resets)


def back_kernel(
    chan_size, seq_size,
    table, mask, xw_ref,
    gated_in, outw_in, cot_in, step_in, act_in, pj_in, dec_in, dy_in, h0_in, dgate_in, normed_in, inw_in, x_in,
    msum_ref, dsum_ref, za_out, zb_out, zc_out, zd_out, gsum_ref,
    gated, outw, step_ref, act, pjf, decb, dy, h0, dgate, inw, rows_buf, low, dx, dc, taps_red, gin1,
    du, s1, ds2, totals, wb, b8, c8, db8, dc8, red, p0, gate_part, a_scr, ah_scr, pback,
    part, pair_buf, land, pair_d, land_d, from_pair, pair, from_chips, pj,
    za, zb, zc, zd, zha, zhb, zhc, zhd, gp, gz, gc,
    in_sem, out_sem, m_s1, m_r1, m_s2, m_r2, d_s1, d_r1, d_s2, d_r2,
    rd_send, rd_recv, z_send, z_recv, gz_send, gz_recv, gc_send, gc_recv,
):
    here = Here(chan_size)
    channels, tokens = gated.shape
    rows_n = pair_buf.shape[0]
    width = outw.shape[1]
    project = pj.shape[0]
    t = Tiles(channels, rows_n)
    tile_count = channels // 16 * rows_n

    loads = {}
    for index, (name, src, dst) in enumerate(
        (
            ("gated", gated_in, gated), ("outw", outw_in, outw), ("cot", cot_in.at[0], rows_buf.at[0]),
            ("step", step_in, step_ref), ("act", act_in, act), ("pj", pj_in, pjf), ("dec", dec_in, decb),
            ("dy", dy_in, dy), ("h0", h0_in, h0), ("dgate", dgate_in, dgate),
            ("normed", normed_in.at[0], rows_buf.at[1]), ("inw", inw_in, inw), ("x", x_in, du),
        )
    ):
        loads[name] = pltpu.make_async_copy(src, dst, in_sem.at[index])
    early = ("gated", "outw", "cot")
    for name in early:
        loads[name].start()

    barrier = pltpu.get_barrier_semaphore()
    for k in range(1, chan_size):
        pl.semaphore_signal(barrier, inc=1, device_id=(here.seq, flip(here.chan, k)), device_id_type=MESH)
    for k in range(1, seq_size):
        pl.semaphore_signal(barrier, inc=1, device_id=(flip(here.seq, k), here.chan), device_id_type=MESH)

    reduce = Reduce(here, pback, from_pair, pair, from_chips, pj, rd_send, rd_recv)
    mixed = Scatter(here, part, pair_buf, land, m_s1, m_r1, m_s2, m_r2)
    own = (pair_d, land_d) if rows_n == 1 else (pair_buf, land)
    normed_grad = Scatter(here, part, *own, d_s1, d_r1, d_s2, d_r2)
    sum_a = SeqSum(here, seq_size, za, zha, z_send.at[0], z_recv.at[0])
    sum_b = SeqSum(here, seq_size, zb, zhb, z_send.at[1], z_recv.at[1])
    sum_c = SeqSum(here, seq_size, zc, zhc, z_send.at[2], z_recv.at[2])
    sum_d = SeqSum(here, seq_size, zd, zhd, z_send.at[3], z_recv.at[3])
    if za.shape[0] > channels:
        for buf in (za, zb, zc, zd):
            buf[channels:, :] = jnp.zeros((buf.shape[0] - channels, buf.shape[1]), bf16)

    def row_block(slot):
        return rows_buf[slot].reshape(SEQ_LEN, width)

    def row_cols(r):
        return slice(r * SEQ_LEN, (r + 1) * SEQ_LEN)

    def fetch(src, r, slot, name):
        index = list(loads).index(name)
        c = pltpu.make_async_copy(src.at[r], rows_buf.at[slot], in_sem.at[index])
        c.start()
        return c

    loads["gated"].wait()
    loads["outw"].wait()
    for name in loads:
        if name not in early and name != "x":
            loads[name].start()
    low[0] = outw[...].astype(bf16)
    pl.semaphore_wait(barrier, chan_size - 1 + seq_size - 1)
    mixed.produce(lambda cols: dot_tn(gated[:, cols], low[0]), True, lambda: None)
    mixed.send(PIECES - 1)
    loads["cot"].wait()
    out_grad = dot_nn(gated[:, row_cols(0)], row_block(0))
    for r in range(1, rows_n):
        fetch(cot_in, r, 0, "cot").wait()
        out_grad = out_grad + dot_nn(gated[:, row_cols(r)], row_block(0))
    za[0:channels, :] = out_grad.astype(bf16)
    sum_a.start()
    loads["dgate"].wait()
    loads["normed"].wait()
    in_grad = dot_nn(dgate[:, row_cols(0)], row_block(1))
    for r in range(1, rows_n):
        fetch(normed_in, r, 1, "normed").wait()
        in_grad = in_grad + dot_nn(dgate[:, row_cols(r)], row_block(1))
    gin1[...] = in_grad
    zb[0:channels, :] = in_grad.astype(bf16)
    sum_b.start()
    loads["inw"].wait()
    low[0] = inw[0].astype(bf16)
    low[1] = inw[1].astype(bf16)

    for name in ("step", "act", "pj", "dec", "dy", "h0"):
        loads[name].wait()
    red[...] = jnp.zeros_like(red)

    def prelude(index, carry):
        i = index // rows_n
        r = index % rows_n
        rows = pl.ds(pl.multiple_of(i * 16, 16), 16)
        total = jnp.zeros((16, LANES), f32)
        for s in range(SLABS):
            cols = t.cols(r, s)
            value = step_ref[rows, cols]
            du[rows, cols] = value * act[rows, cols].astype(f32)
            s1[rows, cols] = jnp.zeros((16, LANES), f32)
            ds2[rows, cols] = jnp.zeros((16, LANES), f32)
            total = total + jnp.where(mask[0:1, cols] > 0.0, HUGE, value)
        totals[pl.ds(pl.multiple_of(r * channels + i * 16, 16), 16), :] = total
        return carry

    lax.fori_loop(0, tile_count, prelude, 0)
    windows(totals, wb, True)
    expand = expand_matrix()

    high = tall(channels)
    levels = seq_size.bit_length() - 1

    def adjoint_row(r):
        whole_row = t.row_cols(r)
        block = pjf[DR:, whole_row]
        b8[...] = dot_nn(expand, block[0:DS].astype(f32), highest)
        c8[...] = dot_nn(expand, block[DS:].astype(f32), highest)
        db8[...] = jnp.zeros_like(db8)
        dc8[...] = jnp.zeros_like(dc8)

        def tile(ref, rows, s):
            return ref[rows, t.cols(r, s)].reshape(1, t.ct, 8, LANES)

        def state(ref, s):
            return ref[:, slab(s)].reshape(DS, 1, 8, LANES)

        def keep(dec, rows, s):
            stepk = jnp.where(mask[0:1, t.cols(r, s)] > 0.0, HUGE, step_ref[rows, t.cols(r, s)])
            return jnp.exp2(dec * stepk.reshape(1, t.ct, 8, LANES))

        def chunk_ends(i, carry):
            rows = t.rows(i)
            dec = decb[:, rows, :].reshape(DS, t.ct, 8, LANES)
            p = jnp.zeros((DS, t.ct, 8, LANES), f32)
            for s in reversed(range(SLABS)):
                p = keep(dec, rows, s) * (tile(dy, rows, s) * state(c8, s) + p)
            p0[:, rows, :] = p.reshape(DS, t.span, LANES)
            return carry

        def chunk_starts(i, carry):
            rows = pl.ds(pl.multiple_of(i * high, high), high)
            at = pl.ds(pl.multiple_of(r * channels + i * high, high), high)
            p0[:, rows, :] = lane_scan(p0[:, rows, :], decb[:, rows, :], wb, at, True)
            return carry

        def adjoints(index, carry):
            i, g = index // (DS // NG), index % (DS // NG)
            rows = t.rows(i)
            some = pl.ds(g * NG, NG)
            lines = pl.ds(pl.multiple_of(g * (NG * 8), NG * 8), NG * 8)
            shape = (NG, t.ct, 8, LANES)

            def state(ref, s):
                return ref[lines, slab(s)].reshape(NG, 1, 8, LANES)

            dec = decb[some, rows, :].reshape(shape)
            h = h0[pl.ds(r * DS + g * NG, NG), rows, :].reshape(shape)
            for s in range(SLABS):
                a = keep(dec, rows, s)
                a_scr[s] = a
                ah = a * h
                ah_scr[s] = ah
                h = ah + state(b8, s) * tile(du, rows, s)
                dc8[lines, slab(s)] += jnp.sum(tile(dy, rows, s) * h, axis=1).reshape(NG * 8, LANES)
            p = p0[some, rows, :].reshape(shape)
            rate = jnp.zeros(shape, f32)
            for s in reversed(range(SLABS)):
                lam = tile(dy, rows, s) * state(c8, s) + p
                p = a_scr[s] * lam
                s1[rows, t.cols(r, s)] += jnp.sum(lam * state(b8, s), axis=0).reshape(t.span, LANES)
                db8[lines, slab(s)] += jnp.sum(lam * tile(du, rows, s), axis=1).reshape(NG * 8, LANES)
                q = lam * ah_scr[s]
                ds2[rows, t.cols(r, s)] += jnp.sum(dec * q, axis=0).reshape(t.span, LANES)
                rate = rate + q * tile(step_ref, rows, s)
            for n in range(NG):
                cols = pl.ds(pl.multiple_of((g * NG + n) * LANES, LANES), LANES)
                red[rows, cols] += rate[n].reshape(t.span, LANES)
            return carry

        lax.fori_loop(0, t.tiles, chunk_ends, 0)
        lax.fori_loop(0, channels // high, chunk_starts, 0)
        if rows_n == 1:
            sum_a.step(0)
            sum_b.step(0)
        lax.fori_loop(0, t.tiles * (DS // NG), adjoints, 0)
        pback[DR : DR + DS, whole_row] = dot_tn(expand, db8[...], highest).astype(bf16)
        pback[DR + DS :, whole_row] = dot_tn(expand, dc8[...], highest).astype(bf16)

    t.each_row(adjoint_row)
    if rows_n > 1:
        sum_a.step(0)
        sum_b.step(0)
    if rows_n > 1:
        mixed.finish(msum_ref)
    loads["x"].start()
    x_buf = du

    def adjoint_tile(index, carry):
        i = index // rows_n
        r = index % rows_n
        rows = pl.ds(pl.multiple_of(i * 16, 16), 16)
        skip = jnp.broadcast_to(table[rows, KC + 2 : KC + 3], (16, LANES))
        skip_sum = jnp.zeros((16, LANES), f32)
        bias_sum = jnp.zeros((16, LANES), f32)
        for s in range(SLABS):
            cols = t.cols(r, s)
            value = step_ref[rows, cols]
            lam_b = s1[rows, cols]
            d_y = dy[rows, cols]
            act_s = act[rows, cols].astype(f32)
            s1[rows, cols] = d_y * skip + lam_b * value
            small = value * (1.0 - value * (0.5 - value * (1.0 / 6.0)))
            slope = jnp.where(value < 0.01, small, 1.0 - jnp.exp(-value))
            back = ((lam_b * act_s + LN2 * ds2[rows, cols]) * slope).astype(bf16)
            dx[rows, cols] = back
            skip_sum = skip_sum + d_y * act_s
            bias_sum = bias_sum + back.astype(f32)
        red[rows, DS * LANES : (DS + 1) * LANES] += skip_sum
        red[rows, (DS + 1) * LANES :] += bias_sum
        return carry

    lax.fori_loop(0, tile_count, adjoint_tile, 0)
    low_table = table[...].astype(bf16)
    for r in range(rows_n):
        pback[0:DR, row_cols(r)] = dot_tn(low_table, dx[:, row_cols(r)])[DT_COL : DT_COL + DR].astype(bf16)
    reduce.step1()
    pick = jnp.where(iota(((DS + 2) * LANES, LANES), 0) // LANES == iota(((DS + 2) * LANES, LANES), 1), 1.0, 0.0)
    dt_grad = jnp.concatenate(
        [
            jnp.zeros((channels, DT_COL), f32),
            dot_nt(dx[...], pjf[0:DR, :]),
            jnp.zeros((channels, LANES - DT_COL - DR), f32),
        ],
        axis=1,
    )
    zd[0:channels, :] = (dot_nn(red[...], pick, highest) + dt_grad).astype(bf16)
    sum_d.start()
    reduce.step2()
    reduce.step3()
    if rows_n == 1:
        for q in range(PIECES):
            cols = slice(q * SEQ_LEN // PIECES, (q + 1) * SEQ_LEN // PIECES)
            gate_part[cols, :] = dot_tn(dgate[:, cols], low[1])
    reduce.step4()
    for i in range(1, levels):
        sum_a.step(i)
        sum_b.step(i)
    sum_d.step(0)
    loads["x"].wait()
    x_low = xw_ref[...].astype(bf16)
    reduce.step5()
    for r in range(rows_n):
        s1[:, row_cols(r)] += dot_tn(x_low, pj[:, row_cols(r)])

    def conv_tile(index, carry):
        i = index // rows_n
        r = index % rows_n
        rows = pl.ds(pl.multiple_of(i * high, high), high)
        taps = [jnp.broadcast_to(table[rows, k : k + 1], (high, LANES)) for k in range(KC + 1)]
        earlier = {s: pltpu.roll(x_buf[rows, t.cols(r, s)], 1, 1) for s in range(SLABS - KC + 1, SLABS)}
        sums = [jnp.zeros((high, LANES), f32) for _ in range(KC + 1)]
        for s in range(SLABS):
            cols = t.cols(r, s)
            inputs = []
            conv = taps[KC]
            for j in range(KC):
                value = x_buf[rows, t.cols(r, s - j)] if s >= j else earlier[SLABS + s - j]
                if j > 0:
                    value = value * mask[j : j + 1, cols]
                inputs.append(value)
                conv = conv + taps[KC - 1 - j] * value
            sig = jax.nn.sigmoid(conv)
            d_conv = s1[rows, cols] * (sig * (1.0 + conv * (1.0 - sig)))
            dc[:, slab(s)] = d_conv
            for j in range(KC):
                sums[KC - 1 - j] = sums[KC - 1 - j] + d_conv * inputs[j]
            sums[KC] = sums[KC] + d_conv
        wrapped = {}
        for s in range(KC - 1):
            for j in range(s + 1, KC):
                wrapped[s, j] = pltpu.roll(dc[:, slab(s)] * mask[j : j + 1, t.cols(r, s)], LANES - 1, 1)
        for s in range(SLABS):
            d_x = taps[KC - 1] * dc[:, slab(s)]
            for j in range(1, KC):
                if s + j < SLABS:
                    value = dc[:, slab(s + j)] * mask[j : j + 1, t.cols(r, s + j)]
                else:
                    value = wrapped[s + j - SLABS, j]
                d_x = d_x + taps[KC - 1 - j] * value
            dx[rows, t.cols(r, s)] = d_x.astype(bf16)
        for k in range(KC + 1):
            @pl.when(r == 0)
            def _():
                taps_red[rows, slab(k)] = sums[k]

            @pl.when(r > 0)
            def _():
                taps_red[rows, slab(k)] += sums[k]
        return carry

    lax.fori_loop(0, channels // high * rows_n, conv_tile, 0)

    def weight_sums():
        if rows_n > 1:
            fetch(normed_in, 0, 1, "normed").wait()
        in_grad = dot_nn(dx[:, row_cols(0)], row_block(1))
        for r in range(1, rows_n):
            fetch(normed_in, r, 1, "normed").wait()
            in_grad = in_grad + dot_nn(dx[:, row_cols(r)], row_block(1))
        zc[0:channels, 0:width] = in_grad.astype(bf16)
        x_grad = dot_nt(act[...], pj[...])
        x_grad = jnp.concatenate([x_grad, jnp.zeros((channels, LANES - project), f32)], axis=1)
        k_i = iota(((KC + 1) * LANES, LANES), 0)
        pick = jnp.where(k_i // LANES + project == iota(((KC + 1) * LANES, LANES), 1), 1.0, 0.0)
        zc[0:channels, width : width + LANES] = (x_grad + dot_nn(taps_red[...], pick, highest)).astype(bf16)
        sum_c.start()

        both = low[0].astype(f32) * in_grad + low[1].astype(f32) * gin1[...]
        gp[...] = jnp.sum(both.reshape(channels // 8, 8, width), axis=0)

    def normed_part(cols):
        gate = gate_part[cols, :] if rows_n == 1 else dot_tn(dgate[:, cols], low[1])
        return dot_tn(dx[:, cols], low[0]) + gate

    weight_sums()
    normed_grad.produce(normed_part, True, lambda: None)
    normed_grad.send(PIECES - 1)

    def gain_seq(k):
        return pltpu.make_async_remote_copy(
            src_ref=gp, dst_ref=gz.at[k - 1], send_sem=gz_send.at[k - 1], recv_sem=gz_recv.at[k - 1],
            device_id=(flip(here.seq, k), here.chan), device_id_type=MESH,
        )

    def gain_chan(k):
        return here.copy(gz.at[seq_size - 1], gc.at[k - 1], gc_send.at[k - 1], gc_recv.at[k - 1], flip(here.chan, k))

    for k in range(1, seq_size):
        gain_seq(k).start()
    for k in range(1, seq_size):
        gain_seq(k).wait()
    total = gp[...]
    for k in range(1, seq_size):
        total = total + gz[k - 1]
    gz[seq_size - 1] = total
    for k in range(1, chan_size):
        gain_chan(k).start()
    saves = sum_a.finish(za_out, out_sem.at[0])
    saves += sum_b.finish(zb_out, out_sem.at[1])
    for i in range(1, levels):
        sum_d.step(i)
    if rows_n == 1:
        mixed.finish(msum_ref)
    for i in range(levels):
        sum_c.step(i)
    saves += sum_d.finish(zd_out, out_sem.at[3])
    for k in range(1, chan_size):
        gain_chan(k).wait()
        total = total + gc[k - 1]
    gsum_ref[...] = total
    normed_grad.finish(dsum_ref)
    saves += sum_c.finish(zc_out, out_sem.at[2])
    reduce.close()
    for c in saves:
        c.wait()


def back_call(
    chan_size, seq_size, own_rows, table, masks, x_weight, gated, out_weight, cot_all, step, act, pj, decays, dy, h0,
    dgate, normed_all, in_weight, x_cols,
):
    channels, width = out_weight.shape
    count = masks.shape[1]
    chips = chan_size // 2
    rows = count // SEQ_LEN
    per_row = SEQ_LEN // own_rows // 2
    lanes = own_rows // SLABS
    project = DR + 2 * DS
    wide = (channels, count)
    padded = (channels + 31) // 32 * 32
    levels = seq_size.bit_length() - 1
    any_spec = pl.BlockSpec(memory_space=pl.ANY)
    vmem = pl.BlockSpec(memory_space=pltpu.VMEM)
    dma = pltpu.SemaphoreType.DMA
    sums = ((padded, width), (padded, width), (padded, width + LANES), (padded, LANES))
    states = (DS * 8, SEQ_LEN)
    loops = (SLABS, NG, tile_depth(rows), 8, LANES)
    outs = [
        ((own_rows, width), f32), ((own_rows, width), f32), (sums[0], bf16), (sums[1], bf16), (sums[2], bf16),
        (sums[3], bf16), ((8, width), f32),
    ]
    scratch = [
        (wide, bf16), ((channels, width), f32), (wide, f32), (wide, bf16), ((project, count), bf16),
        ((DS, channels, LANES), f32), (wide, f32), ((rows * DS, channels, LANES), f32), (wide, bf16),
        ((2, channels, width), f32), ((2, SLABS, 2 * per_row, lanes, width), bf16),
        ((2, channels, width), bf16), (wide, bf16), ((tall(channels), SEQ_LEN), f32), ((channels, (KC + 1) * LANES), f32),
        ((channels, width), f32),
        (wide, f32), (wide, f32), (wide, f32), ((rows * channels, LANES), f32), ((7, rows * channels, LANES), f32),
        (states, f32), (states, f32), (states, f32), (states, f32), ((channels, (DS + 2) * LANES), f32),
        ((DS, channels, LANES), f32), ((SEQ_LEN if rows == 1 else 8, width), f32), (loops, f32), (loops, f32), ((project, count), bf16),
        ((min(rows, 2), SLABS, per_row, 2, lanes, width), bf16), ((rows, SLABS, per_row, lanes, width), bf16),
        ((chips - 1, SLABS, lanes, width), bf16),
        ((rows, SLABS, per_row, lanes, width) if rows == 1 else (16, LANES), bf16),
        ((chips - 1, SLABS, lanes, width) if rows == 1 else (16, LANES), bf16),
        ((project, count // 2), bf16), ((project, count // 2), bf16),
        ((chips - 1, project, count // 2 // chips), bf16), ((project, count), bf16),
        (sums[0], bf16), (sums[1], bf16), (sums[2], bf16), (sums[3], bf16),
    ]
    scratch += [((levels + 1, padded // 2, s[1]), bf16) for s in sums]
    scratch += [((8, width), f32), ((seq_size, 8, width), f32), ((chan_size - 1, 8, width), f32)]
    return pl.pallas_call(
        functools.partial(back_kernel, chan_size, seq_size),
        in_specs=[vmem] * 3 + [any_spec] * 13,
        out_specs=[vmem, vmem, any_spec, any_spec, any_spec, any_spec, vmem],
        out_shape=[jax.ShapeDtypeStruct(*o) for o in outs],
        scratch_shapes=[pltpu.VMEM(*s) for s in scratch]
        + [dma((13,)), dma((4, 2))]
        + ([dma((rows * PIECES,))] * 2 + [dma((chips * PIECES,))] * 2) * 2
        + [dma((2 * chips,))] * 2
        + [dma((4, levels + 1))] * 2
        + [dma((seq_size,))] * 2
        + [dma((chan_size,))] * 2,
        compiler_params=pltpu.CompilerParams(collective_id=1, has_side_effects=True, vmem_limit_bytes=60 * MIB),
        name="back",
    )(
        table, masks, x_weight, gated, out_weight, cot_all, step, act, pj, decays, dy, h0, dgate, normed_all, in_weight, x_cols
    )


def update(grad, master, first, second, rate, outs):
    new = adamw_core(master, first, second, grad, rate)
    for ref, value in zip(outs, new):
        ref[...] = value
    outs[3][...] = new[0].astype(bf16)


def finish_kernel(
    tok_ref, cot_ref, msum_ref, dsum_ref, za_ref, zb_ref, zc_ref, zb_all, zc_all, gsum_ref,
    gain_m, gain_f, gain_s, in_m, in_f, in_s, x_m, x_f, x_s, dt_m, dt_f, dt_s, out_m, out_f, out_s, ch_m, ch_f, ch_s,
    mixed_ref, tgrad_ref, *rest,
):
    gain_o, in_o, x_o, dt_o, out_o, ch_o = (rest[i * 4 : i * 4 + 4] for i in range(6))
    ch_grad = rest[24]
    i = pl.program_id(0)
    width = tok_ref.shape[1]
    own_rows = msum_ref.shape[0]
    block = tok_ref.shape[0]
    lanes = own_rows // SLABS
    channels = x_m.shape[1]

    r = lax.broadcasted_iota(jnp.int32, (block, own_rows), 0) + i * block
    q = lax.broadcasted_iota(jnp.int32, (block, own_rows), 1)
    order = jnp.where(r == (q % lanes) * SLABS + q // lanes, 1.0, 0.0).astype(bf16)

    def in_order(ref):
        values = ref[...]
        high = values.astype(bf16)
        return dot_nn(order, high) + dot_nn(order, (values - high.astype(f32)).astype(bf16))

    values = tok_ref[...].astype(f32)
    mixed_ref[...] = (values + in_order(msum_ref)).astype(bf16)
    d_normed = in_order(dsum_ref)
    rstd = lax.rsqrt(jnp.mean(values * values, axis=-1, keepdims=True) + norm_epsilon)
    gain_row = gain_m[...].reshape(1, width)
    scaled = gain_row * d_normed
    mean = jnp.mean(scaled * values, axis=-1, keepdims=True)
    tgrad_ref[...] = cot_ref[...].astype(f32) + rstd * scaled - values * (rstd * rstd * rstd * mean)

    out_grad = za_ref[...].astype(f32)
    update(out_grad, out_m[...], out_f[...], out_s[...], rate_output, out_o)
    for k, ref in ((0, zc_ref), (1, zb_ref)):
        grad = ref[:, 0:width].astype(f32)
        new = adamw_core(in_m[k], in_f[k], in_s[k], grad, rate_inner)
        for o, value in zip(in_o, new):
            o[k] = value
        in_o[3][k] = new[0].astype(bf16)

    @pl.when(i == 0)
    def _():
        grad_b = zb_all[...].astype(f32).T
        grad_c = zc_all[...].astype(f32).T
        update(grad_b[64 : 64 + DR, 0:channels], dt_m[...], dt_f[...], dt_s[...], rate_step, dt_o)
        project = x_m.shape[0]
        update(grad_c[0:project, 0:channels], x_m[...], x_f[...], x_s[...], rate_project, x_o)
        ch_grad[0 : KC + 1, :] = grad_c[project : project + KC + 1, 0:channels]
        ch_grad[KC + 1 : KC + 2, :] = grad_b[DS + 1 : DS + 2, 0:channels]
        ch_grad[KC + 2 : KC + 3, :] = grad_b[DS : DS + 1, 0:channels]
        ch_grad[KC + 3 :, :] = grad_b[0:DS, 0:channels] * -jnp.exp(ch_m[KC + 3 :, :])
        update(ch_grad[...], ch_m[...], ch_f[...], ch_s[...], rate_channel, ch_o)
        gain_grad = jnp.sum(gsum_ref[...], axis=0, keepdims=True) / gain_row
        moments = (ref[...].reshape(1, width) for ref in (gain_f, gain_s))
        new = adamw_core(gain_row, *moments, gain_grad, rate_gain)
        for ref, value in zip(gain_o, (*new, new[0].astype(bf16))):
            ref[...] = value.reshape(width)


def finish_call(tokens, cotangent, msum, dsum, za, zb, zc, zd, gsum, gains, inners, projects, steps, outputs, chans):
    own_rows, width = tokens.shape
    channels = outputs[0].shape[0]
    cb = 96 if channels % 96 == 0 else channels
    grid = channels // cb
    block = own_rows // grid
    row = pl.BlockSpec((block, width), lambda i: (i, 0))

    def full(shape):
        return pl.BlockSpec(shape, lambda i: (0,) * len(shape))

    inner = pl.BlockSpec((2, cb, width), lambda i: (0, i, 0))
    outer = pl.BlockSpec((cb, width), lambda i: (i, 0))
    tails = [full(zd.shape), pl.BlockSpec((zc.shape[0], LANES), lambda i: (0, width // LANES))]
    zed = pl.BlockSpec((cb, width), lambda i: (i, 0))
    groups = (gains, inners, projects, steps, outputs, chans)
    specs = (full(gains[0].shape), inner, full(projects[0].shape), full(steps[0].shape), outer, full(chans[0].shape))
    in_specs = [row, row, full(msum.shape), full(dsum.shape), zed, zed, zed, *tails, full(gsum.shape)]
    out_specs = [row, row]
    out_shape = [jax.ShapeDtypeStruct(tokens.shape, bf16), jax.ShapeDtypeStruct(tokens.shape, f32)]
    args = [tokens, cotangent, msum, dsum, za, zb, zc, zd, zc, gsum]
    for arrays, spec in zip(groups, specs):
        in_specs += [spec] * 3
        out_specs += [spec] * 4
        out_shape += [jax.ShapeDtypeStruct(arrays[0].shape, f32)] * 3 + [jax.ShapeDtypeStruct(arrays[0].shape, bf16)]
        args += list(arrays)
    return pl.pallas_call(
        finish_kernel,
        grid=(grid,),
        in_specs=in_specs,
        out_specs=out_specs,
        out_shape=out_shape,
        scratch_shapes=[pltpu.VMEM(chans[0].shape, f32)],
        compiler_params=pltpu.CompilerParams(dimension_semantics=("arbitrary",), vmem_limit_bytes=60 * MIB),
        name="finish",
    )(*args)


def per_device(
    tokens,
    resets,
    cotangent,
    norm_gain,
    in_weight,
    x_weight,
    dt_weight,
    out_weight,
    chan_params,
    gain_first,
    gain_second,
    in_first,
    in_second,
    x_first,
    x_second,
    dt_first,
    dt_second,
    out_first,
    out_second,
    chan_first,
    chan_second,
):
    own_count = tokens.shape[0]
    chan_size = lax.axis_size("chan")
    seq_size = lax.axis_size("seq")
    inners = [jnp.swapaxes(a, 1, 2) for a in (in_weight, in_first, in_second)]
    projects = [a.T for a in (x_weight, x_first, x_second)]
    x_cols, act, step, dy, gated, dgate, pj, normed_all, cot_all, h0, decays, masks, table = front_call(
        chan_size, tokens, cotangent, norm_gain, inners[0], projects[0], out_weight, chan_params, dt_weight,
        resets.reshape(-1, LANES),
    )
    msum, dsum, za, zb, zc, zd, gsum = back_call(
        chan_size, seq_size, own_count, table, masks, projects[0], gated, out_weight, cot_all, step, act, pj, decays, dy, h0,
        dgate, normed_all, inners[0], x_cols,
    )
    result = finish_call(
        tokens, cotangent, msum, dsum, za, zb, zc, zd, gsum,
        (norm_gain, gain_first, gain_second),
        inners,
        projects,
        (dt_weight, dt_first, dt_second),
        (out_weight, out_first, out_second),
        (chan_params, chan_first, chan_second),
    )
    result = list(result)
    result[6:10] = [jnp.swapaxes(a, 1, 2) for a in result[6:10]]
    result[10:14] = [a.T for a in result[10:14]]
    return tuple(result)


def solution(mesh):
    rows = P(("seq", "chan"), None)
    inner = P(None, None, "chan")
    by_row = P("chan", None)
    by_col = P(None, "chan")
    placed = (rows, P("seq"), rows, P(), inner, by_row, by_col, by_row, by_col, P(), P())
    placed += (inner, inner, by_row, by_row, by_col, by_col, by_row, by_row, by_col, by_col)
    return jax.shard_map(
        per_device,
        mesh=mesh,
        in_specs=placed,
        out_specs=(rows, rows)
        + (P(),) * 4
        + (inner,) * 4
        + (by_row,) * 4
        + (by_col,) * 4
        + (by_row,) * 4
        + (by_col,) * 4,
        check_vma=False,
    )
```

```python
import functools

import jax
import jax.numpy as jnp
from jax import lax
from jax.experimental import pallas as pl
from jax.experimental.pallas import tpu as pltpu
from jax.sharding import PartitionSpec as P

DS = 16
DR = 48
KC = 4
SEQ_LEN = 2048
STEP = 10
SLABS = 16
LANES = 128
NG = 4
PIECES = 2
MIB = 1024 * 1024
MESH = pl.DeviceIdType.MESH

highest = lax.Precision.HIGHEST
norm_epsilon = 1e-05
beta_first = 0.9
beta_second = 0.999
adam_epsilon = 1e-08
weight_decay = 0.1
rate_gain = 0.4
rate_inner = 0.05
rate_project = 0.04
rate_step = 0.1
rate_output = 0.08
rate_channel = 0.5
LOG2E = 1.4426950408889634
LN2 = 0.6931471805599453
HUGE = 1e30
f32 = jnp.float32
bf16 = jnp.bfloat16


def adamw_core(master, moment_one, moment_two, gradient, rate_value):
    first_new = beta_first * moment_one + (1.0 - beta_first) * gradient
    second_new = beta_second * moment_two + (1.0 - beta_second) * gradient * gradient
    scale = jnp.sqrt(second_new * (1.0 / (1.0 - beta_second**STEP))) + adam_epsilon
    corrected = first_new * (rate_value / (1.0 - beta_first**STEP)) / scale
    master_new = master * (1.0 - rate_value * weight_decay) - corrected
    return (master_new, first_new, second_new)


def dot_nn(a, b, precision=None):
    return lax.dot_general(a, b, (((1,), (0,)), ((), ())), precision=precision, preferred_element_type=f32)


def dot_nt(a, b, precision=None):
    return lax.dot_general(a, b, (((1,), (1,)), ((), ())), precision=precision, preferred_element_type=f32)


def dot_tn(a, b, precision=None):
    return lax.dot_general(a, b, (((0,), (0,)), ((), ())), precision=precision, preferred_element_type=f32)


def slab(s):
    return slice(s * LANES, (s + 1) * LANES)


def flip(index, bits):
    result = index
    place = 1
    while place <= bits:
        if bits & place:
            result = result + place * (1 - 2 * ((index // place) % 2))
        place *= 2
    return result


class Here:
    def __init__(self, chan_size):
        self.seq = lax.axis_index("seq")
        self.chan = lax.axis_index("chan")
        self.chips = chan_size // 2
        self.core = self.chan % 2
        self.chip = self.chan // 2
        self.partner = self.chan + 1 - 2 * self.core

    def same_core(self, k):
        return flip(self.chip, k) * 2 + self.core

    def other_core(self, k):
        return flip(self.chip, k) * 2 + 1 - self.core

    def copy(self, src, dst, send, recv, chan):
        return pltpu.make_async_remote_copy(
            src_ref=src, dst_ref=dst, send_sem=send, recv_sem=recv,
            device_id=(self.seq, chan), device_id_type=MESH,
        )


class Gather:
    def __init__(self, here, buf, hop, send, recv, rsend, rrecv, fsend, frecv):
        self.here, self.buf, self.hop = here, buf, hop
        self.send, self.recv, self.rsend, self.rrecv = send, recv, rsend, rrecv
        self.fsend, self.frecv = fsend, frecv
        self.half = PIECES // 2

    def place(self, j, q):
        per_row = self.buf.shape[2]
        step = SLABS // PIECES
        return self.buf.at[j // per_row, pl.ds(q * step, step), j % per_row]

    def direct(self, k, q, shard):
        h = self.here
        to = h.partner if k == 0 else h.same_core(k)
        return h.copy(self.place(shard, q), self.place(shard, q), self.send.at[k, q], self.recv.at[k, q], to)

    def relay(self, k, q, shard):
        return self.here.copy(
            self.place(shard, q), self.place(shard, q), self.rsend.at[k, q], self.rrecv.at[k, q], self.here.partner
        )

    def onward(self, q, shard, k):
        return self.here.copy(
            self.place(shard, q), self.place(shard, q), self.fsend.at[q], self.frecv.at[q], self.here.same_core(k)
        )

    def pieces(self, k):
        every = list(range(PIECES))
        return every[self.half :] + every[: self.half] if k == 1 else every

    def start(self):
        h = self.here
        for i in range(PIECES):
            for k in range(1, 3 if self.hop else h.chips):
                self.direct(k, self.pieces(k)[i] if self.hop else i, h.chan).start()
        for q in range(PIECES):
            self.direct(0, q, h.chan).start()

    def take(self, k, q):
        shard = self.here.same_core(k)
        self.direct(k, q, shard).wait_recv()
        if self.hop and (q >= self.half) == (k == 1):
            self.onward(q, shard, 3 - k).start()
        self.relay(k, q, shard).start()

    def take_across(self, q):
        shard = self.here.same_core(3)
        self.onward(q, shard, 1).wait_recv()
        self.relay(3, q, shard).start()

    def pass_on(self, i):
        if not self.hop:
            if i < PIECES:
                for k in range(1, self.here.chips):
                    self.take(k, i)
        elif i < PIECES:
            self.take(1, self.pieces(1)[i])
            self.take(2, self.pieces(2)[i])
        else:
            for q in range(self.half):
                self.take_across(q)
                self.take_across(self.half + q)

    def arrive(self, q):
        self.direct(0, q, self.here.partner).wait_recv()
        for k in range(1, self.here.chips):
            self.relay(k, q, self.here.other_core(k)).wait_recv()

    def close(self):
        for q in range(PIECES):
            for k in range(3 if self.hop else self.here.chips):
                self.direct(k, q, self.here.chan).wait_send()
            if self.hop:
                k = 1 if q >= self.half else 2
                self.onward(q, self.here.same_core(k), 3 - k).wait_send()
            for k in range(1, self.here.chips):
                self.relay(k, q, self.here.same_core(k)).wait_send()


class Reduce:
    def __init__(self, here, part, from_pair, pair, from_chips, total, send, recv):
        self.here, self.part, self.from_pair, self.pair = here, part, from_pair, pair
        self.from_chips, self.total, self.send, self.recv = from_chips, total, send, recv
        self.half = part.shape[1] // 2
        self.own = self.half // here.chips

    def half_cols(self, core):
        return pl.ds(pl.multiple_of(core * self.half, LANES), self.half)

    def own_cols(self, chip):
        return pl.ds(pl.multiple_of(chip * self.own, LANES), self.own)

    def own_total(self, chip):
        start = pl.multiple_of(self.here.core * self.half + chip * self.own, LANES)
        return self.total.at[:, pl.ds(start, self.own)]

    def swap(self):
        h = self.here
        return h.copy(
            self.part.at[:, self.half_cols(1 - h.core)], self.from_pair, self.send.at[0], self.recv.at[0], h.partner
        )

    def scatter(self, k):
        h = self.here
        return h.copy(
            self.pair.at[:, self.own_cols(flip(h.chip, k))], self.from_chips.at[k - 1],
            self.send.at[k], self.recv.at[k], h.same_core(k),
        )

    def spread(self, k, chip):
        h = self.here
        index = h.chips + k
        return h.copy(
            self.own_total(chip), self.own_total(chip), self.send.at[index], self.recv.at[index], h.same_core(k)
        )

    def share(self, core):
        h = self.here
        cols = self.total.at[:, self.half_cols(core)]
        return h.copy(cols, cols, self.send.at[h.chips], self.recv.at[h.chips], h.partner)

    def step1(self):
        self.swap().start()

    def step2(self):
        self.swap().wait()
        pair = self.part[:, self.half_cols(self.here.core)].astype(f32) + self.from_pair[...].astype(f32)
        self.from_pair[...] = pair.astype(self.from_pair.dtype)
        self.pair[...] = pair.astype(bf16)
        for k in range(1, self.here.chips):
            self.scatter(k).start()

    def step3(self):
        total = self.from_pair[:, self.own_cols(self.here.chip)].astype(f32)
        for k in range(1, self.here.chips):
            self.scatter(k).wait_recv()
            total = total + self.from_chips[k - 1].astype(f32)
        start = pl.multiple_of(self.here.core * self.half + self.here.chip * self.own, LANES)
        self.total[:, pl.ds(start, self.own)] = total.astype(bf16)
        for k in range(1, self.here.chips):
            self.spread(k, self.here.chip).start()

    def step4(self):
        for k in range(1, self.here.chips):
            self.spread(k, flip(self.here.chip, k)).wait_recv()
        self.share(self.here.core).start()

    def step5(self):
        self.share(1 - self.here.core).wait_recv()

    def close(self):
        for k in range(1, self.here.chips):
            self.scatter(k).wait_send()
            self.spread(k, self.here.chip).wait_send()
        self.share(self.here.core).wait_send()


def reorder(own_rows):
    lanes = own_rows // SLABS
    r = lax.broadcasted_iota(jnp.int32, (own_rows, own_rows), 0)
    q = lax.broadcasted_iota(jnp.int32, (own_rows, own_rows), 1)
    return jnp.where(q == (r % lanes) * SLABS + r // lanes, 1.0, 0.0)


class Scatter:
    def __init__(self, here, part, pair, landed, send1, recv1, send2, recv2):
        self.here, self.part, self.pair, self.landed = here, part, pair, landed
        self.send1, self.recv1, self.send2, self.recv2 = send1, recv1, send2, recv2
        self.slots, self.rows, self.per_row = part.shape[0], pair.shape[0], pair.shape[2]

    def slabs(self, q):
        step = SLABS // PIECES
        return pl.ds(q * step, step)

    def swap(self, r, q):
        h = self.here
        index = r * PIECES + q
        return h.copy(
            self.part.at[r % self.slots, self.slabs(q), :, 1 - h.core], self.pair.at[r, self.slabs(q)],
            self.send1.at[index], self.recv1.at[index], h.partner,
        )

    def out(self, k, q):
        h = self.here
        chip = flip(h.chip, k)
        index = (k - 1) * PIECES + q
        return h.copy(
            self.pair.at[chip // self.per_row, self.slabs(q), chip % self.per_row],
            self.landed.at[k - 1, self.slabs(q)],
            self.send2.at[index], self.recv2.at[index], h.same_core(k),
        )

    def add(self, r, q):
        step = SLABS // PIECES
        self.swap(r, q).wait()
        for s in range(q * step, (q + 1) * step):
            mine = self.part[r % self.slots, s, :, self.here.core].astype(f32)
            self.pair[r, s] = (self.pair[r, s].astype(f32) + mine).astype(bf16)

    def produce(self, partial, pipelined, between):
        step = SLABS // PIECES
        _, _, per_row, _, lanes, width = self.part.shape
        for r in range(self.rows):
            for q in range(PIECES):
                start = (r * SLABS + q * step) * LANES
                rows = partial(slice(start, start + step * LANES)).astype(bf16)
                self.part[r % self.slots, q * step : (q + 1) * step] = rows.reshape(step, per_row, 2, lanes, width)
                self.swap(r, q).start()
                if pipelined and r + 1 == self.rows and q > 0:
                    self.send(q - 1)
                    if q == 1:
                        between()
            if r + 1 < self.rows:
                for q in range(PIECES):
                    self.add(r, q)

    def send(self, q):
        self.add(self.rows - 1, q)
        for k in range(1, self.here.chips):
            self.out(k, q).start()

    def finish(self, result):
        h = self.here
        lanes = self.part.shape[4]
        for q in range(PIECES):
            for k in range(1, h.chips):
                self.out(k, q).wait()
        for s in range(SLABS):
            total = self.pair[h.chip // self.per_row, s, h.chip % self.per_row].astype(f32)
            for k in range(1, h.chips):
                total = total + self.landed[k - 1, s].astype(f32)
            result[s * lanes : (s + 1) * lanes, :] = total


class SeqSum:
    def __init__(self, here, seq_size, buf, half_in, send, recv):
        self.here, self.size, self.buf, self.half_in = here, seq_size, buf, half_in
        self.send, self.recv = send, recv
        self.half = buf.shape[0] // 2
        self.levels = seq_size.bit_length() - 1

    def rows(self, side):
        return pl.ds(pl.multiple_of(side * self.half, 16), self.half)

    def copy(self, index, src, dst, bit):
        h = self.here
        return pltpu.make_async_remote_copy(
            src_ref=src, dst_ref=dst, send_sem=self.send.at[index], recv_sem=self.recv.at[index],
            device_id=(flip(h.seq, bit), h.chan), device_id_type=MESH,
        )

    def level(self, i):
        side = self.here.seq % 2
        rows = self.rows(1 - side) if i == 0 else self.rows(side)
        return self.copy(i, self.buf.at[rows], self.half_in.at[i], 1 << i)

    def back(self):
        return self.copy(self.levels, self.buf.at[self.rows(self.here.seq % 2)], self.half_in.at[self.levels], 1)

    def start(self):
        self.level(0).start()

    def step(self, i):
        side = self.here.seq % 2
        self.level(i).wait()
        rows = self.rows(side)
        total = self.buf[rows, :].astype(f32) + self.half_in[i].astype(f32)
        self.buf[rows, :] = total.astype(bf16)
        if i + 1 < self.levels:
            self.level(i + 1).start()
        else:
            self.back().start()

    def finish(self, out, sems):
        side = self.here.seq % 2
        self.back().wait()
        copies = [
            pltpu.make_async_copy(self.buf.at[self.rows(side)], out.at[self.rows(side)], sems.at[0]),
            pltpu.make_async_copy(self.half_in.at[self.levels], out.at[self.rows(1 - side)], sems.at[1]),
        ]
        for c in copies:
            c.start()
        return copies


def iota(shape, dim):
    return lax.broadcasted_iota(jnp.int32, shape, dim)


def row_masks(resets_ref, mask_ref):
    per_row = SEQ_LEN // LANES
    chunk, place = iota((SLABS, LANES), 1), iota((SLABS, LANES), 0)
    group = LANES // SLABS
    pick_row = jnp.where(iota((LANES, per_row), 0) // group == iota((LANES, per_row), 1), 1.0, 0.0).astype(bf16)
    pick_place = jnp.where(iota((SLABS, LANES), 1) % SLABS == iota((SLABS, LANES), 0), 1.0, 0.0).astype(bf16)
    own_chunk = iota((LANES, LANES), 1) // SLABS == iota((LANES, LANES), 0) % group

    def before(values):
        moved = pltpu.roll(values, 1, 0)
        return jnp.where(place == 0, pltpu.roll(moved, 1, 1), moved)

    for r in range(mask_ref.shape[1] // SEQ_LEN):
        block = resets_ref[r * per_row : (r + 1) * per_row, :].astype(f32).astype(bf16)
        spread = jnp.where(own_chunk, dot_nn(pick_row, block), 0.0).astype(bf16)
        start = dot_nt(pick_place, spread)
        start = jnp.where((place == 0) & (chunk == 0), 1.0, start)
        keep1 = 1.0 - start
        keep2 = keep1 * before(keep1)
        keep3 = keep2 * before(before(keep1))
        for s in range(SLABS):
            cols = slice(r * SEQ_LEN + s * LANES, r * SEQ_LEN + (s + 1) * LANES)
            for j, values in enumerate((start, keep1, keep2, keep3)):
                mask_ref[j : j + 1, cols] = values[s : s + 1, :]


DECAY_COL = 8
DT_COL = 64


def softplus(values):
    e = jnp.exp(-jnp.abs(values))
    return jnp.maximum(values, 0.0) + jnp.where(e < 1e-3, e * (1.0 - e * (0.5 - e * (1.0 / 3.0))), jnp.log(1.0 + e))


def tall(channels):
    return 48 if channels % 48 == 0 else 16


def windows(total_ref, window_ref, later):
    channels = total_ref.shape[0]
    part = 96 if channels % 96 == 0 else channels
    for start in range(0, channels, part):
        rows = slice(start, start + part)
        total = total_ref[rows, :]
        for k in range(7):
            window_ref[k, rows, :] = total
            if k < 6:
                total = total + pltpu.roll(total, LANES - (1 << k) if later else 1 << k, 1)


def expand_matrix():
    return jnp.where(iota((DS * 8, DS), 0) // 8 == iota((DS * 8, DS), 1), 1.0, 0.0)


def lane_scan(values, decay, window_ref, at, later):
    for k in range(7):
        gain = jnp.exp2(decay * window_ref[k, at, :][None])
        values = values + gain * pltpu.roll(values, LANES - (1 << k) if later else 1 << k, 2)
    return pltpu.roll(values, LANES - 1 if later else 1, 2)


def tile_depth(rows_n):
    return 2 if rows_n == 1 else 1


class Tiles:
    def __init__(self, channels, rows_n):
        self.ct = tile_depth(rows_n)
        self.rows_n, self.span = rows_n, self.ct * 8
        self.tiles = channels // self.span

    def rows(self, i):
        return pl.ds(pl.multiple_of(i * self.span, self.span), self.span)

    def cols(self, r, s):
        if self.rows_n == 1:
            return slab(s)
        return pl.ds(pl.multiple_of(r * SEQ_LEN + s * LANES, LANES), LANES)

    def row_cols(self, r):
        if self.rows_n == 1:
            return slice(0, SEQ_LEN)
        return pl.ds(pl.multiple_of(r * SEQ_LEN, SEQ_LEN), SEQ_LEN)

    def each_row(self, body):
        if self.rows_n == 1:
            body(0)
        else:
            lax.fori_loop(0, self.rows_n, lambda r, carry: (body(r), carry)[1], 0)


def front_kernel(
    chan_size,
    tok_ref, cot_ref, gain_ref, inw_ref, xw_ref, outw_ref, ch_ref, dtw_ref, resets_ref,
    x_out, act_out, step_out, dy_out, gated_out, dgate_out, pj_out, ng_out, cg_out, h0_out, dec_out, mask_out, ct_out,
    ng, cg, xs, gs, slope, acts, dgs, wxg, part, from_pair, pair, from_chips, pj,
    mask, table, rowf, padded, step_ref, du_ref, y_ref, sums, wf, b8, c8, decb, h0, gated, dgate, inw, outw,
    ag_send, ag_recv, ag_rsend, ag_rrecv, ag_fsend, ag_frecv, rd_send, rd_recv, out_sem,
):
    here = Here(chan_size)
    chips = here.chips
    own_rows, width = tok_ref.shape
    lanes = own_rows // SLABS
    rows_n, _, per_row = ng.shape[:3]
    channels, tokens = xs.shape
    t = Tiles(channels, rows_n)
    copies = []

    def save(src, dst):
        c = pltpu.make_async_copy(src, dst, out_sem.at[len(copies)])
        c.start()
        copies.append(c)

    barrier = pltpu.get_barrier_semaphore()
    for k in range(1, chips):
        pl.semaphore_signal(barrier, inc=1, device_id=(here.seq, here.same_core(k)), device_id_type=MESH)
    pl.semaphore_signal(barrier, inc=1, device_id=(here.seq, here.partner), device_id_type=MESH)

    inner_load = pltpu.make_async_copy(inw_ref, inw, out_sem.at[out_sem.shape[0] - 1])
    outer_load = pltpu.make_async_copy(outw_ref, outw, out_sem.at[out_sem.shape[0] - 2])
    inner_load.start()
    outer_load.start()
    order = reorder(own_rows).astype(bf16)
    values = tok_ref[...].astype(f32)
    normed = values * lax.rsqrt(jnp.mean(values * values, axis=-1, keepdims=True) + norm_epsilon) * gain_ref[...].reshape(1, width)
    shape = (SLABS, lanes, width)
    ng[here.chan // per_row, :, here.chan % per_row] = (
        dot_nn(order, normed.astype(bf16)).astype(bf16).reshape(shape)
    )
    pl.semaphore_wait(barrier, chips)
    first = Gather(
        here, ng, chips == 4, *(sems.at[0] for sems in (ag_send, ag_recv, ag_rsend, ag_rrecv, ag_fsend, ag_frecv))
    )
    second = Gather(
        here, cg, False, *(sems.at[1] for sems in (ag_send, ag_recv, ag_rsend, ag_rrecv, ag_fsend, ag_frecv))
    )
    first.start()

    cg[here.chan // per_row, :, here.chan % per_row] = dot_nn(order, cot_ref[...]).astype(bf16).reshape(shape)
    inner_load.wait()
    outer_load.wait()
    wxg[0:channels, :] = inw[0].astype(bf16)
    wxg[channels:, :] = inw[1].astype(bf16)
    row_masks(resets_ref, mask)
    rowf[...] = jnp.zeros_like(rowf)
    rowf[0 : KC + 3, :] = ch_ref[0 : KC + 3, :]
    rowf[DECAY_COL : DECAY_COL + DS, :] = -jnp.exp(ch_ref[KC + 3 :, :]) * LOG2E
    rowf[DT_COL : DT_COL + DR, :] = dtw_ref[...]
    table[...] = rowf[...].T
    for n in range(DS):
        decb[n] = jnp.broadcast_to(table[:, DECAY_COL + n : DECAY_COL + n + 1], (channels, LANES))
    padded[...] = jnp.zeros_like(padded)
    save(mask, mask_out)
    save(table, ct_out)
    save(decb, dec_out)

    step = SLABS // PIECES
    span = step * per_row * lanes

    def project(q):
        first.arrive(q)
        for r in range(rows_n):
            block = ng[r, q * step : (q + 1) * step].reshape(span, width)
            cols = slice((r * PIECES + q) * span, (r * PIECES + q + 1) * span)
            both = dot_nt(wxg[...], block)
            xs[:, cols] = both[0:channels]
            gs[:, cols] = both[channels:]

    if first.hop:
        for i in range(PIECES + 1):
            first.pass_on(i)
        for q in range(PIECES):
            project(q)
    else:
        first.pass_on(0)
        for q in range(PIECES):
            if q + 1 < PIECES:
                first.pass_on(q + 1)
            project(q)
    save(xs, x_out)
    save(ng, ng_out)

    high = tall(channels)

    def conv_tile(index, carry):
        i = index // rows_n
        r = index % rows_n
        rows = pl.ds(pl.multiple_of(i * high, high), high)
        taps = [jnp.broadcast_to(table[rows, k : k + 1], (high, LANES)) for k in range(KC + 1)]
        earlier = {s: pltpu.roll(xs[rows, t.cols(r, s)], 1, 1) for s in range(SLABS - KC + 1, SLABS)}
        for s in range(SLABS):
            conv = taps[KC]
            for j in range(KC):
                value = xs[rows, t.cols(r, s - j)] if s >= j else earlier[SLABS + s - j]
                if j > 0:
                    value = value * mask[j : j + 1, t.cols(r, s)]
                conv = conv + taps[KC - 1 - j] * value
            acts[rows, t.cols(r, s)] = (conv * jax.nn.sigmoid(conv)).astype(bf16)
        return carry

    lax.fori_loop(0, channels // high * rows_n, conv_tile, 0)
    part[...] = dot_nn(xw_ref[...].astype(bf16), acts[...])
    reduce = Reduce(here, part, from_pair, pair, from_chips, pj, rd_send, rd_recv)
    reduce.step1()
    save(acts, act_out)
    reduce.step2()
    second.start()

    def gate_tile(index, carry):
        i = index // rows_n
        r = index % rows_n
        rows = pl.ds(pl.multiple_of(i * 16, 16), 16)
        for s in range(SLABS):
            gate = gs[rows, t.cols(r, s)]
            sig = jax.nn.sigmoid(gate)
            gs[rows, t.cols(r, s)] = gate * sig
            slope[rows, t.cols(r, s)] = sig * (1.0 + gate * (1.0 - sig))
        return carry

    lax.fori_loop(0, channels // 16 * rows_n, gate_tile, 0)
    reduce.step3()
    reduce.step4()
    reduce.step5()
    save(pj, pj_out)

    padded[DT_COL : DT_COL + DR, :] = pj[0:DR, :]
    step_ref[...] = dot_nn(table[...].astype(bf16), padded[...])

    def prelude(index, carry):
        i = index // rows_n
        r = index % rows_n
        rows = pl.ds(pl.multiple_of(i * 16, 16), 16)
        bias = jnp.broadcast_to(table[rows, KC + 1 : KC + 2], (16, LANES))
        total = jnp.zeros((16, LANES), f32)
        for s in range(SLABS):
            cols = t.cols(r, s)
            value = softplus(step_ref[rows, cols] + bias)
            step_ref[rows, cols] = value
            du_ref[rows, cols] = value * acts[rows, cols].astype(f32)
            total = total + jnp.where(mask[0:1, cols] > 0.0, HUGE, value)
        sums[pl.ds(pl.multiple_of(r * channels + i * 16, 16), 16), :] = total
        return carry

    lax.fori_loop(0, channels // 16 * rows_n, prelude, 0)
    windows(sums, wf, False)
    save(step_ref, step_out)
    expand = expand_matrix()

    def scan_row(r):
        block = pj[DR:, t.row_cols(r)]
        b8[...] = dot_nn(expand, block[0:DS].astype(f32), highest)
        c8[...] = dot_nn(expand, block[DS:].astype(f32), highest)

        def tile(ref, rows, s):
            return ref[rows, t.cols(r, s)].reshape(1, t.ct, 8, LANES)

        def state(ref, s):
            return ref[:, slab(s)].reshape(DS, 1, 8, LANES)

        def keep(dec, rows, s):
            stepk = jnp.where(mask[0:1, t.cols(r, s)] > 0.0, HUGE, step_ref[rows, t.cols(r, s)])
            return jnp.exp2(dec * stepk.reshape(1, t.ct, 8, LANES))

        of_row = pl.ds(r * DS, DS)

        def chunk_ends(i, carry):
            rows = t.rows(i)
            dec = decb[:, rows, :].reshape(DS, t.ct, 8, LANES)
            h = jnp.zeros((DS, t.ct, 8, LANES), f32)
            for s in range(SLABS):
                h = keep(dec, rows, s) * h + state(b8, s) * tile(du_ref, rows, s)
            h0[of_row, rows, :] = h.reshape(DS, t.span, LANES)
            return carry

        def chunk_starts(i, carry):
            rows = pl.ds(pl.multiple_of(i * high, high), high)
            at = pl.ds(pl.multiple_of(r * channels + i * high, high), high)
            h0[of_row, rows, :] = lane_scan(h0[of_row, rows, :], decb[:, rows, :], wf, at, False)
            return carry

        def outputs(i, carry):
            rows = t.rows(i)
            dec = decb[:, rows, :].reshape(DS, t.ct, 8, LANES)
            h = h0[of_row, rows, :].reshape(DS, t.ct, 8, LANES)
            for s in range(SLABS):
                h = keep(dec, rows, s) * h + state(b8, s) * tile(du_ref, rows, s)
                y_ref[rows, t.cols(r, s)] = jnp.sum(state(c8, s) * h, axis=0).reshape(t.span, LANES)
            return carry

        lax.fori_loop(0, t.tiles, chunk_ends, 0)
        lax.fori_loop(0, channels // high, chunk_starts, 0)
        if rows_n == 1:
            second.pass_on(0)
        lax.fori_loop(0, t.tiles, outputs, 0)

    t.each_row(scan_row)
    for q in range(1 if rows_n == 1 else 0, PIECES):
        second.pass_on(q)
    save(h0, h0_out)

    def skip_tile(index, carry):
        i = index // rows_n
        r = index % rows_n
        rows = pl.ds(pl.multiple_of(i * 16, 16), 16)
        skip = jnp.broadcast_to(table[rows, KC + 2 : KC + 3], (16, LANES))
        for s in range(SLABS):
            cols = t.cols(r, s)
            y = y_ref[rows, cols] + skip * acts[rows, cols].astype(f32)
            gated[rows, cols] = (y * gs[rows, cols]).astype(bf16)
            y_ref[rows, cols] = y * slope[rows, cols]
        return carry

    lax.fori_loop(0, channels // 16 * rows_n, skip_tile, 0)
    save(gated, gated_out)
    low = outw[...].astype(bf16)
    for q in range(PIECES):
        second.arrive(q)
        save(cg.at[:, q * step : (q + 1) * step], cg_out.at[:, q * step : (q + 1) * step])
        for r in range(rows_n):
            block = cg[r, q * step : (q + 1) * step].reshape(span, width)
            cols = slice((r * PIECES + q) * span, (r * PIECES + q + 1) * span)
            dgs[:, cols] = dot_nt(low, block)

    def grad_tile(index, carry):
        i = index // rows_n
        r = index % rows_n
        rows = pl.ds(pl.multiple_of(i * 16, 16), 16)
        for s in range(SLABS):
            cols = t.cols(r, s)
            dg = dgs[rows, cols]
            dgate[rows, cols] = (dg * y_ref[rows, cols]).astype(bf16)
            dgs[rows, cols] = dg * gs[rows, cols]
        return carry

    lax.fori_loop(0, channels // 16 * rows_n, grad_tile, 0)
    save(dgs, dy_out)
    save(dgate, dgate_out)
    first.close()
    second.close()
    reduce.close()
    for c in copies:
        c.wait()


def front_call(chan_size, tokens, cotangent, gain, in_weight, x_weight, out_weight, chan_params, dt_weight, resets):
    own_rows, width = tokens.shape
    count = resets.shape[0] * LANES
    channels = out_weight.shape[0]
    chips = chan_size // 2
    rows = count // SEQ_LEN
    wide = (channels, count)
    whole = (rows, SLABS, SEQ_LEN // own_rows, own_rows // SLABS, width)
    project = DR + 2 * DS
    any_spec = pl.BlockSpec(memory_space=pl.ANY)
    vmem = pl.BlockSpec(memory_space=pltpu.VMEM)
    dma = pltpu.SemaphoreType.DMA
    gather_sems = (2, chips, PIECES)
    states = (rows * DS, channels, LANES)
    decays = (DS, channels, LANES)
    outs = [
        (wide, f32), (wide, bf16), (wide, f32), (wide, f32), (wide, bf16), (wide, bf16), ((project, count), bf16),
        (whole, bf16), (whole, bf16), (states, f32), (decays, f32), ((4, count), f32), ((channels, LANES), f32),
    ]
    scratch = [
        (whole, bf16), (whole, bf16), (wide, f32), (wide, f32), (wide, f32), (wide, bf16), (wide, f32),
        ((2 * channels, width), bf16),
        ((project, count), f32), ((project, count // 2), f32), ((project, count // 2), bf16),
        ((chips - 1, project, count // 2 // chips), bf16), ((project, count), bf16),
        ((4, count), f32), ((channels, LANES), f32), ((LANES, channels), f32), ((LANES, count), bf16),
        (wide, f32), (wide, f32), (wide, f32), ((rows * channels, LANES), f32), ((7, rows * channels, LANES), f32),
        ((DS * 8, SEQ_LEN), f32), ((DS * 8, SEQ_LEN), f32), (decays, f32), (states, f32),
        (wide, bf16), (wide, bf16),
        ((2, channels, width), f32), ((channels, width), f32),
    ]
    return pl.pallas_call(
        functools.partial(front_kernel, chan_size),
        in_specs=[vmem] * 3 + [any_spec, vmem, any_spec] + [vmem] * 3,
        out_specs=[any_spec] * len(outs),
        out_shape=[jax.ShapeDtypeStruct(*o) for o in outs],
        scratch_shapes=[pltpu.VMEM(*s) for s in scratch]
        + [dma(gather_sems)] * 4
        + [dma((2, PIECES))] * 2
        + [dma((2 * chips,))] * 2
        + [dma((len(outs) + PIECES + 2,))],
        compiler_params=pltpu.CompilerParams(collective_id=0, has_side_effects=True, vmem_limit_bytes=60 * MIB),
        name="front",
    )(tokens, cotangent, gain, in_weight, x_weight, out_weight, chan_params, dt_weight, resets)


def back_kernel(
    chan_size, seq_size,
    table, mask, xw_ref,
    gated_in, outw_in, cot_in, step_in, act_in, pj_in, dec_in, dy_in, h0_in, dgate_in, normed_in, inw_in, x_in,
    msum_ref, dsum_ref, za_out, zb_out, zc_out, zd_out, gsum_ref,
    gated, outw, step_ref, act, pjf, decb, dy, h0, dgate, inw, rows_buf, low, dx, dc, taps_red, gin1,
    du, s1, ds2, totals, wb, b8, c8, db8, dc8, red, p0, gate_part, a_scr, ah_scr, pback,
    part, pair_buf, land, pair_d, land_d, from_pair, pair, from_chips, pj,
    za, zb, zc, zd, zha, zhb, zhc, zhd, gp, gz, gc,
    in_sem, out_sem, m_s1, m_r1, m_s2, m_r2, d_s1, d_r1, d_s2, d_r2,
    rd_send, rd_recv, z_send, z_recv, gz_send, gz_recv, gc_send, gc_recv,
):
    here = Here(chan_size)
    channels, tokens = gated.shape
    rows_n = pair_buf.shape[0]
    width = outw.shape[1]
    project = pj.shape[0]
    t = Tiles(channels, rows_n)
    tile_count = channels // 16 * rows_n

    loads = {}
    for index, (name, src, dst) in enumerate(
        (
            ("gated", gated_in, gated), ("outw", outw_in, outw), ("cot", cot_in.at[0], rows_buf.at[0]),
            ("step", step_in, step_ref), ("act", act_in, act), ("pj", pj_in, pjf), ("dec", dec_in, decb),
            ("dy", dy_in, dy), ("h0", h0_in, h0), ("dgate", dgate_in, dgate),
            ("normed", normed_in.at[0], rows_buf.at[1]), ("inw", inw_in, inw), ("x", x_in, du),
        )
    ):
        loads[name] = pltpu.make_async_copy(src, dst, in_sem.at[index])
    early = ("gated", "outw", "cot")
    for name in early:
        loads[name].start()

    barrier = pltpu.get_barrier_semaphore()
    for k in range(1, chan_size):
        pl.semaphore_signal(barrier, inc=1, device_id=(here.seq, flip(here.chan, k)), device_id_type=MESH)
    for k in range(1, seq_size):
        pl.semaphore_signal(barrier, inc=1, device_id=(flip(here.seq, k), here.chan), device_id_type=MESH)

    reduce = Reduce(here, pback, from_pair, pair, from_chips, pj, rd_send, rd_recv)
    mixed = Scatter(here, part, pair_buf, land, m_s1, m_r1, m_s2, m_r2)
    own = (pair_d, land_d) if rows_n == 1 else (pair_buf, land)
    normed_grad = Scatter(here, part, *own, d_s1, d_r1, d_s2, d_r2)
    sum_a = SeqSum(here, seq_size, za, zha, z_send.at[0], z_recv.at[0])
    sum_b = SeqSum(here, seq_size, zb, zhb, z_send.at[1], z_recv.at[1])
    sum_c = SeqSum(here, seq_size, zc, zhc, z_send.at[2], z_recv.at[2])
    sum_d = SeqSum(here, seq_size, zd, zhd, z_send.at[3], z_recv.at[3])
    if za.shape[0] > channels:
        for buf in (za, zb, zc, zd):
            buf[channels:, :] = jnp.zeros((buf.shape[0] - channels, buf.shape[1]), bf16)

    def row_block(slot):
        return rows_buf[slot].reshape(SEQ_LEN, width)

    def row_cols(r):
        return slice(r * SEQ_LEN, (r + 1) * SEQ_LEN)

    def fetch(src, r, slot, name):
        index = list(loads).index(name)
        c = pltpu.make_async_copy(src.at[r], rows_buf.at[slot], in_sem.at[index])
        c.start()
        return c

    loads["gated"].wait()
    loads["outw"].wait()
    for name in loads:
        if name not in early and name != "x":
            loads[name].start()
    low[0] = outw[...].astype(bf16)
    pl.semaphore_wait(barrier, chan_size - 1 + seq_size - 1)
    mixed.produce(lambda cols: dot_tn(gated[:, cols], low[0]), True, lambda: None)
    mixed.send(PIECES - 1)
    loads["cot"].wait()
    out_grad = dot_nn(gated[:, row_cols(0)], row_block(0))
    for r in range(1, rows_n):
        fetch(cot_in, r, 0, "cot").wait()
        out_grad = out_grad + dot_nn(gated[:, row_cols(r)], row_block(0))
    za[0:channels, :] = out_grad.astype(bf16)
    sum_a.start()
    loads["dgate"].wait()
    loads["normed"].wait()
    in_grad = dot_nn(dgate[:, row_cols(0)], row_block(1))
    for r in range(1, rows_n):
        fetch(normed_in, r, 1, "normed").wait()
        in_grad = in_grad + dot_nn(dgate[:, row_cols(r)], row_block(1))
    gin1[...] = in_grad
    zb[0:channels, :] = in_grad.astype(bf16)
    sum_b.start()
    loads["inw"].wait()
    low[0] = inw[0].astype(bf16)
    low[1] = inw[1].astype(bf16)

    for name in ("step", "act", "pj", "dec", "dy", "h0"):
        loads[name].wait()
    red[...] = jnp.zeros_like(red)

    def prelude(index, carry):
        i = index // rows_n
        r = index % rows_n
        rows = pl.ds(pl.multiple_of(i * 16, 16), 16)
        total = jnp.zeros((16, LANES), f32)
        for s in range(SLABS):
            cols = t.cols(r, s)
            value = step_ref[rows, cols]
            du[rows, cols] = value * act[rows, cols].astype(f32)
            s1[rows, cols] = jnp.zeros((16, LANES), f32)
            ds2[rows, cols] = jnp.zeros((16, LANES), f32)
            total = total + jnp.where(mask[0:1, cols] > 0.0, HUGE, value)
        totals[pl.ds(pl.multiple_of(r * channels + i * 16, 16), 16), :] = total
        return carry

    lax.fori_loop(0, tile_count, prelude, 0)
    windows(totals, wb, True)
    expand = expand_matrix()

    high = tall(channels)
    levels = seq_size.bit_length() - 1

    def adjoint_row(r):
        whole_row = t.row_cols(r)
        block = pjf[DR:, whole_row]
        b8[...] = dot_nn(expand, block[0:DS].astype(f32), highest)
        c8[...] = dot_nn(expand, block[DS:].astype(f32), highest)
        db8[...] = jnp.zeros_like(db8)
        dc8[...] = jnp.zeros_like(dc8)

        def tile(ref, rows, s):
            return ref[rows, t.cols(r, s)].reshape(1, t.ct, 8, LANES)

        def state(ref, s):
            return ref[:, slab(s)].reshape(DS, 1, 8, LANES)

        def keep(dec, rows, s):
            stepk = jnp.where(mask[0:1, t.cols(r, s)] > 0.0, HUGE, step_ref[rows, t.cols(r, s)])
            return jnp.exp2(dec * stepk.reshape(1, t.ct, 8, LANES))

        def chunk_ends(i, carry):
            rows = t.rows(i)
            dec = decb[:, rows, :].reshape(DS, t.ct, 8, LANES)
            p = jnp.zeros((DS, t.ct, 8, LANES), f32)
            for s in reversed(range(SLABS)):
                p = keep(dec, rows, s) * (tile(dy, rows, s) * state(c8, s) + p)
            p0[:, rows, :] = p.reshape(DS, t.span, LANES)
            return carry

        def chunk_starts(i, carry):
            rows = pl.ds(pl.multiple_of(i * high, high), high)
            at = pl.ds(pl.multiple_of(r * channels + i * high, high), high)
            p0[:, rows, :] = lane_scan(p0[:, rows, :], decb[:, rows, :], wb, at, True)
            return carry

        def adjoints(index, carry):
            i, g = index // (DS // NG), index % (DS // NG)
            rows = t.rows(i)
            some = pl.ds(g * NG, NG)
            lines = pl.ds(pl.multiple_of(g * (NG * 8), NG * 8), NG * 8)
            shape = (NG, t.ct, 8, LANES)

            def state(ref, s):
                return ref[lines, slab(s)].reshape(NG, 1, 8, LANES)

            dec = decb[some, rows, :].reshape(shape)
            h = h0[pl.ds(r * DS + g * NG, NG), rows, :].reshape(shape)
            for s in range(SLABS):
                a = keep(dec, rows, s)
                a_scr[s] = a
                ah = a * h
                ah_scr[s] = ah
                h = ah + state(b8, s) * tile(du, rows, s)
                dc8[lines, slab(s)] += jnp.sum(tile(dy, rows, s) * h, axis=1).reshape(NG * 8, LANES)
            p = p0[some, rows, :].reshape(shape)
            rate = jnp.zeros(shape, f32)
            for s in reversed(range(SLABS)):
                lam = tile(dy, rows, s) * state(c8, s) + p
                p = a_scr[s] * lam
                s1[rows, t.cols(r, s)] += jnp.sum(lam * state(b8, s), axis=0).reshape(t.span, LANES)
                db8[lines, slab(s)] += jnp.sum(lam * tile(du, rows, s), axis=1).reshape(NG * 8, LANES)
                q = lam * ah_scr[s]
                ds2[rows, t.cols(r, s)] += jnp.sum(dec * q, axis=0).reshape(t.span, LANES)
                rate = rate + q * tile(step_ref, rows, s)
            for n in range(NG):
                cols = pl.ds(pl.multiple_of((g * NG + n) * LANES, LANES), LANES)
                red[rows, cols] += rate[n].reshape(t.span, LANES)
            return carry

        lax.fori_loop(0, t.tiles, chunk_ends, 0)
        lax.fori_loop(0, channels // high, chunk_starts, 0)
        if rows_n == 1:
            sum_a.step(0)
            sum_b.step(0)
        lax.fori_loop(0, t.tiles * (DS // NG), adjoints, 0)
        pback[DR : DR + DS, whole_row] = dot_tn(expand, db8[...], highest).astype(bf16)
        pback[DR + DS :, whole_row] = dot_tn(expand, dc8[...], highest).astype(bf16)

    t.each_row(adjoint_row)
    if rows_n > 1:
        sum_a.step(0)
        sum_b.step(0)
    if rows_n > 1:
        mixed.finish(msum_ref)
    loads["x"].start()
    x_buf = du

    def adjoint_tile(index, carry):
        i = index // rows_n
        r = index % rows_n
        rows = pl.ds(pl.multiple_of(i * 16, 16), 16)
        skip = jnp.broadcast_to(table[rows, KC + 2 : KC + 3], (16, LANES))
        skip_sum = jnp.zeros((16, LANES), f32)
        bias_sum = jnp.zeros((16, LANES), f32)
        for s in range(SLABS):
            cols = t.cols(r, s)
            value = step_ref[rows, cols]
            lam_b = s1[rows, cols]
            d_y = dy[rows, cols]
            act_s = act[rows, cols].astype(f32)
            s1[rows, cols] = d_y * skip + lam_b * value
            small = value * (1.0 - value * (0.5 - value * (1.0 / 6.0)))
            slope = jnp.where(value < 0.01, small, 1.0 - jnp.exp(-value))
            back = ((lam_b * act_s + LN2 * ds2[rows, cols]) * slope).astype(bf16)
            dx[rows, cols] = back
            skip_sum = skip_sum + d_y * act_s
            bias_sum = bias_sum + back.astype(f32)
        red[rows, DS * LANES : (DS + 1) * LANES] += skip_sum
        red[rows, (DS + 1) * LANES :] += bias_sum
        return carry

    lax.fori_loop(0, tile_count, adjoint_tile, 0)
    low_table = table[...].astype(bf16)
    for r in range(rows_n):
        pback[0:DR, row_cols(r)] = dot_tn(low_table, dx[:, row_cols(r)])[DT_COL : DT_COL + DR].astype(bf16)
    reduce.step1()
    pick = jnp.where(iota(((DS + 2) * LANES, LANES), 0) // LANES == iota(((DS + 2) * LANES, LANES), 1), 1.0, 0.0)
    dt_grad = jnp.concatenate(
        [
            jnp.zeros((channels, DT_COL), f32),
            dot_nt(dx[...], pjf[0:DR, :]),
            jnp.zeros((channels, LANES - DT_COL - DR), f32),
        ],
        axis=1,
    )
    zd[0:channels, :] = (dot_nn(red[...], pick, highest) + dt_grad).astype(bf16)
    sum_d.start()
    reduce.step2()
    reduce.step3()
    if rows_n == 1:
        for q in range(PIECES):
            cols = slice(q * SEQ_LEN // PIECES, (q + 1) * SEQ_LEN // PIECES)
            gate_part[cols, :] = dot_tn(dgate[:, cols], low[1])
    reduce.step4()
    for i in range(1, levels):
        sum_a.step(i)
        sum_b.step(i)
    sum_d.step(0)
    loads["x"].wait()
    x_low = xw_ref[...].astype(bf16)
    reduce.step5()
    for r in range(rows_n):
        s1[:, row_cols(r)] += dot_tn(x_low, pj[:, row_cols(r)])

    def conv_tile(index, carry):
        i = index // rows_n
        r = index % rows_n
        rows = pl.ds(pl.multiple_of(i * high, high), high)
        taps = [jnp.broadcast_to(table[rows, k : k + 1], (high, LANES)) for k in range(KC + 1)]
        earlier = {s: pltpu.roll(x_buf[rows, t.cols(r, s)], 1, 1) for s in range(SLABS - KC + 1, SLABS)}
        sums = [jnp.zeros((high, LANES), f32) for _ in range(KC + 1)]
        for s in range(SLABS):
            cols = t.cols(r, s)
            inputs = []
            conv = taps[KC]
            for j in range(KC):
                value = x_buf[rows, t.cols(r, s - j)] if s >= j else earlier[SLABS + s - j]
                if j > 0:
                    value = value * mask[j : j + 1, cols]
                inputs.append(value)
                conv = conv + taps[KC - 1 - j] * value
            sig = jax.nn.sigmoid(conv)
            d_conv = s1[rows, cols] * (sig * (1.0 + conv * (1.0 - sig)))
            dc[:, slab(s)] = d_conv
            for j in range(KC):
                sums[KC - 1 - j] = sums[KC - 1 - j] + d_conv * inputs[j]
            sums[KC] = sums[KC] + d_conv
        wrapped = {}
        for s in range(KC - 1):
            for j in range(s + 1, KC):
                wrapped[s, j] = pltpu.roll(dc[:, slab(s)] * mask[j : j + 1, t.cols(r, s)], LANES - 1, 1)
        for s in range(SLABS):
            d_x = taps[KC - 1] * dc[:, slab(s)]
            for j in range(1, KC):
                if s + j < SLABS:
                    value = dc[:, slab(s + j)] * mask[j : j + 1, t.cols(r, s + j)]
                else:
                    value = wrapped[s + j - SLABS, j]
                d_x = d_x + taps[KC - 1 - j] * value
            dx[rows, t.cols(r, s)] = d_x.astype(bf16)
        for k in range(KC + 1):
            @pl.when(r == 0)
            def _():
                taps_red[rows, slab(k)] = sums[k]

            @pl.when(r > 0)
            def _():
                taps_red[rows, slab(k)] += sums[k]
        return carry

    lax.fori_loop(0, channels // high * rows_n, conv_tile, 0)

    def weight_sums():
        if rows_n > 1:
            fetch(normed_in, 0, 1, "normed").wait()
        in_grad = dot_nn(dx[:, row_cols(0)], row_block(1))
        for r in range(1, rows_n):
            fetch(normed_in, r, 1, "normed").wait()
            in_grad = in_grad + dot_nn(dx[:, row_cols(r)], row_block(1))
        zc[0:channels, 0:width] = in_grad.astype(bf16)
        x_grad = dot_nt(act[...], pj[...])
        x_grad = jnp.concatenate([x_grad, jnp.zeros((channels, LANES - project), f32)], axis=1)
        k_i = iota(((KC + 1) * LANES, LANES), 0)
        pick = jnp.where(k_i // LANES + project == iota(((KC + 1) * LANES, LANES), 1), 1.0, 0.0)
        zc[0:channels, width : width + LANES] = (x_grad + dot_nn(taps_red[...], pick, highest)).astype(bf16)
        sum_c.start()

        both = low[0].astype(f32) * in_grad + low[1].astype(f32) * gin1[...]
        gp[...] = jnp.sum(both.reshape(channels // 8, 8, width), axis=0)

    def normed_part(cols):
        gate = gate_part[cols, :] if rows_n == 1 else dot_tn(dgate[:, cols], low[1])
        return dot_tn(dx[:, cols], low[0]) + gate

    weight_sums()
    normed_grad.produce(normed_part, True, lambda: None)
    normed_grad.send(PIECES - 1)

    def gain_seq(k):
        return pltpu.make_async_remote_copy(
            src_ref=gp, dst_ref=gz.at[k - 1], send_sem=gz_send.at[k - 1], recv_sem=gz_recv.at[k - 1],
            device_id=(flip(here.seq, k), here.chan), device_id_type=MESH,
        )

    def gain_chan(k):
        return here.copy(gz.at[seq_size - 1], gc.at[k - 1], gc_send.at[k - 1], gc_recv.at[k - 1], flip(here.chan, k))

    for k in range(1, seq_size):
        gain_seq(k).start()
    for k in range(1, seq_size):
        gain_seq(k).wait()
    total = gp[...]
    for k in range(1, seq_size):
        total = total + gz[k - 1]
    gz[seq_size - 1] = total
    for k in range(1, chan_size):
        gain_chan(k).start()
    saves = sum_a.finish(za_out, out_sem.at[0])
    saves += sum_b.finish(zb_out, out_sem.at[1])
    for i in range(1, levels):
        sum_d.step(i)
    if rows_n == 1:
        mixed.finish(msum_ref)
    for i in range(levels):
        sum_c.step(i)
    saves += sum_d.finish(zd_out, out_sem.at[3])
    for k in range(1, chan_size):
        gain_chan(k).wait()
        total = total + gc[k - 1]
    gsum_ref[...] = total
    normed_grad.finish(dsum_ref)
    saves += sum_c.finish(zc_out, out_sem.at[2])
    reduce.close()
    for c in saves:
        c.wait()


def back_call(
    chan_size, seq_size, own_rows, table, masks, x_weight, gated, out_weight, cot_all, step, act, pj, decays, dy, h0,
    dgate, normed_all, in_weight, x_cols,
):
    channels, width = out_weight.shape
    count = masks.shape[1]
    chips = chan_size // 2
    rows = count // SEQ_LEN
    per_row = SEQ_LEN // own_rows // 2
    lanes = own_rows // SLABS
    project = DR + 2 * DS
    wide = (channels, count)
    padded = (channels + 31) // 32 * 32
    levels = seq_size.bit_length() - 1
    any_spec = pl.BlockSpec(memory_space=pl.ANY)
    vmem = pl.BlockSpec(memory_space=pltpu.VMEM)
    dma = pltpu.SemaphoreType.DMA
    sums = ((padded, width), (padded, width), (padded, width + LANES), (padded, LANES))
    states = (DS * 8, SEQ_LEN)
    loops = (SLABS, NG, tile_depth(rows), 8, LANES)
    outs = [
        ((own_rows, width), f32), ((own_rows, width), f32), (sums[0], bf16), (sums[1], bf16), (sums[2], bf16),
        (sums[3], bf16), ((8, width), f32),
    ]
    scratch = [
        (wide, bf16), ((channels, width), f32), (wide, f32), (wide, bf16), ((project, count), bf16),
        ((DS, channels, LANES), f32), (wide, f32), ((rows * DS, channels, LANES), f32), (wide, bf16),
        ((2, channels, width), f32), ((2, SLABS, 2 * per_row, lanes, width), bf16),
        ((2, channels, width), bf16), (wide, bf16), ((tall(channels), SEQ_LEN), f32), ((channels, (KC + 1) * LANES), f32),
        ((channels, width), f32),
        (wide, f32), (wide, f32), (wide, f32), ((rows * channels, LANES), f32), ((7, rows * channels, LANES), f32),
        (states, f32), (states, f32), (states, f32), (states, f32), ((channels, (DS + 2) * LANES), f32),
        ((DS, channels, LANES), f32), ((SEQ_LEN if rows == 1 else 8, width), f32), (loops, f32), (loops, f32), ((project, count), bf16),
        ((min(rows, 2), SLABS, per_row, 2, lanes, width), bf16), ((rows, SLABS, per_row, lanes, width), bf16),
        ((chips - 1, SLABS, lanes, width), bf16),
        ((rows, SLABS, per_row, lanes, width) if rows == 1 else (16, LANES), bf16),
        ((chips - 1, SLABS, lanes, width) if rows == 1 else (16, LANES), bf16),
        ((project, count // 2), bf16), ((project, count // 2), bf16),
        ((chips - 1, project, count // 2 // chips), bf16), ((project, count), bf16),
        (sums[0], bf16), (sums[1], bf16), (sums[2], bf16), (sums[3], bf16),
    ]
    scratch += [((levels + 1, padded // 2, s[1]), bf16) for s in sums]
    scratch += [((8, width), f32), ((seq_size, 8, width), f32), ((chan_size - 1, 8, width), f32)]
    return pl.pallas_call(
        functools.partial(back_kernel, chan_size, seq_size),
        in_specs=[vmem] * 3 + [any_spec] * 13,
        out_specs=[vmem, vmem, any_spec, any_spec, any_spec, any_spec, vmem],
        out_shape=[jax.ShapeDtypeStruct(*o) for o in outs],
        scratch_shapes=[pltpu.VMEM(*s) for s in scratch]
        + [dma((13,)), dma((4, 2))]
        + ([dma((rows * PIECES,))] * 2 + [dma((chips * PIECES,))] * 2) * 2
        + [dma((2 * chips,))] * 2
        + [dma((4, levels + 1))] * 2
        + [dma((seq_size,))] * 2
        + [dma((chan_size,))] * 2,
        compiler_params=pltpu.CompilerParams(collective_id=1, has_side_effects=True, vmem_limit_bytes=60 * MIB),
        name="back",
    )(
        table, masks, x_weight, gated, out_weight, cot_all, step, act, pj, decays, dy, h0, dgate, normed_all, in_weight, x_cols
    )


def update(grad, master, first, second, rate, outs):
    new = adamw_core(master, first, second, grad, rate)
    for ref, value in zip(outs, new):
        ref[...] = value
    outs[3][...] = new[0].astype(bf16)


def finish_kernel(
    tok_ref, cot_ref, msum_ref, dsum_ref, za_ref, zb_ref, zc_ref, zb_all, zc_all, gsum_ref,
    gain_m, gain_f, gain_s, in_m, in_f, in_s, x_m, x_f, x_s, dt_m, dt_f, dt_s, out_m, out_f, out_s, ch_m, ch_f, ch_s,
    mixed_ref, tgrad_ref, *rest,
):
    gain_o, in_o, x_o, dt_o, out_o, ch_o = (rest[i * 4 : i * 4 + 4] for i in range(6))
    ch_grad = rest[24]
    i = pl.program_id(0)
    width = tok_ref.shape[1]
    own_rows = msum_ref.shape[0]
    block = tok_ref.shape[0]
    lanes = own_rows // SLABS
    channels = x_m.shape[1]

    r = lax.broadcasted_iota(jnp.int32, (block, own_rows), 0) + i * block
    q = lax.broadcasted_iota(jnp.int32, (block, own_rows), 1)
    order = jnp.where(r == (q % lanes) * SLABS + q // lanes, 1.0, 0.0).astype(bf16)

    def in_order(ref):
        values = ref[...]
        high = values.astype(bf16)
        return dot_nn(order, high) + dot_nn(order, (values - high.astype(f32)).astype(bf16))

    values = tok_ref[...].astype(f32)
    mixed_ref[...] = (values + in_order(msum_ref)).astype(bf16)
    d_normed = in_order(dsum_ref)
    rstd = lax.rsqrt(jnp.mean(values * values, axis=-1, keepdims=True) + norm_epsilon)
    gain_row = gain_m[...].reshape(1, width)
    scaled = gain_row * d_normed
    mean = jnp.mean(scaled * values, axis=-1, keepdims=True)
    tgrad_ref[...] = cot_ref[...].astype(f32) + rstd * scaled - values * (rstd * rstd * rstd * mean)

    out_grad = za_ref[...].astype(f32)
    update(out_grad, out_m[...], out_f[...], out_s[...], rate_output, out_o)
    for k, ref in ((0, zc_ref), (1, zb_ref)):
        grad = ref[:, 0:width].astype(f32)
        new = adamw_core(in_m[k], in_f[k], in_s[k], grad, rate_inner)
        for o, value in zip(in_o, new):
            o[k] = value
        in_o[3][k] = new[0].astype(bf16)

    @pl.when(i == 0)
    def _():
        grad_b = zb_all[...].astype(f32).T
        grad_c = zc_all[...].astype(f32).T
        update(grad_b[64 : 64 + DR, 0:channels], dt_m[...], dt_f[...], dt_s[...], rate_step, dt_o)
        project = x_m.shape[0]
        update(grad_c[0:project, 0:channels], x_m[...], x_f[...], x_s[...], rate_project, x_o)
        ch_grad[0 : KC + 1, :] = grad_c[project : project + KC + 1, 0:channels]
        ch_grad[KC + 1 : KC + 2, :] = grad_b[DS + 1 : DS + 2, 0:channels]
        ch_grad[KC + 2 : KC + 3, :] = grad_b[DS : DS + 1, 0:channels]
        ch_grad[KC + 3 :, :] = grad_b[0:DS, 0:channels] * -jnp.exp(ch_m[KC + 3 :, :])
        update(ch_grad[...], ch_m[...], ch_f[...], ch_s[...], rate_channel, ch_o)
        gain_grad = jnp.sum(gsum_ref[...], axis=0, keepdims=True) / gain_row
        moments = (ref[...].reshape(1, width) for ref in (gain_f, gain_s))
        new = adamw_core(gain_row, *moments, gain_grad, rate_gain)
        for ref, value in zip(gain_o, (*new, new[0].astype(bf16))):
            ref[...] = value.reshape(width)


def finish_call(tokens, cotangent, msum, dsum, za, zb, zc, zd, gsum, gains, inners, projects, steps, outputs, chans):
    own_rows, width = tokens.shape
    channels = outputs[0].shape[0]
    cb = 96 if channels % 96 == 0 else channels
    grid = channels // cb
    block = own_rows // grid
    row = pl.BlockSpec((block, width), lambda i: (i, 0))

    def full(shape):
        return pl.BlockSpec(shape, lambda i: (0,) * len(shape))

    inner = pl.BlockSpec((2, cb, width), lambda i: (0, i, 0))
    outer = pl.BlockSpec((cb, width), lambda i: (i, 0))
    tails = [full(zd.shape), pl.BlockSpec((zc.shape[0], LANES), lambda i: (0, width // LANES))]
    zed = pl.BlockSpec((cb, width), lambda i: (i, 0))
    groups = (gains, inners, projects, steps, outputs, chans)
    specs = (full(gains[0].shape), inner, full(projects[0].shape), full(steps[0].shape), outer, full(chans[0].shape))
    in_specs = [row, row, full(msum.shape), full(dsum.shape), zed, zed, zed, *tails, full(gsum.shape)]
    out_specs = [row, row]
    out_shape = [jax.ShapeDtypeStruct(tokens.shape, bf16), jax.ShapeDtypeStruct(tokens.shape, f32)]
    args = [tokens, cotangent, msum, dsum, za, zb, zc, zd, zc, gsum]
    for arrays, spec in zip(groups, specs):
        in_specs += [spec] * 3
        out_specs += [spec] * 4
        out_shape += [jax.ShapeDtypeStruct(arrays[0].shape, f32)] * 3 + [jax.ShapeDtypeStruct(arrays[0].shape, bf16)]
        args += list(arrays)
    return pl.pallas_call(
        finish_kernel,
        grid=(grid,),
        in_specs=in_specs,
        out_specs=out_specs,
        out_shape=out_shape,
        scratch_shapes=[pltpu.VMEM(chans[0].shape, f32)],
        compiler_params=pltpu.CompilerParams(dimension_semantics=("arbitrary",), vmem_limit_bytes=60 * MIB),
        name="finish",
    )(*args)


def per_device(
    tokens,
    resets,
    cotangent,
    norm_gain,
    in_weight,
    x_weight,
    dt_weight,
    out_weight,
    chan_params,
    gain_first,
    gain_second,
    in_first,
    in_second,
    x_first,
    x_second,
    dt_first,
    dt_second,
    out_first,
    out_second,
    chan_first,
    chan_second,
):
    own_count = tokens.shape[0]
    chan_size = lax.axis_size("chan")
    seq_size = lax.axis_size("seq")
    inners = [jnp.swapaxes(a, 1, 2) for a in (in_weight, in_first, in_second)]
    projects = [a.T for a in (x_weight, x_first, x_second)]
    x_cols, act, step, dy, gated, dgate, pj, normed_all, cot_all, h0, decays, masks, table = front_call(
        chan_size, tokens, cotangent, norm_gain, inners[0], projects[0], out_weight, chan_params, dt_weight,
        resets.reshape(-1, LANES),
    )
    msum, dsum, za, zb, zc, zd, gsum = back_call(
        chan_size, seq_size, own_count, table, masks, projects[0], gated, out_weight, cot_all, step, act, pj, decays, dy, h0,
        dgate, normed_all, inners[0], x_cols,
    )
    result = finish_call(
        tokens, cotangent, msum, dsum, za, zb, zc, zd, gsum,
        (norm_gain, gain_first, gain_second),
        inners,
        projects,
        (dt_weight, dt_first, dt_second),
        (out_weight, out_first, out_second),
        (chan_params, chan_first, chan_second),
    )
    result = list(result)
    result[6:10] = [jnp.swapaxes(a, 1, 2) for a in result[6:10]]
    result[10:14] = [a.T for a in result[10:14]]
    return tuple(result)


def solution(mesh):
    rows = P(("seq", "chan"), None)
    inner = P(None, None, "chan")
    by_row = P("chan", None)
    by_col = P(None, "chan")
    placed = (rows, P("seq"), rows, P(), inner, by_row, by_col, by_row, by_col, P(), P())
    placed += (inner, inner, by_row, by_row, by_col, by_col, by_row, by_row, by_col, by_col)
    return jax.shard_map(
        per_device,
        mesh=mesh,
        in_specs=placed,
        out_specs=(rows, rows)
        + (P(),) * 4
        + (inner,) * 4
        + (by_row,) * 4
        + (by_col,) * 4
        + (by_row,) * 4
        + (by_col,) * 4,
        check_vma=False,
    )
```
